32 devices in a mesh: section: 2 (over core), dp: 16 (over z, y, x).
Axes of the slice: x: 2, y: 2, z: 4, core: 2. Of those that a mesh axis runs over, the one named last changes fastest.
Arguments:
- endpoints: bfloat16 [2, 16384, 768], P('section', 'dp'), may hold values from -6 to 6
- projection: bfloat16 [2, 768, 2304], P('section'), may hold values from -0.21875 to 0.21875
- projection_bias: bfloat16 [2, 2304], P('section'), may hold values from -3 to 3
- output_weight: bfloat16 [2, 768, 768], P('section'), may hold values from -0.875 to 0.875
- output_bias: bfloat16 [2, 768], P('section'), may hold values from -3 to 3
- first_gain: bfloat16 [2, 768], P('section'), may hold values from 0.099609375 to 1.8984375
- first_shift: bfloat16 [2, 768], P('section'), may hold values from -3 to 3
- up_weight: bfloat16 [2, 768, 3072], P('section'), may hold values from -0.21875 to 0.21875
- up_bias: bfloat16 [2, 3072], P('section'), may hold values from -3 to 3
- down_weight: bfloat16 [2, 3072, 768], P('section'), may hold values from -0.109375 to 0.109375
- down_bias: bfloat16 [2, 768], P('section'), may hold values from -3 to 3
- second_gain: bfloat16 [2, 768], P('section'), may hold values from 0.099609375 to 1.8984375
- second_shift: bfloat16 [2, 768], P('section'), may hold values from -3 to 3
- segment_length: int32 [16], P('dp'), may hold values from 128 to 512, as said below
Outputs:
- results: float32 [2, 16384, 768], P('section', 'dp')
- projection_grad: float32 [2, 768, 2304], P('section')
- projection_bias_grad: float32 [2, 2304], P('section')
- output_weight_grad: float32 [2, 768, 768], P('section')
- output_bias_grad: float32 [2, 768], P('section')
- first_gain_grad: float32 [2, 768], P('section')
- first_shift_grad: float32 [2, 768], P('section')
- up_weight_grad: float32 [2, 768, 3072], P('section')
- up_bias_grad: float32 [2, 3072], P('section')
- down_weight_grad: float32 [2, 3072, 768], P('section')
- down_bias_grad: float32 [2, 768], P('section')
- second_gain_grad: float32 [2, 768], P('section')
- second_shift_grad: float32 [2, 768], P('section')
The draws below stay inside these ranges and needn't reach their ends.
Inputs may be any that keep to these rules, and one draw needn't show every extreme that they name: `segment_length`: each data group's document length is 128, 256 or 512, each of the three taken by some group; documents tile the group's tokens from its first one.
All inputs are finite; a program needn't handle non-finite values.
Results may differ from the reference program's by a relative error of at most 0.014.
Values may be sent and summed in bfloat16 or wider, within the bound.
A program may use at most 256 MiB of HBM per device.

```python
import math
import jax
import jax.numpy as jnp
from jax import lax

D = 768
HEADS = 12
FF = 3072
MB_ROWS = 512
DOC_MAX = 512
TOK_DEV = 1024
GROUPS = 16
TOKENS = 16384


def draw_segment_length(key, part):
    key = jax.random.fold_in(key, 11)
    shuffled = jax.random.permutation(key, GROUPS)
    residue = shuffled % 3
    return jnp.where(residue == 0, DOC_MAX // 4, jnp.where(residue == 1, DOC_MAX // 2, DOC_MAX)).astype(jnp.int32)


def shard_levels(rng, dims, shards, least, largest):
    def one(dim, shards_of):
        draws = jax.random.uniform(jax.random.fold_in(jax.random.fold_in(rng, 6), dim), (shards_of,), jnp.float32, least / len(shards), largest / len(shards))
        return jnp.repeat(jnp.exp(draws), dims[dim] // shards_of).reshape((-1,) + (1,) * (len(dims) - dim - 1))

    level = one(*shards[0])
    for cut in shards[1:]:
        level = level * one(*cut)
    return level


def normal_values(stream_key, shape, width, bound, cuts=(), held_as=jnp.bfloat16):
    entries = width * jax.random.normal(stream_key, shape, jnp.float32)
    if cuts:
        entries = entries * shard_levels(stream_key, shape, cuts, -0.22, 0.18)
    return jnp.clip(entries, -bound, bound).astype(held_as)


def setup_inputs(seed: int = 0) -> dict:
    keys = jax.random.split(jax.random.key(seed), 15)
    endpoints = normal_values(keys[0], (2, TOKENS, D), 1.0, 6.0, ((0, 2), (1, 16)))
    projection = normal_values(keys[1], (2, D, 3 * D), D ** -0.5, 0.21875, ((0, 2),))
    projection_bias = normal_values(keys[2], (2, 3 * D), 0.5, 3.0, ((0, 2),))
    output_weight = normal_values(keys[3], (2, D, D), (D // 16) ** -0.5, 0.875, ((0, 2),))
    output_bias = normal_values(keys[4], (2, D), 0.5, 3.0, ((0, 2),))
    first_gain = jnp.clip(1.0 + 0.18 * jax.random.normal(keys[5], (2, D), jnp.float32), 0.099609375, 1.8984375).astype(jnp.bfloat16)
    first_shift = normal_values(keys[6], (2, D), 0.5, 3.0, ((0, 2),))
    up_weight = normal_values(keys[7], (2, D, FF), D ** -0.5, 0.21875, ((0, 2),))
    up_bias = normal_values(keys[8], (2, FF), 0.5, 3.0, ((0, 2),))
    down_weight = normal_values(keys[9], (2, FF, D), FF ** -0.5, 0.109375, ((0, 2),))
    down_bias = normal_values(keys[10], (2, D), 0.5, 3.0, ((0, 2),))
    second_gain = jnp.clip(1.0 + 0.18 * jax.random.normal(keys[11], (2, D), jnp.float32), 0.099609375, 1.8984375).astype(jnp.bfloat16)
    second_shift = normal_values(keys[12], (2, D), 0.5, 3.0, ((0, 2),))
    segment_length = draw_segment_length(jax.random.fold_in(keys[14], 71), 0)
    return dict(endpoints=endpoints, projection=projection, projection_bias=projection_bias, output_weight=output_weight, output_bias=output_bias, first_gain=first_gain, first_shift=first_shift, up_weight=up_weight, up_bias=up_bias, down_weight=down_weight, down_bias=down_bias, second_gain=second_gain, second_shift=second_shift, segment_length=segment_length)


EPSILON = 1e-05

@jax.custom_vjp
def low(v):
    return lax.optimization_barrier(v.astype(jnp.bfloat16)).astype(jnp.float32)

@jax.custom_vjp
def low_back(v):
    return v

def low_keep(v):
    return (low(v), None)

def low_pass(kept, grad):
    return (grad,)

def back_keep(v):
    return (v, None)

def back_low(kept, grad):
    return (low(grad),)
low.defvjp(low_keep, low_pass)
low_back.defvjp(back_keep, back_low)

def matmul(left_mat, right_mat):
    return jnp.dot(left_mat, right_mat, precision=lax.Precision.HIGHEST, preferred_element_type=jnp.float32)

def normalize(summed, gain_vec, shift_vec):
    centre = summed - lax.optimization_barrier(jnp.mean(summed, axis=-1, keepdims=True))
    spread = lax.optimization_barrier(jnp.mean(centre * centre, axis=-1, keepdims=True))
    return centre * lax.rsqrt(spread + EPSILON) * gain_vec + shift_vec

def block_mix(operands):
    queries, keys_in, values, length = operands
    block_rows = queries.shape[0]
    places = jnp.arange(block_rows, dtype=jnp.int32)
    same_doc = places[:, None] // length == places[None, :] // length
    earlier = places[:, None] >= places[None, :]
    allowed = jnp.where(same_doc & earlier, 1.0, 0.0).astype(jnp.float32)
    scores = jnp.einsum('qhe,khe->hqk', queries, keys_in, precision=lax.Precision.HIGHEST) * allowed
    scores = low_back(scores)
    totals = lax.optimization_barrier(jnp.sum(scores, axis=-1, keepdims=True))
    weights = low(scores / totals)
    return jnp.einsum('hqk,khd->qhd', weights, values, precision=lax.Precision.HIGHEST)

def one_layer(inputs_f, params, cosine, sine_rows, block_docs):
    proj_w, proj_b, out_w, out_b, gain_one, shift_one, up_w, up_b, down_w, down_b, gain_two, shift_two = params
    tokens = inputs_f.shape[0]
    model_width = inputs_f.shape[1]
    head_dim = model_width // HEADS
    projected = low_back(matmul(inputs_f, proj_w) + proj_b)
    query_pre = projected[:, :model_width].reshape(tokens, HEADS, head_dim)
    key_pre = projected[:, model_width:2 * model_width].reshape(tokens, HEADS, head_dim)
    values = low(projected[:, 2 * model_width:]).reshape(tokens, HEADS, head_dim)

    def featured(pre_rows):
        softened = jax.nn.softplus(pre_rows)
        return low(jnp.concatenate([softened * cosine[:, None, None], softened * sine_rows[:, None, None]], axis=-1))
    block_rows = min(512, MB_ROWS)
    blocks = tokens // block_rows

    def into_blocks(array_in):
        return array_in.reshape((blocks, block_rows) + array_in.shape[1:])
    mixed_out = lax.map(jax.checkpoint(block_mix), (into_blocks(featured(query_pre)), into_blocks(featured(key_pre)), into_blocks(values), block_docs))
    mixed_out = low_back(low(mixed_out.reshape(tokens, model_width)))
    branch = low_back(matmul(mixed_out, out_w) + out_b)
    normed = normalize(inputs_f + branch, gain_one, shift_one)
    hidden = low_back(matmul(low(normed), up_w) + up_b)
    active = low(jax.nn.gelu(hidden, approximate=False))
    second = low_back(matmul(active, down_w) + down_b)
    return normalize(normed + second, gain_two, shift_two)

def reference(endpoints, projection, projection_bias, output_weight, output_bias, first_gain, first_shift, up_weight, up_bias, down_weight, down_bias, second_gain, second_shift, segment_length):
    weights = tuple((member.astype(jnp.float32) for member in (projection, projection_bias, output_weight, output_bias, first_gain, first_shift, up_weight, up_bias, down_weight, down_bias, second_gain, second_shift)))
    source = endpoints[0].astype(jnp.float32)
    cotangent = endpoints[1].astype(jnp.float32)
    block_rows = min(512, MB_ROWS)
    local_place = jnp.arange(TOKENS, dtype=jnp.int32) % TOK_DEV
    token_docs = jnp.repeat(segment_length, TOK_DEV, total_repeat_length=TOKENS).astype(jnp.int32)
    position = local_place % token_docs
    angles = 0.5 * math.pi * position.astype(jnp.float32) / token_docs.astype(jnp.float32)
    cosine = jnp.cos(angles)
    sine_rows = jnp.sin(angles)
    block_docs = jnp.repeat(segment_length, TOK_DEV // block_rows, total_repeat_length=TOKENS // block_rows).astype(jnp.int32)

    def forward(params, start):
        middle = one_layer(start, tuple((member[0] for member in params)), cosine, sine_rows, block_docs)
        middle = low_back(low(middle))
        return one_layer(middle, tuple((member[1] for member in params)), cosine, sine_rows, block_docs)
    final_out, pullback = jax.vjp(forward, weights, source)
    gradients, grad_source = pullback(cotangent)
    results = jnp.stack([grad_source, final_out])
    return (results, gradients[0], gradients[1], gradients[2], gradients[3], gradients[4], gradients[5], gradients[6], gradients[7], gradients[8], gradients[9], gradients[10], gradients[11])
```

```python
from functools import partial
import math

import jax
import jax.numpy as jnp
from jax import lax
from jax.experimental import pallas as pl
from jax.experimental.pallas import tpu as pltpu
from jax.sharding import PartitionSpec as P

HEADS = 12
MICRO = 2


EPSILON = 1e-05
MESH = pl.DeviceIdType.MESH


def from_behind(value, axis, steps):
    count = lax.axis_size(axis)
    leading, last = (max(0, -steps), min(count, count - steps))
    return lax.ppermute(value, axis, [(source, source + steps) for source in range(leading, last)])


def rows_product(left_mat, right_mat):
    return lax.dot_general(
        left_mat, right_mat, (((0,), (0,)), ((), ())), preferred_element_type=jnp.float32
    )


def back_product(grad_mat, weight_mat):
    return lax.dot_general(
        grad_mat, weight_mat, (((1,), (1,)), ((), ())), preferred_element_type=jnp.float32
    )


def normalize(summed, gain_vec, shift_vec):
    centre = summed - jnp.mean(summed, axis=-1, keepdims=True)
    spread = jnp.mean(centre * centre, axis=-1, keepdims=True)
    scaling = lax.rsqrt(spread + EPSILON)
    unit_rows = centre * scaling
    return (
        unit_rows * gain_vec.astype(jnp.float32) + shift_vec.astype(jnp.float32),
        unit_rows,
        scaling,
    )


def normalize_back(grad_unit, unit_rows, scaling):
    mean_grad = jnp.mean(grad_unit, axis=-1, keepdims=True)
    mean_cross = jnp.mean(grad_unit * unit_rows, axis=-1, keepdims=True)
    return scaling * (grad_unit - mean_grad - unit_rows * mean_cross)


def geometry(block_rows, length):
    places = jnp.arange(block_rows, dtype=jnp.int32)
    angles = 0.5 * math.pi * (places % length).astype(jnp.float32) / length.astype(jnp.float32)
    same_doc = places[:, None] // length == places[None, :] // length
    earlier = places[:, None] >= places[None, :]
    allowed = jnp.where(same_doc & earlier, 1.0, 0.0).astype(jnp.float32)
    return (jnp.cos(angles), jnp.sin(angles), allowed)


def featured(pre_rows, cosine, sine_rows):
    softened = jax.nn.softplus(pre_rows)
    return jnp.concatenate(
        [softened * cosine[:, None, None], softened * sine_rows[:, None, None]], axis=-1
    ).astype(jnp.bfloat16)


def featured_back(grad_rows, pre_rows, cosine, sine_rows):
    half_dim = pre_rows.shape[-1]
    combined = (
        grad_rows[..., :half_dim] * cosine[:, None, None]
        + grad_rows[..., half_dim:] * sine_rows[:, None, None]
    )
    return combined * jax.nn.sigmoid(pre_rows)


def into_blocks(array_in, blocks):
    return array_in.reshape((blocks, array_in.shape[0] // blocks) + array_in.shape[1:])


def mix_block(operands, allowed):
    queries, keys_in, values = operands
    scores = (
        jnp.einsum("qhe,khe->hqk", queries, keys_in, preferred_element_type=jnp.float32) * allowed
    )
    totals = jnp.sum(scores, axis=-1, keepdims=True)
    weights = (scores / totals).astype(jnp.bfloat16)
    return jnp.einsum("hqk,khd->qhd", weights, values, preferred_element_type=jnp.float32)


def mix_block_back(operands, allowed):
    queries, keys_in, values, grad_out = operands
    scores = (
        jnp.einsum("qhe,khe->hqk", queries, keys_in, preferred_element_type=jnp.float32) * allowed
    )
    totals = jnp.sum(scores, axis=-1, keepdims=True)
    probs = scores / totals
    weights = probs.astype(jnp.bfloat16)
    grad_values = jnp.einsum("hqk,qhd->khd", weights, grad_out, preferred_element_type=jnp.float32)
    grad_weights = jnp.einsum("qhd,khd->hqk", grad_out, values, preferred_element_type=jnp.float32)
    inner = jnp.sum(grad_weights * probs, axis=-1, keepdims=True)
    grad_scores = ((grad_weights - inner) / totals * allowed).astype(jnp.bfloat16)
    grad_queries = jnp.einsum(
        "hqk,khe->qhe", grad_scores, keys_in, preferred_element_type=jnp.float32
    )
    grad_keys = jnp.einsum("hqk,qhe->khe", grad_scores, queries, preferred_element_type=jnp.float32)
    return (grad_queries, grad_keys, grad_values)


def layer_forward(layer_in, params, layout):
    (
        proj_w,
        proj_b,
        out_w,
        out_b,
        gain_one,
        shift_one,
        up_w,
        up_b,
        down_w,
        down_b,
        gain_two,
        shift_two,
    ) = params
    cosine, sine_rows, allowed, block_rows = layout
    tokens, model_width = layer_in.shape
    head_dim = model_width // HEADS
    blocks = tokens // block_rows
    projected = jnp.dot(layer_in, proj_w, preferred_element_type=jnp.float32) + proj_b.astype(
        jnp.float32
    )
    query_pre = projected[:, :model_width].reshape(tokens, HEADS, head_dim)
    key_pre = projected[:, model_width : 2 * model_width].reshape(tokens, HEADS, head_dim)
    values = projected[:, 2 * model_width :].astype(jnp.bfloat16).reshape(tokens, HEADS, head_dim)
    queries = featured(query_pre, cosine, sine_rows)
    keys_in = featured(key_pre, cosine, sine_rows)
    mixed = lax.map(
        partial(mix_block, allowed=allowed),
        (into_blocks(queries, blocks), into_blocks(keys_in, blocks), into_blocks(values, blocks)),
    )
    mixed_out = mixed.reshape(tokens, model_width).astype(jnp.bfloat16)
    first_sum = layer_in.astype(jnp.float32) + (
        jnp.dot(mixed_out, out_w, preferred_element_type=jnp.float32) + out_b.astype(jnp.float32)
    )
    normed, unit_one, scale_one = normalize(first_sum, gain_one, shift_one)
    up_in = normed.astype(jnp.bfloat16)
    hidden = jnp.dot(up_in, up_w, preferred_element_type=jnp.float32) + up_b.astype(jnp.float32)
    active = jax.nn.gelu(hidden, approximate=False).astype(jnp.bfloat16)
    second_sum = normed + (
        jnp.dot(active, down_w, preferred_element_type=jnp.float32) + down_b.astype(jnp.float32)
    )
    layer_out, unit_two, scale_two = normalize(second_sum, gain_two, shift_two)
    kept = (
        layer_in,
        query_pre,
        key_pre,
        queries,
        keys_in,
        values,
        mixed_out,
        unit_one,
        scale_one,
        up_in,
        hidden,
        active,
        unit_two,
        scale_two,
    )
    return (layer_out, kept)


def tail_back(grad_out, params, kept):
    (
        proj_w,
        proj_b,
        out_w,
        out_b,
        gain_one,
        shift_one,
        up_w,
        up_b,
        down_w,
        down_b,
        gain_two,
        shift_two,
    ) = params
    (
        layer_in,
        query_pre,
        key_pre,
        queries,
        keys_in,
        values,
        mixed_out,
        unit_one,
        scale_one,
        up_in,
        hidden,
        active,
        unit_two,
        scale_two,
    ) = kept
    gain_two_grad = jnp.sum(grad_out * unit_two, axis=0)
    shift_two_grad = jnp.sum(grad_out, axis=0)
    second_full = normalize_back(grad_out * gain_two.astype(jnp.float32), unit_two, scale_two)
    second_low = second_full.astype(jnp.bfloat16)
    down_b_grad = jnp.sum(second_low.astype(jnp.float32), axis=0)
    grad_active = back_product(second_low, down_w)
    gelu_pull = jax.vjp(partial(jax.nn.gelu, approximate=False), hidden)[1]
    hidden_low = gelu_pull(grad_active)[0].astype(jnp.bfloat16)
    up_b_grad = jnp.sum(hidden_low.astype(jnp.float32), axis=0)
    grad_normed = second_full + back_product(hidden_low, up_w)
    gain_one_grad = jnp.sum(grad_normed * unit_one, axis=0)
    shift_one_grad = jnp.sum(grad_normed, axis=0)
    grad_first = normalize_back(grad_normed * gain_one.astype(jnp.float32), unit_one, scale_one)
    return (
        grad_first,
        (
            gain_one_grad,
            shift_one_grad,
            up_b_grad,
            down_b_grad,
            gain_two_grad,
            shift_two_grad,
        ),
        (hidden_low, second_low),
    )


def head_back(grad_first, params, kept, layout):
    (
        proj_w,
        proj_b,
        out_w,
        out_b,
        gain_one,
        shift_one,
        up_w,
        up_b,
        down_w,
        down_b,
        gain_two,
        shift_two,
    ) = params
    (
        layer_in,
        query_pre,
        key_pre,
        queries,
        keys_in,
        values,
        mixed_out,
        unit_one,
        scale_one,
        up_in,
        hidden,
        active,
        unit_two,
        scale_two,
    ) = kept
    cosine, sine_rows, allowed, block_rows = layout
    tokens, model_width = layer_in.shape
    head_dim = model_width // HEADS
    blocks = tokens // block_rows
    first_low = grad_first.astype(jnp.bfloat16)
    out_b_grad = jnp.sum(first_low.astype(jnp.float32), axis=0)
    grad_mixed = (
        back_product(first_low, out_w).astype(jnp.bfloat16).reshape(tokens, HEADS, head_dim)
    )
    grad_queries, grad_keys, grad_values = lax.map(
        partial(mix_block_back, allowed=allowed),
        (
            into_blocks(queries, blocks),
            into_blocks(keys_in, blocks),
            into_blocks(values, blocks),
            into_blocks(grad_mixed, blocks),
        ),
    )
    grad_query_pre = featured_back(
        grad_queries.reshape(tokens, HEADS, 2 * head_dim), query_pre, cosine, sine_rows
    )
    grad_key_pre = featured_back(
        grad_keys.reshape(tokens, HEADS, 2 * head_dim), key_pre, cosine, sine_rows
    )
    grad_projected = jnp.concatenate(
        [
            grad_query_pre.reshape(tokens, model_width),
            grad_key_pre.reshape(tokens, model_width),
            grad_values.reshape(tokens, model_width),
        ],
        axis=1,
    ).astype(jnp.bfloat16)
    proj_b_grad = jnp.sum(grad_projected.astype(jnp.float32), axis=0)
    grad_in = grad_first + back_product(grad_projected, proj_w)
    return (grad_in, (proj_b_grad, out_b_grad), (first_low, grad_projected))


def factor_dims(count):
    bits = count.bit_length() - 1
    return (1 << (bits // 3), 1 << ((bits + 1) // 3), 1 << ((bits + 2) // 3))


ORDERS = {"a": (0, 1, 2), "b": (1, 2, 0), "c": (2, 0, 1)}
PATTERN = "abacabc"
LAG = 3
UNIT = 256


def stage_list(order, dims, rows):
    stages, size, landing = [], rows, 0
    for level, ax in enumerate(order):
        part = size // dims[ax]
        for step in range(1, dims[ax]):
            stages.append(("reduce", level, ax, step, part, landing))
            landing += part if dims[ax] == 2 else 2 * part
        size = part
    for level in reversed(range(3)):
        ax = order[level]
        for step in range(1, dims[ax]):
            stages.append(("gather", level, ax, step, size, 0))
        size *= dims[ax]
    return stages, landing


def unit_blocks(unit):
    up, out, proj = unit - 36, unit - 72, unit - 81
    left = jnp.where(
        unit < 36,
        unit // 3,
        jnp.where(unit < 72, 12 + up // 12, jnp.where(unit < 81, 15 + out // 3, 18 + proj // 9)),
    )
    right = jnp.where(
        unit < 36,
        unit % 3,
        jnp.where(unit < 72, 3 + up % 12, jnp.where(unit < 81, 15 + out % 3, 18 + proj % 9)),
    )
    return left, right


def reduce_kernel(dims, pieces, rows, units, left_hbm, right_hbm, vec_hbm, sum_hbm,
                  acc, landing, full, vec_buf, left_buf, right_buf, load_sem, vec_sem, out_sem,
                  send_sem, recv_sem):
    here = lax.axis_index("dp")
    strides = (1, dims[0], dims[0] * dims[1])
    place = [(here // strides[ax]) % dims[ax] for ax in range(3)]
    slots = send_sem.shape[0]
    ring = left_buf.shape[0]
    per_piece = rows // UNIT
    land_rows = landing.shape[0] // slots
    plans = {name: stage_list(order, dims, rows)[0] for name, order in ORDERS.items()}
    n_stages = len(plans["a"])
    n_shards = dims[0] * dims[1] * dims[2]
    period = len(PATTERN)
    rounds = -(-pieces // period)
    all_rounds = -(-(pieces + n_stages * LAG) // period)

    bases = {}
    for name, order in ORDERS.items():
        base, size, found = 0, rows, []
        for ax in order:
            found.append(base)
            size = size // dims[ax]
            base = base + place[ax] * size
        bases[name] = found

    def neighbour(ax, sign):
        return {"dp": here + sign * strides[ax]}

    barrier = pltpu.get_barrier_semaphore()
    for ax in range(3):
        for sign, can in ((1, place[ax] < dims[ax] - 1), (-1, place[ax] > 0)):
            @pl.when(can)
            def _():
                pl.semaphore_signal(
                    barrier, inc=1, device_id=neighbour(ax, sign), device_id_type=MESH
                )
    around = sum(
        (place[ax] < dims[ax] - 1).astype(jnp.int32) + (place[ax] > 0).astype(jnp.int32)
        for ax in range(3)
    )
    pl.semaphore_wait(barrier, around)

    def loads(unit):
        slot = unit % ring
        left, right = unit_blocks(unit)
        return (
            pltpu.make_async_copy(left_hbm.at[left], left_buf.at[slot], load_sem.at[slot, 0]),
            pltpu.make_async_copy(right_hbm.at[right], right_buf.at[slot], load_sem.at[slot, 1]),
        )

    vec_copy = pltpu.make_async_copy(vec_hbm, vec_buf, vec_sem)
    vec_copy.start()
    for unit in range(ring):
        for copy in loads(jnp.int32(unit)):
            copy.start()
    vec_copy.wait()

    def form(piece, sub):
        unit = piece * per_piece + sub
        start = (piece % slots) * rows + sub * UNIT

        @pl.when(unit < units)
        def _():
            for copy in loads(unit):
                copy.wait()
            slot = unit % ring
            acc[pl.ds(pl.multiple_of(start, UNIT), UNIT), :] = lax.dot_general(
                left_buf[slot], right_buf[slot], (((0,), (0,)), ((), ())),
                preferred_element_type=jnp.float32,
            ).astype(jnp.bfloat16)

            @pl.when(unit + ring < units)
            def _():
                for copy in loads(unit + ring):
                    copy.start()

        @pl.when(unit >= units)
        def _():
            acc[pl.ds(pl.multiple_of(start, UNIT), UNIT), :] = vec_buf[
                sub * UNIT : (sub + 1) * UNIT
            ]

    def copies(name, stage, piece):
        kind, level, ax, step, part, land = plans[name][stage]
        count, spot = dims[ax], place[ax]
        slot = piece % slots
        held, index = (acc, slot) if kind == "reduce" else (full, piece)
        start = index * rows + bases[name][level]
        land_start = pl.multiple_of(slot * land_rows + land, 16)

        def chunk(q):
            return held.at[pl.ds(pl.multiple_of(start + q * part, 16), part)]

        def landed(way):
            return landing.at[pl.ds(pl.multiple_of(land_start + way * part, 16), part)]

        def remote(src, dst, way, sign):
            return lambda: pltpu.make_async_remote_copy(
                src_ref=src, dst_ref=dst, send_sem=send_sem.at[slot, stage, way],
                recv_sem=recv_sem.at[slot, stage, way], device_id=neighbour(ax, sign),
                device_id_type=MESH,
            )

        sends, receives = [], []
        if count == 2:
            sign = 1 - 2 * spot
            mine, other = spot, 1 - spot
            if kind == "reduce":
                sends.append((None, remote(chunk(other), landed(0), 0, sign)))
                receives.append((None, remote(chunk(mine), landed(0), 0, sign), mine, landed(0)))
            else:
                sends.append((None, remote(chunk(mine), chunk(mine), 0, sign)))
                receives.append((None, remote(chunk(other), chunk(other), 0, sign), other, None))
            return sends, receives, chunk
        back = count - 1 - spot
        if kind == "reduce":
            for way, sign, can, q in (
                (0, 1, spot < step, spot + count - step),
                (1, -1, back < step, step - 1 - back),
            ):
                q = jnp.clip(q, 0, count - 1)
                sends.append((can, remote(chunk(q), landed(way), way, sign)))
            for way, sign, can, q in (
                (0, 1, jnp.logical_and(spot >= 1, spot - 1 < step), spot - 1 + count - step),
                (1, -1, jnp.logical_and(back >= 1, back - 1 < step), step - back),
            ):
                q = jnp.clip(q, 0, count - 1)
                receives.append((can, remote(chunk(q), landed(way), way, sign), q, landed(way)))
        else:
            for way, sign, can, q in (
                (0, 1, jnp.logical_and(back >= 1, spot >= step - 1), spot - step + 1),
                (1, -1, jnp.logical_and(spot >= 1, back >= step - 1), spot + step - 1),
            ):
                q = jnp.clip(q, 0, count - 1)
                sends.append((can, remote(chunk(q), chunk(q), way, sign)))
            for way, sign, can, q in (
                (0, 1, spot >= step, spot - step),
                (1, -1, back >= step, spot + step),
            ):
                q = jnp.clip(q, 0, count - 1)
                receives.append((can, remote(chunk(q), chunk(q), way, sign), q, None))
        return sends, receives, chunk

    def guarded(can, action):
        if can is None:
            action()
        else:
            pl.when(can)(action)

    def out_copy(piece):
        block = pl.ds(pl.multiple_of(piece * rows, rows), rows)
        return pltpu.make_async_copy(full.at[block], sum_hbm.at[block], out_sem.at[piece])

    def work(name, stage, piece):
        if stage > 0:
            sends, receives, chunk = copies(name, stage - 1, piece)
            for can, copy, q, landed in receives:
                def finish():
                    copy().wait_recv()
                    if landed is not None:
                        block = chunk(q)
                        block[...] = block[...] + landed[...]
                guarded(can, finish)
        if stage == n_stages // 2:
            mine = bases[name][2] + place[ORDERS[name][2]] * (rows // n_shards)
            kept = acc[pl.ds(pl.multiple_of((piece % slots) * rows + mine, 16), rows // n_shards), :]
            full[pl.ds(pl.multiple_of(piece * rows + mine, 16), rows // n_shards), :] = kept
        if stage < n_stages:
            for can, copy in copies(name, stage, piece)[0]:
                guarded(can, lambda: copy().start())
        else:
            out_copy(piece).start()
        if stage > 0:
            for can, copy in sends:
                guarded(can, lambda: copy().wait_send())

    def one_round(turn, carry):
        for spot_in in range(period):
            tick = turn * period + spot_in
            for stage in reversed(range(1, n_stages + 1)):
                piece = tick - stage * LAG
                name = PATTERN[(spot_in - stage * LAG) % period]

                @pl.when(jnp.logical_and(piece >= 0, piece < pieces))
                def _():
                    work(name, stage, jnp.clip(piece, 0, pieces - 1))

            @pl.when(tick < pieces)
            def _():
                piece = jnp.minimum(tick, pieces - 1)
                for sub in range(per_piece):
                    form(piece, sub)
                work(PATTERN[spot_in], 0, piece)
        return carry

    lax.fori_loop(0, all_rounds, one_round, 0)

    def drain(piece, carry):
        out_copy(piece).wait()
        return carry

    lax.fori_loop(0, pieces, drain, 0)


def reduce_gradients(left, right, vec, dp_size):
    dims = factor_dims(dp_size)
    rows = 16 * dp_size
    units = 108
    pieces = (units * UNIT + vec.shape[0]) // rows
    slots = 4 * len(PATTERN)
    ring = 4 if dp_size <= 16 else 2
    land = max(stage_list(order, dims, rows)[1] for order in ORDERS.values())
    n_stages = 2 * (sum(dims) - 3)
    tokens = left.shape[1]
    total = pieces * rows
    return pl.pallas_call(
        partial(reduce_kernel, dims, pieces, rows, units),
        out_shape=jax.ShapeDtypeStruct((total, UNIT), jnp.bfloat16),
        in_specs=[pl.BlockSpec(memory_space=pl.ANY)] * 3,
        out_specs=pl.BlockSpec(memory_space=pl.ANY),
        scratch_shapes=[
            pltpu.VMEM((slots * rows, UNIT), jnp.bfloat16),
            pltpu.VMEM((slots * land, UNIT), jnp.bfloat16),
            pltpu.VMEM((total, UNIT), jnp.bfloat16),
            pltpu.VMEM((rows, UNIT), jnp.bfloat16),
            pltpu.VMEM((ring, tokens, UNIT), jnp.bfloat16),
            pltpu.VMEM((ring, tokens, UNIT), jnp.bfloat16),
            pltpu.SemaphoreType.DMA((ring, 2)),
            pltpu.SemaphoreType.DMA,
            pltpu.SemaphoreType.DMA((pieces,)),
            pltpu.SemaphoreType.DMA((slots, n_stages, 2)),
            pltpu.SemaphoreType.DMA((slots, n_stages, 2)),
        ],
        compiler_params=pltpu.CompilerParams(
            collective_id=1, has_side_effects=True, vmem_limit_bytes=62 << 20
        ),
        cost_estimate=pl.CostEstimate(
            flops=2 * units * UNIT * UNIT * tokens, bytes_accessed=120 << 20, transcendentals=0
        ),
    )(left, right, vec)


def shards(
    endpoints,
    projection,
    projection_bias,
    output_weight,
    output_bias,
    first_gain,
    first_shift,
    up_weight,
    up_bias,
    down_weight,
    down_bias,
    second_gain,
    second_shift,
    segment_length,
):
    section_index = lax.axis_index("section")
    is_first = section_index == 0
    params = (
        projection[0],
        projection_bias[0],
        output_weight[0],
        output_bias[0],
        first_gain[0],
        first_shift[0],
        up_weight[0],
        up_bias[0],
        down_weight[0],
        down_bias[0],
        second_gain[0],
        second_shift[0],
    )
    local_rows = endpoints[0]
    micro_rows = local_rows.shape[0] // MICRO
    model_width = local_rows.shape[1]
    block_rows = min(512, micro_rows)
    cosine, sine_rows, allowed = geometry(block_rows, segment_length[0])
    repeats = micro_rows // block_rows
    layout = (jnp.tile(cosine, repeats), jnp.tile(sine_rows, repeats), allowed, block_rows)
    pieces = [
        local_rows[micro_idx * micro_rows : (micro_idx + 1) * micro_rows]
        for micro_idx in range(MICRO)
    ]
    empty_rows = jnp.zeros((micro_rows, model_width), jnp.bfloat16)
    received = empty_rows
    inputs_kept = []
    states_kept = []
    outputs_kept = []
    for tick_fwd in range(MICRO + 1):
        own_rows = pieces[tick_fwd] if tick_fwd < MICRO else empty_rows
        layer_in = jnp.where(is_first, own_rows, received)
        layer_out, kept = layer_forward(layer_in, params, layout)
        inputs_kept.append(layer_in)
        outputs_kept.append(layer_out)
        states_kept.append(kept)
        if tick_fwd < MICRO:
            received = from_behind(layer_out.astype(jnp.bfloat16), "section", 1)
    zero_grad = jnp.zeros((micro_rows, model_width), jnp.float32)
    came_back = zero_grad
    input_grads = [zero_grad for micro_idx in range(MICRO)]
    vectors = 0.0
    factors = []
    for back_step in range(MICRO + 1):
        tick_fwd = MICRO - back_step
        own_index = MICRO - 1 - back_step
        own_grad = pieces[own_index].astype(jnp.float32) if own_index >= 0 else zero_grad
        grad_out = jnp.where(is_first, came_back, own_grad)
        kept = states_kept[tick_fwd]
        grad_first, tail_terms, tail_factors = tail_back(grad_out, params, kept)
        grad_in, head_terms, head_factors = head_back(grad_first, params, kept, layout)
        vectors = vectors + jnp.concatenate(head_terms + tail_terms)
        factors.append(
            (
                (kept[11], kept[9], kept[6], kept[0]),
                (tail_factors[1], tail_factors[0], head_factors[0], head_factors[1]),
            )
        )
        if tick_fwd < MICRO:
            input_grads[tick_fwd] = grad_in
        if back_step < MICRO:
            came_back = from_behind(grad_in.astype(jnp.bfloat16), "section", -1).astype(jnp.float32)
    factors.reverse()

    def chosen(side):
        picked = []
        for member in range(4):
            ticks = [factors[tick][side][member] for tick in range(MICRO + 1)]
            early = jnp.concatenate(ticks[:MICRO], axis=0)
            late = jnp.concatenate(ticks[1:], axis=0)
            picked.append(jnp.where(is_first, early, late))
        joined = jnp.concatenate(picked, axis=1)
        return joined.reshape(joined.shape[0], -1, UNIT).transpose(1, 0, 2)

    dp_size = lax.axis_size("dp")
    vec_rows = 16 * dp_size
    vec = jnp.zeros((vec_rows * UNIT,), jnp.float32).at[: vectors.shape[0]].set(vectors)
    summed = reduce_gradients(
        chosen(0), chosen(1), vec.astype(jnp.bfloat16).reshape(vec_rows, UNIT), dp_size
    ).astype(jnp.float32)

    def matrix(start, across, down):
        blocks = summed[start * UNIT : (start + across * down) * UNIT]
        return (
            blocks.reshape(down, across, UNIT, UNIT)
            .transpose(0, 2, 1, 3)
            .reshape(down * UNIT, across * UNIT)
        )

    flat = summed[108 * UNIT :].reshape(-1)
    spots, start = [], 0
    for size in (3 * model_width, model_width, model_width, model_width, 4 * model_width) + (
        model_width,
    ) * 3:
        spots.append(flat[start : start + size])
        start += size
    summed_all = (
        matrix(81, 9, 3), spots[0], matrix(72, 3, 3), spots[1], spots[2], spots[3],
        matrix(36, 12, 3), spots[4], matrix(0, 3, 12), spots[5], spots[6], spots[7],
    )
    answers = jnp.where(
        is_first, jnp.concatenate(input_grads, axis=0), jnp.concatenate(outputs_kept[1:], axis=0)
    )[None]
    return (answers,) + tuple((member[None] for member in summed_all))


def solution(mesh):
    in_specs = (
        P("section", "dp", None),
        P("section", None, None),
        P("section", None),
        P("section", None, None),
        P("section", None),
        P("section", None),
        P("section", None),
        P("section", None, None),
        P("section", None),
        P("section", None, None),
        P("section", None),
        P("section", None),
        P("section", None),
        P("dp"),
    )
    out_specs = (
        P("section", "dp", None),
        P("section", None, None),
        P("section", None),
        P("section", None, None),
        P("section", None),
        P("section", None),
        P("section", None),
        P("section", None, None),
        P("section", None),
        P("section", None, None),
        P("section", None),
        P("section", None),
        P("section", None),
    )
    return jax.shard_map(shards, mesh=mesh, in_specs=in_specs, out_specs=out_specs, check_vma=False)
```

```python
from functools import partial
import math

import jax
import jax.numpy as jnp
from jax import lax
from jax.experimental import pallas as pl
from jax.experimental.pallas import tpu as pltpu
from jax.sharding import PartitionSpec as P

HEADS = 12
EPSILON = 1e-05
MESH = pl.DeviceIdType.MESH


def rows_product(left_mat, right_mat):
    return lax.dot_general(
        left_mat, right_mat, (((0,), (0,)), ((), ())), preferred_element_type=jnp.float32
    )


def back_product(grad_mat, weight_mat):
    return lax.dot_general(
        grad_mat, weight_mat, (((1,), (1,)), ((), ())), preferred_element_type=jnp.float32
    )


def factor_dims(count):
    bits = count.bit_length() - 1
    return (1 << (bits // 3), 1 << ((bits + 1) // 3), 1 << ((bits + 2) // 3))


ORDERS = {"a": (0, 1, 2), "b": (1, 2, 0), "c": (2, 0, 1)}
PATTERN = "abacabc"
LAG = 3
UNIT = 256


def stage_list(order, dims, rows):
    stages, size, landing = [], rows, 0
    for level, ax in enumerate(order):
        part = size // dims[ax]
        for step in range(1, dims[ax]):
            stages.append(("reduce", level, ax, step, part, landing))
            landing += part if dims[ax] == 2 else 2 * part
        size = part
    for level in reversed(range(3)):
        ax = order[level]
        for step in range(1, dims[ax]):
            stages.append(("gather", level, ax, step, size, 0))
        size *= dims[ax]
    return stages, landing


def unit_blocks(unit):
    up, out, proj = unit - 36, unit - 72, unit - 81
    left = jnp.where(
        unit < 36,
        unit // 3,
        jnp.where(unit < 72, 12 + up // 12, jnp.where(unit < 81, 15 + out // 3, 18 + proj // 9)),
    )
    right = jnp.where(
        unit < 36,
        unit % 3,
        jnp.where(unit < 72, 3 + up % 12, jnp.where(unit < 81, 15 + out % 3, 18 + proj % 9)),
    )
    return left, right


def reduce_kernel(dims, pieces, rows, units, left_hbm, right_hbm, vec_hbm,
                  proj_hbm, out_hbm, up_hbm, down_hbm, small_hbm, acc, landing, full, vec_buf, left_buf, right_buf, load_sem, vec_sem, out_sem,
                  send_sem, recv_sem):
    here = lax.axis_index("dp")
    strides = (1, dims[0], dims[0] * dims[1])
    place = [(here // strides[ax]) % dims[ax] for ax in range(3)]
    slots = send_sem.shape[0]
    ring = left_buf.shape[0]
    per_piece = rows // UNIT
    land_rows = landing.shape[0] // slots
    plans = {name: stage_list(order, dims, rows)[0] for name, order in ORDERS.items()}
    n_stages = len(plans["a"])
    n_shards = dims[0] * dims[1] * dims[2]
    period = len(PATTERN)
    rounds = -(-pieces // period)
    all_rounds = -(-(pieces + n_stages * LAG) // period)

    bases = {}
    for name, order in ORDERS.items():
        base, size, found = 0, rows, []
        for ax in order:
            found.append(base)
            size = size // dims[ax]
            base = base + place[ax] * size
        bases[name] = found

    def neighbour(ax, sign):
        return {"dp": here + sign * strides[ax]}

    barrier = pltpu.get_barrier_semaphore()
    for ax in range(3):
        for sign, can in ((1, place[ax] < dims[ax] - 1), (-1, place[ax] > 0)):
            @pl.when(can)
            def _():
                pl.semaphore_signal(
                    barrier, inc=1, device_id=neighbour(ax, sign), device_id_type=MESH
                )
    around = sum(
        (place[ax] < dims[ax] - 1).astype(jnp.int32) + (place[ax] > 0).astype(jnp.int32)
        for ax in range(3)
    )
    pl.semaphore_wait(barrier, around)

    def loads(unit):
        slot = unit % ring
        left, right = unit_blocks(unit)
        return (
            pltpu.make_async_copy(left_hbm.at[left], left_buf.at[slot], load_sem.at[slot, 0]),
            pltpu.make_async_copy(right_hbm.at[right], right_buf.at[slot], load_sem.at[slot, 1]),
        )

    vec_copy = pltpu.make_async_copy(vec_hbm, vec_buf, vec_sem)
    vec_copy.start()
    for unit in range(ring):
        for copy in loads(jnp.int32(unit)):
            copy.start()
    vec_copy.wait()

    def form(piece, sub):
        unit = piece * per_piece + sub
        start = (piece % slots) * rows + sub * UNIT

        @pl.when(unit < units)
        def _():
            for copy in loads(unit):
                copy.wait()
            slot = unit % ring
            acc[pl.ds(pl.multiple_of(start, UNIT), UNIT), :] = lax.dot_general(
                left_buf[slot], right_buf[slot], (((0,), (0,)), ((), ())),
                preferred_element_type=jnp.float32,
            ).astype(jnp.bfloat16)

            @pl.when(unit + ring < units)
            def _():
                for copy in loads(unit + ring):
                    copy.start()

        @pl.when(unit >= units)
        def _():
            acc[pl.ds(pl.multiple_of(start, UNIT), UNIT), :] = vec_buf[
                sub * UNIT : (sub + 1) * UNIT
            ].astype(jnp.bfloat16)

    def copies(name, stage, piece):
        kind, level, ax, step, part, land = plans[name][stage]
        count, spot = dims[ax], place[ax]
        slot = piece % slots
        held, index = (acc, slot) if kind == "reduce" else (full, piece)
        start = index * rows + bases[name][level]
        land_start = pl.multiple_of(slot * land_rows + land, 16)

        def chunk(q):
            return held.at[pl.ds(pl.multiple_of(start + q * part, 16), part)]

        def landed(way):
            return landing.at[pl.ds(pl.multiple_of(land_start + way * part, 16), part)]

        def remote(src, dst, way, sign):
            return lambda: pltpu.make_async_remote_copy(
                src_ref=src, dst_ref=dst, send_sem=send_sem.at[slot, stage, way],
                recv_sem=recv_sem.at[slot, stage, way], device_id=neighbour(ax, sign),
                device_id_type=MESH,
            )

        sends, receives = [], []
        if count == 2:
            sign = 1 - 2 * spot
            mine, other = spot, 1 - spot
            if kind == "reduce":
                sends.append((None, remote(chunk(other), landed(0), 0, sign)))
                receives.append((None, remote(chunk(mine), landed(0), 0, sign), mine, landed(0)))
            else:
                sends.append((None, remote(chunk(mine), chunk(mine), 0, sign)))
                receives.append((None, remote(chunk(other), chunk(other), 0, sign), other, None))
            return sends, receives, chunk
        back = count - 1 - spot
        if kind == "reduce":
            for way, sign, can, q in (
                (0, 1, spot < step, spot + count - step),
                (1, -1, back < step, step - 1 - back),
            ):
                q = jnp.clip(q, 0, count - 1)
                sends.append((can, remote(chunk(q), landed(way), way, sign)))
            for way, sign, can, q in (
                (0, 1, jnp.logical_and(spot >= 1, spot - 1 < step), spot - 1 + count - step),
                (1, -1, jnp.logical_and(back >= 1, back - 1 < step), step - back),
            ):
                q = jnp.clip(q, 0, count - 1)
                receives.append((can, remote(chunk(q), landed(way), way, sign), q, landed(way)))
        else:
            for way, sign, can, q in (
                (0, 1, jnp.logical_and(back >= 1, spot >= step - 1), spot - step + 1),
                (1, -1, jnp.logical_and(spot >= 1, back >= step - 1), spot + step - 1),
            ):
                q = jnp.clip(q, 0, count - 1)
                sends.append((can, remote(chunk(q), chunk(q), way, sign)))
            for way, sign, can, q in (
                (0, 1, spot >= step, spot - step),
                (1, -1, back >= step, spot + step),
            ):
                q = jnp.clip(q, 0, count - 1)
                receives.append((can, remote(chunk(q), chunk(q), way, sign), q, None))
        return sends, receives, chunk

    def guarded(can, action):
        if can is None:
            action()
        else:
            pl.when(can)(action)

    def out_copies(piece, action):
        for sub in range(per_piece):
            unit = piece * per_piece + sub
            source = full.at[pl.ds(pl.multiple_of(unit * UNIT, UNIT), UNIT)]
            for begin, end, across, target in (
                (0, 36, 3, down_hbm), (36, 72, 12, up_hbm), (72, 81, 3, out_hbm),
                (81, 108, 9, proj_hbm), (108, 108 + per_piece, 1, small_hbm),
            ):
                @pl.when(jnp.logical_and(unit >= begin, unit < end))
                def _():
                    local = jnp.clip(unit - begin, 0, end - begin - 1)
                    place_in = target.at[
                        pl.ds(pl.multiple_of(local // across * UNIT, UNIT), UNIT),
                        pl.ds(pl.multiple_of(local % across * UNIT, UNIT), UNIT),
                    ]
                    action(pltpu.make_async_copy(source, place_in, out_sem.at[unit]))

    def work(name, stage, piece):
        if stage > 0:
            sends, receives, chunk = copies(name, stage - 1, piece)
            for can, copy, q, landed in receives:
                def finish():
                    copy().wait_recv()
                    if landed is not None:
                        block = chunk(q)
                        block[...] = block[...] + landed[...]
                guarded(can, finish)
        if stage == n_stages // 2:
            mine = bases[name][2] + place[ORDERS[name][2]] * (rows // n_shards)
            kept = acc[pl.ds(pl.multiple_of((piece % slots) * rows + mine, 16), rows // n_shards), :]
            full[pl.ds(pl.multiple_of(piece * rows + mine, 16), rows // n_shards), :] = kept
        if stage < n_stages:
            for can, copy in copies(name, stage, piece)[0]:
                guarded(can, lambda: copy().start())
        else:
            out_copies(piece, lambda copy: copy.start())
        if stage > 0:
            for can, copy in sends:
                guarded(can, lambda: copy().wait_send())

    def one_round(turn, carry):
        for spot_in in range(period):
            tick = turn * period + spot_in
            for stage in reversed(range(1, n_stages + 1)):
                piece = tick - stage * LAG
                name = PATTERN[(spot_in - stage * LAG) % period]

                @pl.when(jnp.logical_and(piece >= 0, piece < pieces))
                def _():
                    work(name, stage, jnp.clip(piece, 0, pieces - 1))

            @pl.when(tick < pieces)
            def _():
                piece = jnp.minimum(tick, pieces - 1)
                for sub in range(per_piece):
                    form(piece, sub)
                work(PATTERN[spot_in], 0, piece)
        return carry

    lax.fori_loop(0, all_rounds, one_round, 0)

    def drain(piece, carry):
        out_copies(piece, lambda copy: copy.wait())
        return carry

    lax.fori_loop(0, pieces, drain, 0)


def reduce_gradients(left, right, vec, dp_size):
    dims = factor_dims(dp_size)
    rows = 16 * dp_size
    units = 108
    pieces = (units * UNIT + vec.shape[0]) // rows
    slots = 4 * len(PATTERN)
    ring = 4 if dp_size <= 16 else 2
    land = max(stage_list(order, dims, rows)[1] for order in ORDERS.values())
    n_stages = 2 * (sum(dims) - 3)
    tokens = left.shape[1]
    total = pieces * rows
    return pl.pallas_call(
        partial(reduce_kernel, dims, pieces, rows, units),
        out_shape=[
            jax.ShapeDtypeStruct(shape, jnp.bfloat16)
            for shape in ((768, 2304), (768, 768), (768, 3072), (3072, 768), (rows, UNIT))
        ],
        in_specs=[pl.BlockSpec(memory_space=pl.ANY)] * 3,
        out_specs=[pl.BlockSpec(memory_space=pl.ANY)] * 5,
        scratch_shapes=[
            pltpu.VMEM((slots * rows, UNIT), jnp.bfloat16),
            pltpu.VMEM((slots * land, UNIT), jnp.bfloat16),
            pltpu.VMEM((total, UNIT), jnp.bfloat16),
            pltpu.VMEM((rows, UNIT), jnp.float32),
            pltpu.VMEM((ring, tokens, UNIT), jnp.bfloat16),
            pltpu.VMEM((ring, tokens, UNIT), jnp.bfloat16),
            pltpu.SemaphoreType.DMA((ring, 2)),
            pltpu.SemaphoreType.DMA,
            pltpu.SemaphoreType.DMA((total // UNIT,)),
            pltpu.SemaphoreType.DMA((slots, n_stages, 2)),
            pltpu.SemaphoreType.DMA((slots, n_stages, 2)),
        ],
        compiler_params=pltpu.CompilerParams(
            collective_id=1, has_side_effects=True, vmem_limit_bytes=62 << 20
        ),
        cost_estimate=pl.CostEstimate(
            flops=2 * units * UNIT * UNIT * tokens, bytes_accessed=120 << 20, transcendentals=0
        ),
        name="reduce",
    )(left, right, vec)


CHUNK = 256
SAVE = {"slope": 0, "u1": 3072, "u2": 3840, "q": 4608, "k": 5376, "sq": 6144, "sk": 6912, "v": 7680}
SAVE_WIDTH = 8448
STAT = {"o": 0, "rden": 768, "s1": 1536, "s2": 1664}
STAT_WIDTH = 1792
TAIL_SCALE = 0.375
TAIL_POLY = (
    0.21141059805705423,
    0.21471795439954675,
    0.17184958530833144,
    0.26915459919947066,
    -0.10973686091480542,
    0.37354383408912983,
    -0.13093832475477368,
)


def dot(left_mat, right_mat):
    return jnp.dot(left_mat, right_mat, preferred_element_type=jnp.float32)


def inverse(value):
    rough = pl.reciprocal(value, approx=True)
    return rough * (2.0 - value * rough)


def gelu_pair(hidden):
    bell = jnp.exp(hidden * hidden * -0.5)
    t = inverse(1.0 + (TAIL_SCALE * math.sqrt(0.5)) * jnp.abs(hidden))
    poly = jnp.full_like(t, 0.5 * TAIL_POLY[-1])
    for coefficient in TAIL_POLY[-2::-1]:
        poly = poly * t + 0.5 * coefficient
    tail = poly * t * bell
    below = jnp.where(hidden >= 0, 1.0 - tail, tail)
    return hidden * below, below + hidden * (bell * (1.0 / math.sqrt(2.0 * math.pi)))


def softplus_pair(value):
    small = jnp.exp(-jnp.abs(value))
    whole = 1.0 + small
    log_whole = jnp.where(
        small < 1e-2, small * (1.0 - small * (0.5 - small * (1.0 / 3.0))), jnp.log(whole)
    )
    return (
        jnp.maximum(value, 0.0) + log_whole,
        jnp.where(value >= 0, 1.0, small) * inverse(whole),
    )


def centred(rows):
    centre = rows - jnp.mean(rows, axis=-1, keepdims=True)
    scaling = lax.rsqrt(jnp.mean(centre * centre, axis=-1, keepdims=True) + EPSILON)
    return centre * scaling, scaling


def wide(column, width=128):
    return jnp.broadcast_to(column, (column.shape[0], width))


def first_half(rows):
    return lax.broadcasted_iota(jnp.int32, (rows, 128), 1) < 64


def row(ref):
    return ref[...].astype(jnp.float32)


def forward_kernel(chunks, x_hbm, wp_hbm, wo_hbm, wu_hbm, wd_hbm, bp, bo, g1, h1, bu, bd, g2, h2, mix,
                   left_hbm, save_hbm, stat_hbm, y_hbm,
                   wp, wo, wu, wd, x_in, h_out, left_buf, save_buf, stat_buf, y_buf, nums, resid,
                   w_sem, x_sem, out_sem, send_sem, recv_sem):
    section = lax.axis_index("section")
    first = section == 0
    partner = {"section": 1 - section}
    width = x_hbm.shape[1]
    pairs = width // 128

    w_copies = [
        pltpu.make_async_copy(src, dst, w_sem.at[n])
        for n, (src, dst) in enumerate(((wp_hbm, wp), (wo_hbm, wo), (wu_hbm, wu), (wd_hbm, wd)))
    ]

    def rows_of(i):
        return pl.ds(pl.multiple_of(i * CHUNK, CHUNK), CHUNK)

    def x_copy(i):
        return pltpu.make_async_copy(x_hbm.at[rows_of(i)], x_in.at[i], x_sem.at[i])

    def hand_over(i):
        return pltpu.make_async_remote_copy(
            src_ref=h_out.at[i], dst_ref=x_in.at[i], send_sem=send_sem.at[i],
            recv_sem=recv_sem.at[i], device_id=partner, device_id_type=MESH,
        )

    def out_copies(i, slot):
        return (
            pltpu.make_async_copy(
                left_buf.at[slot], left_hbm.at[:, rows_of(i), :], out_sem.at[slot, 0]
            ),
            pltpu.make_async_copy(save_buf.at[slot], save_hbm.at[rows_of(i)], out_sem.at[slot, 1]),
            pltpu.make_async_copy(stat_buf.at[slot], stat_hbm.at[rows_of(i)], out_sem.at[slot, 2]),
            pltpu.make_async_copy(y_buf.at[slot], y_hbm.at[rows_of(i)], out_sem.at[slot, 3]),
        )

    w_copies[0].start()

    @pl.when(first)
    def _():
        for i in range(chunks):
            x_copy(i).start()

    for copy in w_copies[1:]:
        copy.start()
    barrier = pltpu.get_barrier_semaphore()
    pl.semaphore_signal(barrier, inc=1, device_id=partner, device_id_type=MESH)
    pl.semaphore_wait(barrier, 1)

    def weights_ready(i, which):
        @pl.when(i == 0)
        def _():
            w_copies[which].wait()

    def body(i, carry):
        slot = lax.rem(i, 2)
        past = 1 - slot

        @pl.when(i >= 2)
        def _():
            for copy in out_copies(i - 2, slot):
                copy.wait()

        weights_ready(i, 0)

        @pl.when(first)
        def _():
            x_copy(i).wait()

        @pl.when(jnp.logical_not(first))
        def _():
            hand_over(i).wait_recv()

        left, save, stat = left_buf.at[slot], save_buf.at[slot], stat_buf.at[slot]
        old = save_buf.at[past]

        def keep(name, start, value):
            save[:, SAVE[name] + start : SAVE[name] + start + value.shape[1]] = value.astype(
                jnp.bfloat16
            )

        def blocks(first_block, value):
            for n in range(value.shape[1] // UNIT):
                left[first_block + n] = value[:, n * UNIT : (n + 1) * UNIT]

        x = x_in[i]
        blocks(18, x)
        for part, (name, slope) in enumerate((("q", "sq"), ("k", "sk"))):
            cols = slice(part * width, (part + 1) * width)
            soft, sigma = softplus_pair(dot(x, wp[:, cols]) + row(bp)[:, cols])
            keep(name, 0, soft)
            keep(slope, 0, sigma)
        cols = slice(2 * width, 3 * width)
        keep("v", 0, dot(x, wp[:, cols]) + row(bp)[:, cols])

        low = first_half(CHUNK)

        def mix_pair(pair, source, table, fresh):
            def cut(ref, name):
                return ref[:, SAVE[name] + pair * 128 : SAVE[name] + (pair + 1) * 128]

            queries, keys_in, values = cut(save, "q"), cut(source, "k"), cut(source, "v")
            zero, one = jnp.zeros_like(keys_in), jnp.ones_like(values)
            for half in range(2):
                own = low if half == 0 else jnp.logical_not(low)
                scores = back_product(queries, jnp.where(own, keys_in, zero)) * table
                num = dot(scores.astype(jnp.bfloat16), jnp.where(own, values, one))
                at = 2 * pair + half
                nums[at] = num if fresh else nums[at] + num

        for pair in range(pairs):
            mix_pair(pair, save, mix[0], True)

        @pl.when(slot == 1)
        def _():
            for pair in range(pairs):
                mix_pair(pair, old, mix[1], False)

        for pair in range(pairs):
            num_a, num_b = nums[2 * pair], nums[2 * pair + 1]
            inv = inverse(
                jnp.where(low, pltpu.roll(num_a, 64, 1), pltpu.roll(num_b, 64, 1))
            )
            mixed = jnp.where(low, num_a, num_b) * inv
            stat[:, STAT["o"] + pair * 128 : STAT["o"] + (pair + 1) * 128] = mixed
            stat[:, STAT["rden"] + pair * 128 : STAT["rden"] + (pair + 1) * 128] = inv
        blocks(15, stat[:, : width].astype(jnp.bfloat16))
        weights_ready(i, 1)
        first_sum = x.astype(jnp.float32) + row(bo)
        for n in range(3):
            first_sum += dot(left[15 + n], wo[n * UNIT : (n + 1) * UNIT, :])
        unit_one, scale_one = centred(first_sum)
        keep("u1", 0, unit_one)
        stat[:, STAT["s1"] : STAT["s1"] + 128] = wide(scale_one)
        normed = unit_one * row(g1) + row(h1)
        resid[...] = normed + row(bd)
        up_in = normed.astype(jnp.bfloat16)
        blocks(12, up_in)
        weights_ready(i, 2)
        for n in range(4):
            cols = slice(n * width, (n + 1) * width)
            active, slope = gelu_pair(dot(up_in, wu[:, cols]) + row(bu)[:, cols])
            active = active.astype(jnp.bfloat16)
            blocks(3 * n, active)
            keep("slope", n * width, slope)
            if n == 0:
                weights_ready(i, 3)
            resid[...] += dot(active, wd[cols, :])
        unit_two, scale_two = centred(resid[...])
        keep("u2", 0, unit_two)
        stat[:, STAT["s2"] : STAT["s2"] + 128] = wide(scale_two)
        result = unit_two * row(g2) + row(h2)
        y_buf[slot] = result

        @pl.when(first)
        def _():
            h_out[i] = result.astype(jnp.bfloat16)
            hand_over(i).start()

        for copy in out_copies(i, slot):
            copy.start()
        return carry

    lax.fori_loop(0, chunks, body, 0)
    for i in (chunks - 2, chunks - 1):
        for copy in out_copies(i, i % 2):
            copy.wait()

    @pl.when(first)
    def _():
        for i in range(chunks):
            hand_over(i).wait_send()


def any_specs(count):
    return [pl.BlockSpec(memory_space=pl.ANY)] * count


def vmem_specs(count):
    return [pl.BlockSpec(memory_space=pltpu.VMEM)] * count


def run_forward(x, mats, rows, mix):
    tokens, width = x.shape
    chunks = tokens // CHUNK
    return pl.pallas_call(
        partial(forward_kernel, chunks),
        out_shape=[
            jax.ShapeDtypeStruct((21, tokens, UNIT), jnp.bfloat16),
            jax.ShapeDtypeStruct((tokens, SAVE_WIDTH), jnp.bfloat16),
            jax.ShapeDtypeStruct((tokens, STAT_WIDTH), jnp.float32),
            jax.ShapeDtypeStruct((tokens, width), jnp.float32),
        ],
        in_specs=any_specs(5) + vmem_specs(9),
        out_specs=any_specs(4),
        scratch_shapes=[pltpu.VMEM(mat.shape, mat.dtype) for mat in mats]
        + [
            pltpu.VMEM((chunks, CHUNK, width), jnp.bfloat16),
            pltpu.VMEM((chunks, CHUNK, width), jnp.bfloat16),
            pltpu.VMEM((2, 21, CHUNK, UNIT), jnp.bfloat16),
            pltpu.VMEM((2, CHUNK, SAVE_WIDTH), jnp.bfloat16),
            pltpu.VMEM((2, CHUNK, STAT_WIDTH), jnp.float32),
            pltpu.VMEM((2, CHUNK, width), jnp.float32),
            pltpu.VMEM((HEADS, CHUNK, 128), jnp.float32),
            pltpu.VMEM((CHUNK, width), jnp.float32),
            pltpu.SemaphoreType.DMA((4,)),
            pltpu.SemaphoreType.DMA((chunks,)),
            pltpu.SemaphoreType.DMA((2, 4)),
            pltpu.SemaphoreType.DMA((chunks,)),
            pltpu.SemaphoreType.DMA((chunks,)),
        ],
        compiler_params=pltpu.CompilerParams(
            collective_id=2, has_side_effects=True, vmem_limit_bytes=62 << 20
        ),
        name="forward",
    )(x, *mats, *rows, mix)


VECTORS = {"bp": (0, 9), "bo": (9, 3), "g1": (12, 3), "h1": (15, 3), "bu": (18, 12), "bd": (30, 3),
           "g2": (33, 3), "h2": (36, 3)}


def backward_kernel(chunks, e_hbm, save_hbm, stat_hbm, y_hbm, wp_hbm, wo_hbm, wu_hbm, wd_hbm, g1, g2, mix,
                    right_hbm, res_hbm, vec,
                    wp, wo, wu, wd, e_in, dh_out, right_buf, save_buf, stat_buf, dx_buf, dn1, dq, dk, dv,
                    w_buf, carry_k, carry_v,
                    w_sem, e_sem, load_sem, out_sem, res_sem, send_sem, recv_sem):
    section = lax.axis_index("section")
    first = section == 0
    partner = {"section": 1 - section}
    width = e_hbm.shape[1]
    pairs = width // 128

    w_copies = [
        pltpu.make_async_copy(src, dst, w_sem.at[n])
        for n, (src, dst) in enumerate(((wd_hbm, wd), (wu_hbm, wu), (wo_hbm, wo), (wp_hbm, wp)))
    ]

    def rows_of(i):
        return pl.ds(pl.multiple_of(i * CHUNK, CHUNK), CHUNK)

    def e_copy(i):
        return pltpu.make_async_copy(e_hbm.at[rows_of(i)], e_in.at[i], e_sem.at[i])

    def hand_over(i):
        return pltpu.make_async_remote_copy(
            src_ref=dh_out.at[i], dst_ref=e_in.at[i], send_sem=send_sem.at[i],
            recv_sem=recv_sem.at[i], device_id=partner, device_id_type=MESH,
        )

    def loads(i, slot):
        return (
            pltpu.make_async_copy(save_hbm.at[rows_of(i)], save_buf.at[slot], load_sem.at[slot, 0]),
            pltpu.make_async_copy(stat_hbm.at[rows_of(i)], stat_buf.at[slot], load_sem.at[slot, 1]),
        )

    def right_copy(i, slot):
        return pltpu.make_async_copy(
            right_buf.at[slot], right_hbm.at[:, rows_of(i), :], out_sem.at[slot]
        )

    def res_copy(i, slot):
        return pltpu.make_async_copy(dx_buf.at[slot], res_hbm.at[rows_of(i)], res_sem.at[slot])

    for i in (chunks - 1, chunks - 2):
        for copy in loads(i, i % 2):
            copy.start()

    @pl.when(jnp.logical_not(first))
    def _():
        for i in reversed(range(chunks)):
            e_copy(i).start()

    for copy in w_copies:
        copy.start()
    barrier = pltpu.get_barrier_semaphore()
    pl.semaphore_signal(barrier, inc=1, device_id=partner, device_id_type=MESH)
    pl.semaphore_wait(barrier, 1)
    vec[...] = jnp.zeros_like(vec)

    def weights_ready(step, which):
        @pl.when(step == 0)
        def _():
            w_copies[which].wait()

    def tally(name, start, values):
        total = jnp.sum(values.astype(jnp.float32), axis=0, keepdims=True)
        at = VECTORS[name][0] + start // UNIT
        for n in range(values.shape[1] // UNIT):
            vec[at + n : at + n + 1, :] += total[:, n * UNIT : (n + 1) * UNIT]

    def body(step, carry):
        i = chunks - 1 - step
        slot = lax.rem(i, 2)
        past = 1 - slot

        @pl.when(step >= 2)
        def _():
            right_copy(i + 2, slot).wait()

            @pl.when(first)
            def _():
                res_copy(i + 2, slot).wait()

        @pl.when(slot == 1)
        def _():
            for copy in loads(i, 1) + loads(i - 1, 0):
                copy.wait()

        @pl.when(first)
        def _():
            hand_over(i).wait_recv()

        @pl.when(jnp.logical_not(first))
        def _():
            e_copy(i).wait()

        right, save, stat = right_buf.at[slot], save_buf.at[slot], stat_buf.at[slot]
        old = save_buf.at[past]

        def kept(name, start=0, size=width):
            return save[:, SAVE[name] + start : SAVE[name] + start + size]

        def blocks(first_block, value):
            for n in range(value.shape[1] // UNIT):
                right[first_block + n] = value[:, n * UNIT : (n + 1) * UNIT]

        def norm_back(grad, unit_rows, scaling):
            mean_grad = jnp.mean(grad, axis=-1, keepdims=True)
            mean_cross = jnp.mean(grad * unit_rows, axis=-1, keepdims=True)
            return scaling * (grad - mean_grad - unit_rows * mean_cross)

        e = e_in[i].astype(jnp.float32)
        unit_two = kept("u2").astype(jnp.float32)
        tally("g2", 0, e * unit_two)
        tally("h2", 0, e)
        second_full = norm_back(
            e * row(g2), unit_two, stat[:, STAT["s2"] : STAT["s2"] + 1]
        )
        second_low = second_full.astype(jnp.bfloat16)
        blocks(0, second_low)
        tally("bd", 0, second_low)
        dn1[...] = second_full
        weights_ready(step, 0)
        for n in range(4):
            cols = slice(n * width, (n + 1) * width)
            hidden_low = (
                back_product(second_low, wd[cols, :])
                * kept("slope", n * width).astype(jnp.float32)
            ).astype(jnp.bfloat16)
            blocks(3 + 3 * n, hidden_low)
            tally("bu", n * width, hidden_low)
            if n == 0:
                weights_ready(step, 1)
            dn1[...] += back_product(hidden_low, wu[:, cols])
        grad_normed = dn1[...]
        unit_one = kept("u1").astype(jnp.float32)
        tally("g1", 0, grad_normed * unit_one)
        tally("h1", 0, grad_normed)
        grad_first = norm_back(
            grad_normed * row(g1), unit_one, stat[:, STAT["s1"] : STAT["s1"] + 1]
        )
        dn1[...] = grad_first
        first_low = grad_first.astype(jnp.bfloat16)
        blocks(15, first_low)
        tally("bo", 0, first_low)
        weights_ready(step, 2)
        grad_mixed = back_product(first_low, wo[...]).astype(jnp.bfloat16).astype(jnp.float32)
        w_buf[...] = (grad_mixed * stat[:, STAT["rden"] : STAT["rden"] + width]).astype(
            jnp.bfloat16
        )

        lanes = lax.broadcasted_iota(jnp.int32, (CHUNK, 128), 1)
        low = lanes < 64

        def pair_back(pair, source, table, target_k, target_v, fresh):
            span = slice(pair * 128, (pair + 1) * 128)

            def cut(ref, name):
                return ref[:, SAVE[name] + pair * 128 : SAVE[name] + (pair + 1) * 128]

            queries, keys_in, values = cut(save, "q"), cut(source, "k"), cut(source, "v")
            weighed = w_buf[:, span]
            cross = weighed.astype(jnp.float32) * stat[:, span]
            zero, one = jnp.zeros_like(keys_in), jnp.ones_like(values)
            total_q, total_k, total_v = 0.0, 0.0, 0.0
            for half in range(2):
                own = low if half == 0 else jnp.logical_not(low)
                spare = 64 * (1 - half)
                inner = jnp.sum(jnp.where(own, cross, 0.0), axis=-1, keepdims=True)
                rough = inner.astype(jnp.bfloat16).astype(jnp.float32)
                extra = jnp.where(
                    lanes == spare, -rough, jnp.where(lanes == spare + 1, rough - inner, 0.0)
                ).astype(jnp.bfloat16)
                own_keys = jnp.where(own, keys_in, zero)
                scores = (back_product(queries, own_keys) * table).astype(jnp.bfloat16)
                grads = (
                    back_product(
                        jnp.where(own, weighed, extra), jnp.where(own, values, one)
                    )
                    * table
                ).astype(jnp.bfloat16)
                total_q += dot(grads, own_keys)
                total_k += rows_product(grads, jnp.where(own, queries, zero))
                total_v += rows_product(scores, jnp.where(own, weighed, zero))
            if fresh:
                dq[:, span] = total_q
            else:
                dq[:, span] += total_q
            target_k[:, span] = total_k
            target_v[:, span] = total_v

        for pair in range(pairs):
            pair_back(pair, save, mix[0], dk, dv, True)

        @pl.when(slot == 0)
        def _():
            dk[...] += carry_k[...]
            dv[...] += carry_v[...]

        @pl.when(slot == 1)
        def _():
            for pair in range(pairs):
                pair_back(pair, old, mix[1], carry_k, carry_v, False)

        weights_ready(step, 3)
        grad_in = dn1[...]
        for n, values in enumerate(
            (
                dq[...] * kept("sq").astype(jnp.float32),
                dk[...] * kept("sk").astype(jnp.float32),
                dv[...],
            )
        ):
            values = values.astype(jnp.bfloat16)
            blocks(18 + 3 * n, values)
            tally("bp", n * width, values)
            grad_in += back_product(values, wp[:, n * width : (n + 1) * width])

        @pl.when(first)
        def _():
            dx_buf[slot] = grad_in
            res_copy(i, slot).start()

        @pl.when(jnp.logical_not(first))
        def _():
            dh_out[i] = grad_in.astype(jnp.bfloat16)
            hand_over(i).start()

        right_copy(i, slot).start()

        @pl.when(jnp.logical_and(slot == 0, i >= 2))
        def _():
            for copy in loads(i - 1, 1) + loads(i - 2, 0):
                copy.start()

        return carry

    lax.fori_loop(0, chunks, body, 0)
    for i in (1, 0):
        right_copy(i, i).wait()

    @pl.when(first)
    def _():
        for i in (1, 0):
            res_copy(i, i).wait()

    @pl.when(jnp.logical_not(first))
    def _():
        for i in range(chunks):
            hand_over(i).wait_send()


def run_backward(e, save, stat, y, mats, gains, mix, vec_rows):
    tokens, width = e.shape
    chunks = tokens // CHUNK
    wp, wo, wu, wd = mats
    return pl.pallas_call(
        partial(backward_kernel, chunks),
        out_shape=[
            jax.ShapeDtypeStruct((27, tokens, UNIT), jnp.bfloat16),
            jax.ShapeDtypeStruct((tokens, width), jnp.float32),
            jax.ShapeDtypeStruct((vec_rows, UNIT), jnp.float32),
        ],
        in_specs=any_specs(8) + vmem_specs(3),
        out_specs=any_specs(2) + vmem_specs(1),
        input_output_aliases={3: 1},
        scratch_shapes=[pltpu.VMEM(mat.shape, mat.dtype) for mat in (wp, wo, wu, wd)]
        + [
            pltpu.VMEM((chunks, CHUNK, width), jnp.bfloat16),
            pltpu.VMEM((chunks, CHUNK, width), jnp.bfloat16),
            pltpu.VMEM((2, 27, CHUNK, UNIT), jnp.bfloat16),
            pltpu.VMEM((2, CHUNK, SAVE_WIDTH), jnp.bfloat16),
            pltpu.VMEM((2, CHUNK, STAT_WIDTH), jnp.float32),
            pltpu.VMEM((2, CHUNK, width), jnp.float32),
            pltpu.VMEM((CHUNK, width), jnp.float32),
            pltpu.VMEM((CHUNK, width), jnp.float32),
            pltpu.VMEM((CHUNK, width), jnp.float32),
            pltpu.VMEM((CHUNK, width), jnp.float32),
            pltpu.VMEM((CHUNK, width), jnp.bfloat16),
            pltpu.VMEM((CHUNK, width), jnp.float32),
            pltpu.VMEM((CHUNK, width), jnp.float32),
            pltpu.SemaphoreType.DMA((4,)),
            pltpu.SemaphoreType.DMA((chunks,)),
            pltpu.SemaphoreType.DMA((2, 2)),
            pltpu.SemaphoreType.DMA((2,)),
            pltpu.SemaphoreType.DMA((2,)),
            pltpu.SemaphoreType.DMA((chunks,)),
            pltpu.SemaphoreType.DMA((chunks,)),
        ],
        compiler_params=pltpu.CompilerParams(
            collective_id=3, has_side_effects=True, vmem_limit_bytes=62 << 20
        ),
        name="backward",
    )(e, save, stat, y, wp, wo, wu, wd, *gains, mix)


def mix_tables(length):
    later = lax.broadcasted_iota(jnp.int32, (CHUNK, CHUNK), 0)
    earlier = lax.broadcasted_iota(jnp.int32, (CHUNK, CHUNK), 1)
    unit = (0.5 * math.pi) / length.astype(jnp.float32)
    seen = jnp.logical_and(later // length == earlier // length, later >= earlier)
    near = jnp.where(seen, jnp.cos((later - earlier).astype(jnp.float32) * unit), 0.0)
    far = jnp.where(
        length > CHUNK, jnp.cos((later + CHUNK - earlier).astype(jnp.float32) * unit), 0.0
    )
    return jnp.stack([near, far])


def shards(
    endpoints,
    projection,
    projection_bias,
    output_weight,
    output_bias,
    first_gain,
    first_shift,
    up_weight,
    up_bias,
    down_weight,
    down_bias,
    second_gain,
    second_shift,
    segment_length,
):
    dp_size = lax.axis_size("dp")
    mats = (projection[0], output_weight[0], up_weight[0], down_weight[0])
    rows = (
        projection_bias, output_bias, first_gain, first_shift, up_bias, down_bias, second_gain,
        second_shift,
    )
    mix = mix_tables(segment_length[0])
    left, save, stat, y = run_forward(endpoints[0], mats, rows, mix)
    right, results, vec = run_backward(
        endpoints[0], save, stat, y, mats, (first_gain, second_gain), mix, 16 * dp_size
    )
    proj, out, up, down, small = reduce_gradients(left, right, vec, dp_size)
    small = small[:39].astype(jnp.float32)

    def vector(name):
        start, count = VECTORS[name]
        return small[start : start + count].reshape(1, count * UNIT)

    def whole(mat):
        return mat.astype(jnp.float32)[None]

    return (
        results[None], whole(proj), vector("bp"), whole(out), vector("bo"), vector("g1"),
        vector("h1"), whole(up), vector("bu"), whole(down), vector("bd"), vector("g2"),
        vector("h2"),
    )


def solution(mesh):
    in_specs = (
        P("section", "dp", None),
        P("section", None, None),
        P("section", None),
        P("section", None, None),
        P("section", None),
        P("section", None),
        P("section", None),
        P("section", None, None),
        P("section", None),
        P("section", None, None),
        P("section", None),
        P("section", None),
        P("section", None),
        P("dp"),
    )
    out_specs = (
        P("section", "dp", None),
        P("section", None, None),
        P("section", None),
        P("section", None, None),
        P("section", None),
        P("section", None),
        P("section", None),
        P("section", None, None),
        P("section", None),
        P("section", None, None),
        P("section", None),
        P("section", None),
        P("section", None),
    )
    return jax.shard_map(shards, mesh=mesh, in_specs=in_specs, out_specs=out_specs, check_vma=False)
```

```python
from functools import partial
import math

import jax
import jax.numpy as jnp
from jax import lax
from jax.experimental import pallas as pl
from jax.experimental.pallas import tpu as pltpu
from jax.sharding import PartitionSpec as P

HEADS = 12
EPSILON = 1e-05
MESH = pl.DeviceIdType.MESH


def rows_product(left_mat, right_mat):
    return lax.dot_general(
        left_mat, right_mat, (((0,), (0,)), ((), ())), preferred_element_type=jnp.float32
    )


def back_product(grad_mat, weight_mat):
    return lax.dot_general(
        grad_mat, weight_mat, (((1,), (1,)), ((), ())), preferred_element_type=jnp.float32
    )


def factor_dims(count):
    bits = count.bit_length() - 1
    return (1 << (bits // 3), 1 << ((bits + 1) // 3), 1 << ((bits + 2) // 3))


ORDERS = {"a": (0, 1, 2), "b": (1, 2, 0), "c": (2, 0, 1)}
PATTERN = "abacabc"
LAG = 3
OUT_LAG = 4
UNIT = 256
UNITS = 108
PIECE_ROWS = 512
SEM_SLOTS = 35


def stage_list(order, dims, rows):
    stages, size, landing = [], rows, 0
    for level, ax in enumerate(order):
        part = size // dims[ax]
        for step in range(1, dims[ax]):
            stages.append(("reduce", level, ax, step, part, landing))
            landing += part if dims[ax] == 2 else 2 * part
        size = part
    for level in reversed(range(3)):
        ax = order[level]
        for step in range(1, dims[ax]):
            stages.append(("gather", level, ax, step, size, 0))
        size *= dims[ax]
    return stages, landing


def unit_blocks(unit):
    up, out, proj = unit - 36, unit - 72, unit - 81
    left = jnp.where(
        unit < 36,
        unit // 3,
        jnp.where(unit < 72, 12 + up // 12, jnp.where(unit < 81, 15 + out // 3, 18 + proj // 9)),
    )
    right = jnp.where(
        unit < 36,
        unit % 3,
        jnp.where(unit < 72, 3 + up % 12, jnp.where(unit < 81, 15 + out % 3, 18 + proj % 9)),
    )
    return left, right


def axis_places(dims):
    here = lax.axis_index("dp")
    strides = (1, dims[0], dims[0] * dims[1])
    return here, strides, [(here // strides[ax]) % dims[ax] for ax in range(3)]


def greet_axes(dims, semaphore):
    here, strides, place = axis_places(dims)
    around = 0
    for ax in range(3):
        for sign, can in ((1, place[ax] < dims[ax] - 1), (-1, place[ax] > 0)):
            @pl.when(can)
            def _():
                pl.semaphore_signal(
                    semaphore, inc=1, device_id={"dp": here + sign * strides[ax]},
                    device_id_type=MESH,
                )
            around = around + can.astype(jnp.int32)
    return around


def gather_sends(spot, count):
    found = {}
    for at in range(count):
        sent = (at + 1 if at < count - 1 else 0) + (count - at if at > 0 else 0)
        found.setdefault(sent, []).append(spot == at)
    options = []
    for sent, spots in found.items():
        can = spots[0]
        for other in spots[1:]:
            can = jnp.logical_or(can, other)
        options.append((can, sent))
    return options


def guarded(can, action):
    if can is None:
        action()
    else:
        pl.when(can)(action)


def summing(dims, pieces, rows, acc, acc_slots, full, full_slots, landing, land_slots, left_hbm,
            right_hbm, vec, outs, left_ring, right_ring, load_sem, out_sem, send_sem, recv_sem):
    here, strides, place = axis_places(dims)
    proj_hbm, out_hbm, up_hbm, down_hbm, small_hbm = outs
    ring, chunks = left_ring.shape[0], left_ring.shape[1]
    per_piece = rows // UNIT
    land_rows = landing.shape[0] // land_slots
    plans = {name: stage_list(order, dims, rows)[0] for name, order in ORDERS.items()}
    n_stages = len(plans["a"])
    shard = rows // (dims[0] * dims[1] * dims[2])
    period = len(PATTERN)

    bases = {}
    for name, order in ORDERS.items():
        base, size, found = 0, rows, []
        for ax in order:
            found.append(base)
            size = size // dims[ax]
            base = base + place[ax] * size
        bases[name] = found + [base]

    sent_rows = {}
    for name, plan in plans.items():
        sure, options = 0, [(None, 0)]
        for kind, _, ax, step, part, _ in plan:
            if dims[ax] == 2 or kind == "reduce":
                sure += part
            elif step == 1:
                options = [
                    (can if other is None else jnp.logical_and(can, other), more + part * count)
                    for other, more in options
                    for can, count in gather_sends(place[ax], dims[ax])
                ]
        sent_rows[name] = [(can, sure + more) for can, more in options]

    def view(ref, slot, start, size):
        across = ref.shape[1] // UNIT
        first = pl.multiple_of(slot // across * rows + start, 16)
        if across == 1:
            return ref.at[pl.ds(first, size)]
        return ref.at[pl.ds(first, size), pl.ds(pl.multiple_of(slot % across * UNIT, UNIT), UNIT)]

    def loads(unit):
        slot = unit % ring
        left, right = unit_blocks(unit)
        return (
            pltpu.make_async_copy(left_hbm.at[left], left_ring.at[slot], load_sem.at[slot, 0]),
            pltpu.make_async_copy(right_hbm.at[right], right_ring.at[slot], load_sem.at[slot, 1]),
        )

    def prime():
        for unit in range(ring):
            for copy in loads(jnp.int32(unit)):
                copy.start()

    def form(piece, sub):
        unit = piece * per_piece + sub
        target = view(acc, piece % acc_slots, sub * UNIT, UNIT)

        @pl.when(unit < UNITS)
        def _():
            for copy in loads(unit):
                copy.wait()
            slot = unit % ring
            tokens = chunks * left_ring.shape[2]
            target[...] = rows_product(
                left_ring[slot].reshape(tokens, UNIT), right_ring[slot].reshape(tokens, UNIT)
            ).astype(jnp.bfloat16)

            @pl.when(unit + ring < UNITS)
            def _():
                for copy in loads(unit + ring):
                    copy.start()

        @pl.when(unit >= UNITS)
        def _():
            target[...] = vec[sub * UNIT : (sub + 1) * UNIT, :].astype(jnp.bfloat16)

    def copies(name, stage, piece):
        kind, level, ax, step, part, land = plans[name][stage]
        count, spot = dims[ax], place[ax]
        slot = piece % SEM_SLOTS
        held, index = (acc, piece % acc_slots) if kind == "reduce" else (full, piece % full_slots)
        land_start = piece % land_slots * land_rows + land

        def chunk(q):
            return view(held, index, bases[name][level] + q * part, part)

        def landed(way):
            return landing.at[pl.ds(pl.multiple_of(land_start + way * part, 16), part)]

        def remote(src, dst, way, sign):
            return lambda: pltpu.make_async_remote_copy(
                src_ref=src, dst_ref=dst, send_sem=send_sem.at[slot],
                recv_sem=recv_sem.at[slot, stage, way],
                device_id={"dp": here + sign * strides[ax]}, device_id_type=MESH,
            )

        sends, receives = [], []
        if count == 2:
            sign = 1 - 2 * spot
            mine, other = spot, 1 - spot
            if kind == "reduce":
                sends.append((None, remote(chunk(other), landed(0), 0, sign)))
                receives.append((None, remote(chunk(mine), landed(0), 0, sign), mine, landed(0)))
            else:
                sends.append((None, remote(chunk(mine), chunk(mine), 0, sign)))
                receives.append((None, remote(chunk(other), chunk(other), 0, sign), other, None))
            return sends, receives, chunk
        back = count - 1 - spot
        if kind == "reduce":
            for way, sign, can, q in (
                (0, 1, spot < step, spot + count - step),
                (1, -1, back < step, step - 1 - back),
            ):
                q = jnp.clip(q, 0, count - 1)
                sends.append((can, remote(chunk(q), landed(way), way, sign)))
            for way, sign, can, q in (
                (0, 1, jnp.logical_and(spot >= 1, spot - 1 < step), spot - 1 + count - step),
                (1, -1, jnp.logical_and(back >= 1, back - 1 < step), step - back),
            ):
                q = jnp.clip(q, 0, count - 1)
                receives.append((can, remote(chunk(q), landed(way), way, sign), q, landed(way)))
        else:
            for way, sign, can, q in (
                (0, 1, jnp.logical_and(back >= 1, spot >= step - 1), spot - step + 1),
                (1, -1, jnp.logical_and(spot >= 1, back >= step - 1), spot + step - 1),
            ):
                q = jnp.clip(q, 0, count - 1)
                sends.append((can, remote(chunk(q), chunk(q), way, sign)))
            for way, sign, can, q in (
                (0, 1, spot >= step, spot - step),
                (1, -1, back >= step, spot + step),
            ):
                q = jnp.clip(q, 0, count - 1)
                receives.append((can, remote(chunk(q), chunk(q), way, sign), q, None))
        return sends, receives, chunk

    def out_copies(piece, action):
        for sub in range(per_piece):
            unit = piece * per_piece + sub
            source = view(full, piece % full_slots, sub * UNIT, UNIT)
            for begin, end, across, target in (
                (0, 36, 3, down_hbm), (36, 72, 12, up_hbm), (72, 81, 3, out_hbm),
                (81, 108, 9, proj_hbm), (108, 108 + per_piece, 1, small_hbm),
            ):
                @pl.when(jnp.logical_and(unit >= begin, unit < end))
                def _():
                    local = jnp.clip(unit - begin, 0, end - begin - 1)
                    place_in = target.at[
                        pl.ds(pl.multiple_of(local // across * UNIT, UNIT), UNIT),
                        pl.ds(pl.multiple_of(local % across * UNIT, UNIT), UNIT),
                    ]
                    action(pltpu.make_async_copy(source, place_in, out_sem.at[unit]))

    def work(name, stage, piece):
        if stage > 0:
            sends, receives, chunk = copies(name, stage - 1, piece)
            for can, copy, q, landed in receives:
                def finish():
                    copy().wait_recv()
                    if landed is not None:
                        block = chunk(q)
                        block[...] = block[...] + landed[...]
                guarded(can, finish)
        if stage == n_stages // 2:
            mine = bases[name][3]
            own = view(full, piece % full_slots, mine, shard)
            own[...] = view(acc, piece % acc_slots, mine, shard)[...]
        if stage < n_stages:
            for can, copy in copies(name, stage, piece)[0]:
                guarded(can, lambda: copy().start())
        else:
            out_copies(piece, lambda copy: copy.start())
        if stage == n_stages:
            for can, amount in sent_rows[name]:
                sent = landing.at[pl.ds(0, amount)]
                guarded(
                    can,
                    lambda: pltpu.make_async_copy(
                        sent, sent, send_sem.at[piece % SEM_SLOTS]
                    ).wait(),
                )

    def tick(now):
        oldest = now - n_stages * LAG - OUT_LAG

        @pl.when(jnp.logical_and(oldest >= 0, oldest < pieces))
        def _():
            out_copies(jnp.clip(oldest, 0, pieces - 1), lambda copy: copy.wait())

        for stage in reversed(range(n_stages + 1)):
            piece = now - stage * LAG
            alive = jnp.logical_and(piece >= 0, piece < pieces)
            piece = jnp.clip(piece, 0, pieces - 1)
            spot_in = piece % period

            def on(name):
                found = False
                for n in range(period):
                    if PATTERN[n] == name:
                        found = jnp.logical_or(found, spot_in == n)
                return found

            if stage == 0:
                @pl.when(alive)
                def _():
                    for sub in range(per_piece):
                        form(piece, sub)

            for name in ORDERS:
                @pl.when(jnp.logical_and(alive, on(name)))
                def _():
                    work(name, stage, piece)

    return prime, tick, pieces + n_stages * LAG + OUT_LAG


def sum_sizes(dp_size):
    dims = factor_dims(dp_size)
    rows = max(PIECE_ROWS, 16 * dp_size)
    land = max(stage_list(order, dims, rows)[1] for order in ORDERS.values())
    return dims, rows, -(-(UNITS + 1) * UNIT // rows), land, 2 * (sum(dims) - 3)


def sum_out_shapes(rows):
    return [
        jax.ShapeDtypeStruct(shape, jnp.bfloat16)
        for shape in ((768, 2304), (768, 768), (768, 3072), (3072, 768), (rows, UNIT))
    ]


def sum_semaphores(ring, rows, pieces, stages):
    return [
        pltpu.SemaphoreType.DMA((ring, 2)),
        pltpu.SemaphoreType.DMA((pieces * rows // UNIT,)),
        pltpu.SemaphoreType.DMA((SEM_SLOTS,)),
        pltpu.SemaphoreType.DMA((SEM_SLOTS, stages, 2)),
    ]


def reduce_kernel(dims, pieces, rows, left_hbm, right_hbm, vec, proj_hbm, out_hbm, up_hbm, down_hbm,
                  small_hbm, acc, full, landing, left_ring, right_ring, load_sem, out_sem, send_sem,
                  recv_sem):
    barrier = pltpu.get_barrier_semaphore()
    around = greet_axes(dims, barrier)
    pl.semaphore_wait(barrier, around)
    slots = acc.shape[0] // rows
    prime, tick, ticks = summing(
        dims, pieces, rows, acc, slots, full, pieces, landing, slots, left_hbm, right_hbm,
        vec, (proj_hbm, out_hbm, up_hbm, down_hbm, small_hbm), left_ring, right_ring, load_sem,
        out_sem, send_sem, recv_sem,
    )
    prime()

    def body(now, carry):
        tick(now)
        return carry

    lax.fori_loop(0, ticks, body, 0)


def reduce_gradients(left, right, vec, dp_size):
    dims, rows, pieces, land, stages = sum_sizes(dp_size)
    ring = 4 if dp_size <= 16 else 2
    slots = min(SEM_SLOTS, pieces)
    return pl.pallas_call(
        partial(reduce_kernel, dims, pieces, rows),
        out_shape=sum_out_shapes(rows),
        in_specs=any_specs(2) + vmem_specs(1),
        out_specs=any_specs(5),
        scratch_shapes=[
            pltpu.VMEM((slots * rows, UNIT), jnp.bfloat16),
            pltpu.VMEM((pieces * rows, UNIT), jnp.bfloat16),
            pltpu.VMEM((slots * land, UNIT), jnp.bfloat16),
            pltpu.VMEM((ring,) + left.shape[1:], jnp.bfloat16),
            pltpu.VMEM((ring,) + left.shape[1:], jnp.bfloat16),
        ]
        + sum_semaphores(ring, rows, pieces, stages),
        compiler_params=pltpu.CompilerParams(
            collective_id=1, has_side_effects=True, vmem_limit_bytes=62 << 20
        ),
        name="reduce",
    )(left, right, vec)


CHUNK = 256
KEEP_A = {"slope": 0, "u1": 3072, "u2": 3840}
KEEP_A_WIDTH = 4608
STAT_A = {"rden": 0, "s1": 768, "s2": 896}
STAT_A_WIDTH = 1024
KEEP_B = {"q": 0, "k": 768, "sq": 1536, "sk": 2304, "v": 3072}
KEEP_B_WIDTH = 3840
VECTORS = {
    "bp": (0, 9), "bo": (9, 3), "g1": (12, 3), "h1": (15, 3), "bu": (18, 12), "bd": (30, 3), "g2": (33, 3),
    "h2": (36, 3),
}
TAIL_SCALE = 0.375
TAIL_POLY = (
    0.21141059805705423,
    0.21471795439954675,
    0.17184958530833144,
    0.26915459919947066,
    -0.10973686091480542,
    0.37354383408912983,
    -0.13093832475477368,
)


def dot(left_mat, right_mat):
    return jnp.dot(left_mat, right_mat, preferred_element_type=jnp.float32)


def inverse(value):
    rough = pl.reciprocal(value, approx=True)
    return rough * (2.0 - value * rough)


def gelu_pair(hidden):
    bell = jnp.exp(hidden * hidden * -0.5)
    t = inverse(1.0 + (TAIL_SCALE * math.sqrt(0.5)) * jnp.abs(hidden))
    poly = jnp.full_like(t, 0.5 * TAIL_POLY[-1])
    for coefficient in TAIL_POLY[-2::-1]:
        poly = poly * t + 0.5 * coefficient
    tail = poly * t * bell
    below = jnp.where(hidden >= 0, 1.0 - tail, tail)
    return hidden * below, below + hidden * (bell * (1.0 / math.sqrt(2.0 * math.pi)))


def softplus_pair(value):
    small = jnp.exp(-jnp.abs(value))
    whole = 1.0 + small
    log_whole = jnp.where(
        small < 1e-2, small * (1.0 - small * (0.5 - small * (1.0 / 3.0))), jnp.log(whole)
    )
    return (
        jnp.maximum(value, 0.0) + log_whole,
        jnp.where(value >= 0, 1.0, small) * inverse(whole),
    )


def centred(rows):
    centre = rows - jnp.mean(rows, axis=-1, keepdims=True)
    scaling = lax.rsqrt(jnp.mean(centre * centre, axis=-1, keepdims=True) + EPSILON)
    return centre * scaling, scaling


def wide(column, width=128):
    return jnp.broadcast_to(column, (column.shape[0], width))


def first_half(rows):
    return lax.broadcasted_iota(jnp.int32, (rows, 128), 1) < 64


def row(ref):
    return ref[...].astype(jnp.float32)


def any_specs(count):
    return [pl.BlockSpec(memory_space=pl.ANY)] * count


def vmem_specs(count):
    return [pl.BlockSpec(memory_space=pltpu.VMEM)] * count


def norm_back(grad, unit_rows, scaling):
    mean_grad = jnp.mean(grad, axis=-1, keepdims=True)
    mean_cross = jnp.mean(grad * unit_rows, axis=-1, keepdims=True)
    return scaling * (grad - mean_grad - unit_rows * mean_cross)


def layers_kernel(chunks, *refs):
    (ends_hbm, wp_hbm, wo_hbm, wu_hbm, wd_hbm, bp, bo, g1, h1, bu, bd, g2, h2, mix) = refs[:14]
    left_hbm, right_hbm = refs[14:16]
    own_hbm, peer_hbm, peer_w_hbm = refs[16:20], refs[20:24], refs[24:28]
    res_hbm, vec_out = refs[28:30]
    (wp, wo, wu, wd, x_in, e_in, handed, left, right, keep_a, stat_a, keep_b, stat_b, rows_out, nums, dq,
     dk, dv, carry_k, carry_v, dn1, weighed, vec, vec_sent, vec_peer, gains, gains_peer, w_sem, x_sem, xo_sem, e_sem, left_sem,
     right_sem, load_sem, res_sem, send_f, recv_f, send_b, recv_b, send_w, recv_w, send_e, recv_e,
     send_k, recv_k, send_r, recv_r, send_v, recv_v, send_g, recv_g) = refs[30:]

    section = lax.axis_index("section")
    first = section == 0
    second = jnp.logical_not(first)
    partner = {"section": 1 - section}
    width = ends_hbm.shape[1]
    pairs = width // 128
    half = chunks // 2
    mats_hbm, mats = (wp_hbm, wo_hbm, wu_hbm, wd_hbm), (wp, wo, wu, wd)
    kept_bufs = (keep_a, stat_a, keep_b, stat_b)

    def w_copy(which, sources=mats_hbm):
        return pltpu.make_async_copy(sources[which], mats[which], w_sem.at[which])

    def remote(src, dst, send, recv):
        return pltpu.make_async_remote_copy(
            src_ref=src, dst_ref=dst, send_sem=send, recv_sem=recv, device_id=partner,
            device_id_type=MESH,
        )

    def w_push(which):
        return remote(mats_hbm[which], peer_w_hbm[which], send_w.at[which], recv_w.at[which])

    def rows_of(i):
        return pl.ds(pl.multiple_of(i * CHUNK, CHUNK), CHUNK)

    def x_copy(i):
        return pltpu.make_async_copy(ends_hbm.at[rows_of(i)], x_in.at[i], x_sem.at[i])

    def x_out_copies(i):
        return [
            pltpu.make_async_copy(
                x_in.at[i, :, n * UNIT : (n + 1) * UNIT], left_hbm.at[18 + n, i], xo_sem.at[i, n]
            )
            for n in range(3)
        ]

    def e_copy(i):
        return pltpu.make_async_copy(ends_hbm.at[rows_of(i)], e_in.at[i], e_sem.at[i])

    def e_push(i):
        return remote(ends_hbm.at[rows_of(i)], e_in.at[i], send_e.at[i], recv_e.at[i])

    def hand_on(i):
        return remote(handed.at[i], x_in.at[i], send_f.at[i], recv_f.at[i])

    def hand_back(i):
        return remote(handed.at[i], e_in.at[i], send_b.at[i], recv_b.at[i])

    def left_copy(i):
        return pltpu.make_async_copy(left, left_hbm.at[0:18, i], left_sem)

    spans = ((0, 15), (15, 18), (18, 27))

    def right_copy(i, n):
        start, end = spans[n]
        return pltpu.make_async_copy(
            right.at[start:end], right_hbm.at[start:end, i], right_sem.at[n]
        )

    def right_push(i, n):
        start, end = spans[n]
        return remote(
            right.at[start:end], right_hbm.at[start:end, i], send_r.at[n], recv_r.at[i, n]
        )

    def save(i, slot, n):
        return pltpu.make_async_copy(
            kept_bufs[n].at[slot], own_hbm[n].at[rows_of(i)], load_sem.at[slot, n]
        )

    def push(i, slot, n):
        return remote(
            kept_bufs[n].at[slot], peer_hbm[n].at[rows_of(i)], send_k.at[i, n], recv_k.at[i, n]
        )

    def load(i, slot, n, source):
        return pltpu.make_async_copy(
            source[n].at[rows_of(i)], kept_bufs[n].at[slot], load_sem.at[slot, n]
        )

    def res_copy(i):
        return pltpu.make_async_copy(rows_out, res_hbm.at[rows_of(i)], res_sem)

    def own_gains():
        gains[0:1, :] = row(g1)
        gains[1:2, :] = row(g2)

    def gains_push():
        return remote(gains, gains_peer, send_g, recv_g)

    def vec_push():
        return remote(vec_sent, vec_peer, send_v, recv_v)

    @pl.when(first)
    def _():
        x_copy(0).start()

    for which in range(4):
        w_copy(which).start()

    @pl.when(first)
    def _():
        for i in range(1, chunks):
            x_copy(i).start()

    @pl.when(second)
    def _():
        for i in range(half, chunks):
            e_copy(i).start()

    barrier = pltpu.get_barrier_semaphore()
    pl.semaphore_signal(barrier, inc=1, device_id=partner, device_id_type=MESH)
    vec[...] = jnp.zeros_like(vec)
    gains[...] = jnp.zeros_like(gains)
    own_gains()
    pl.semaphore_wait(barrier, 1)

    @pl.when(second)
    def _():
        gains_push().start()
        for i in range(half):
            e_push(i).start()
        for which in (3, 2, 1, 0):
            w_push(which).start()

    def weights_ready(i, which):
        @pl.when(i == 0)
        def _():
            w_copy(which).wait()

    lanes = lax.broadcasted_iota(jnp.int32, (CHUNK, 128), 1)
    low = lanes < 64

    def forward_chunk(i, carry):
        slot = lax.rem(i, 2)

        @pl.when(i >= 2)
        def _():
            @pl.when(first)
            def _():
                for n in range(4):
                    save(i - 2, slot, n).wait()

            @pl.when(second)
            def _():
                for n in range(4):
                    push(i - 2, slot, n).wait_send()

        weights_ready(i, 0)

        @pl.when(first)
        def _():
            x_copy(i).wait()

        @pl.when(second)
        def _():
            hand_on(i).wait_recv()

        for copy in x_out_copies(i):
            copy.start()
        now_a, now_b, old_b = keep_a.at[slot], keep_b.at[slot], keep_b.at[1 - slot]

        def keep(ref, start, value):
            ref[:, start : start + value.shape[1]] = value.astype(jnp.bfloat16)

        def blocks(first_block, value):
            for n in range(value.shape[1] // UNIT):
                left[first_block + n] = value[:, n * UNIT : (n + 1) * UNIT]

        x = x_in[i]
        for part, (name, slope) in enumerate((("q", "sq"), ("k", "sk"))):
            cols = slice(part * width, (part + 1) * width)
            soft, sigma = softplus_pair(dot(x, wp[:, cols]) + row(bp)[:, cols])
            keep(now_b, KEEP_B[name], soft)
            keep(now_b, KEEP_B[slope], sigma)
        cols = slice(2 * width, 3 * width)
        keep(now_b, KEEP_B["v"], dot(x, wp[:, cols]) + row(bp)[:, cols])

        def mix_pair(pair, source, table, fresh):
            def cut(ref, name):
                return ref[:, KEEP_B[name] + pair * 128 : KEEP_B[name] + (pair + 1) * 128]

            queries, keys_in, values = cut(now_b, "q"), cut(source, "k"), cut(source, "v")
            zero, one = jnp.zeros_like(keys_in), jnp.ones_like(values)
            for half in range(2):
                own = low if half == 0 else jnp.logical_not(low)
                scores = back_product(queries, jnp.where(own, keys_in, zero)) * table
                num = dot(scores.astype(jnp.bfloat16), jnp.where(own, values, one))
                at = 2 * pair + half
                nums[at] = num if fresh else nums[at] + num

        for pair in range(pairs):
            mix_pair(pair, now_b, mix[0], True)

        @pl.when(slot == 1)
        def _():
            for pair in range(pairs):
                mix_pair(pair, old_b, mix[1], False)

        @pl.when(i >= 1)
        def _():
            left_copy(i - 1).wait()

        for pair in range(pairs):
            num_a, num_b = nums[2 * pair], nums[2 * pair + 1]
            inv = inverse(
                jnp.where(low, pltpu.roll(num_a, 64, 1), pltpu.roll(num_b, 64, 1))
            )
            span = slice(pair * 128, (pair + 1) * 128)
            stat_b[slot, :, span] = jnp.where(low, num_a, num_b) * inv
            stat_a[slot, :, span] = inv
        blocks(15, stat_b[slot].astype(jnp.bfloat16))
        weights_ready(i, 1)
        first_sum = x.astype(jnp.float32) + row(bo)
        for n in range(3):
            first_sum += dot(left[15 + n], wo[n * UNIT : (n + 1) * UNIT, :])
        unit_one, scale_one = centred(first_sum)
        keep(now_a, KEEP_A["u1"], unit_one)
        stat_a[slot, :, STAT_A["s1"] : STAT_A["s1"] + 128] = wide(scale_one)
        normed = unit_one * row(g1) + row(h1)
        resid = dn1
        resid[...] = normed + row(bd)
        up_in = normed.astype(jnp.bfloat16)
        blocks(12, up_in)
        weights_ready(i, 2)

        def hidden_of(n):
            cols = slice(n * width, (n + 1) * width)
            return dot(up_in, wu[:, cols]) + row(bu)[:, cols]

        hidden = hidden_of(0)
        for n in range(4):
            later = hidden_of(n + 1) if n < 3 else None
            active, slope = gelu_pair(hidden)
            active = active.astype(jnp.bfloat16)
            blocks(3 * n, active)
            keep(now_a, n * width, slope)
            if n == 0:
                weights_ready(i, 3)
            resid[...] += dot(active, wd[n * width : (n + 1) * width, :])
            hidden = later
        unit_two, scale_two = centred(resid[...])
        keep(now_a, KEEP_A["u2"], unit_two)
        stat_a[slot, :, STAT_A["s2"] : STAT_A["s2"] + 128] = wide(scale_two)
        result = unit_two * row(g2) + row(h2)

        @pl.when(first)
        def _():
            handed[i] = result.astype(jnp.bfloat16)
            hand_on(i).start()

        @pl.when(second)
        def _():
            @pl.when(i >= 1)
            def _():
                res_copy(i - 1).wait()

            rows_out[...] = result
            res_copy(i).start()

        left_copy(i).start()

        @pl.when(first)
        def _():
            for n in range(4):
                save(i, slot, n).start()

        @pl.when(jnp.logical_and(second, i < half))
        def _():
            for n in range(4):
                push(i, slot, n).start()

        return carry

    lax.fori_loop(0, chunks, forward_chunk, 0)
    left_copy(chunks - 1).wait()
    for i in range(chunks):
        for copy in x_out_copies(i):
            copy.wait()

    @pl.when(first)
    def _():
        for i in range(half, chunks):
            for n in range(4):
                save(i, i % 2, n).wait()
        for which in (3, 2, 1, 0):
            w_push(which).wait_recv()
            w_copy(which, peer_w_hbm).start()
        for i in (1, 0):
            for n in range(4):
                push(i, i, n).wait_recv()
                load(i, i, n, peer_hbm).start()
        for i in range(chunks):
            hand_on(i).wait_send()

    @pl.when(second)
    def _():
        res_copy(chunks - 1).wait()
        for i in range(half):
            e_push(i).wait_send()
        gains_push().wait_send()
        for which in range(4):
            w_push(which).wait_send()

    def tally(name, start, values):
        total = jnp.sum(values.astype(jnp.float32), axis=0, keepdims=True)
        at = VECTORS[name][0] + start // UNIT
        for n in range(values.shape[1] // UNIT):
            vec[at + n : at + n + 1, :] += total[:, n * UNIT : (n + 1) * UNIT]

    def right_blocks(first_block, value):
        for n in range(value.shape[1] // UNIT):
            right[first_block + n] = value[:, n * UNIT : (n + 1) * UNIT]

    turns = jnp.where(first, chunks + half, half)

    def chunk_of(turn):
        late = jnp.where(first, turn >= chunks, True)
        return 1 - lax.rem(turn, 2) + jnp.where(late, half, 0)

    def loads(turn, some, action):
        for peers in (True, False):
            @pl.when((turn < half) if peers else (turn >= half))
            def _():
                i = chunk_of(turn)
                for n in some:
                    action(load(i, lax.rem(i, 2), n, peer_hbm if peers else own_hbm))

    def right_done(turn, n):
        i = chunk_of(turn)

        @pl.when(jnp.logical_and(first, turn < half))
        def _():
            right_push(i, n).wait_send()

        @pl.when(jnp.logical_not(jnp.logical_and(first, turn < half)))
        def _():
            right_copy(i, n).wait()

    def right_go(turn, n):
        i = chunk_of(turn)

        @pl.when(jnp.logical_and(first, turn < half))
        def _():
            right_push(i, n).start()

        @pl.when(jnp.logical_not(jnp.logical_and(first, turn < half)))
        def _():
            right_copy(i, n).start()

    def tail_part(turn, i):
        slot = lax.rem(i, 2)

        @pl.when(first)
        def _():
            loads(turn, (0, 1), lambda copy: copy.wait())

            @pl.when(turn < half)
            def _():
                e_push(i).wait_recv()

            @pl.when(turn == 0)
            def _():
                gains_push().wait_recv()
                gains[...] = gains_peer[...]

            @pl.when(turn == half)
            def _():
                own_gains()

            @pl.when(turn >= chunks)
            def _():
                hand_back(i).wait_recv()

        @pl.when(second)
        def _():
            e_copy(i).wait()

        @pl.when(turn >= 1)
        def _():
            for n in range(2):
                right_done(turn - 1, n)

        def ready(which):
            @pl.when(jnp.logical_and(first, jnp.logical_or(turn == 0, turn == half)))
            def _():
                w_copy(which).wait()

        now_a, total = keep_a.at[slot], dn1

        def kept(name, start=0):
            at = KEEP_A[name] + start
            return now_a[:, at : at + width].astype(jnp.float32)

        e = e_in[i].astype(jnp.float32)
        unit_two = kept("u2")
        tally("g2", 0, e * unit_two)
        tally("h2", 0, e)
        second_full = norm_back(
            e * gains[1:2, :], unit_two, stat_a[slot, :, STAT_A["s2"] : STAT_A["s2"] + 1]
        )
        second_low = second_full.astype(jnp.bfloat16)
        right_blocks(0, second_low)
        tally("bd", 0, second_low)
        total[...] = second_full

        ready(3)

        def pulled(n):
            return back_product(second_low, wd[n * width : (n + 1) * width, :])

        grad = pulled(0)
        for n in range(4):
            later = pulled(n + 1) if n < 3 else None
            hidden_low = (grad * kept("slope", n * width)).astype(jnp.bfloat16)
            right_blocks(3 + 3 * n, hidden_low)
            tally("bu", n * width, hidden_low)
            if n == 0:
                ready(2)
            total[...] += back_product(hidden_low, wu[:, n * width : (n + 1) * width])
            grad = later
        right_go(turn, 0)
        grad_normed = total[...]
        unit_one = kept("u1")
        tally("g1", 0, grad_normed * unit_one)
        tally("h1", 0, grad_normed)
        grad_first = norm_back(
            grad_normed * gains[0:1, :], unit_one, stat_a[slot, :, STAT_A["s1"] : STAT_A["s1"] + 1]
        )
        total[...] = grad_first
        first_low = grad_first.astype(jnp.bfloat16)
        right_blocks(15, first_low)
        right_go(turn, 1)
        tally("bo", 0, first_low)
        ready(1)
        grad_mixed = back_product(first_low, wo[...]).astype(jnp.bfloat16).astype(jnp.float32)
        weighed[...] = (grad_mixed * stat_a[slot, :, 0:width]).astype(jnp.bfloat16)

        @pl.when(first)
        def _():
            @pl.when(turn + 2 < turns)
            def _():
                loads(turn + 2, (0, 1), lambda copy: copy.start())

            @pl.when(turn == half - 1)
            def _():
                for which in (3, 2, 1):
                    w_copy(which).start()

    def pair_part(i, pair):
        slot = lax.rem(i, 2)
        now_b, old_b = keep_b.at[slot], keep_b.at[1 - slot]
        span = pl.ds(pl.multiple_of(pair * 128, 128), 128)

        def cut(ref, name):
            return ref[:, pl.ds(pl.multiple_of(KEEP_B[name] + pair * 128, 128), 128)]

        def half_block(source, table):
            queries, keys_in, values = cut(now_b, "q"), cut(source, "k"), cut(source, "v")
            w = weighed[:, span]
            cross = w.astype(jnp.float32) * stat_b[slot, :, span]
            zero, one = jnp.zeros_like(keys_in), jnp.ones_like(values)
            total_q, total_k, total_v = 0.0, 0.0, 0.0
            for half in range(2):
                own = low if half == 0 else jnp.logical_not(low)
                spare = 64 * (1 - half)
                inner = jnp.sum(jnp.where(own, cross, 0.0), axis=-1, keepdims=True)
                rough = inner.astype(jnp.bfloat16).astype(jnp.float32)
                extra = jnp.where(
                    lanes == spare, -rough, jnp.where(lanes == spare + 1, rough - inner, 0.0)
                ).astype(jnp.bfloat16)
                own_keys = jnp.where(own, keys_in, zero)
                scores = (back_product(queries, own_keys) * table).astype(jnp.bfloat16)
                grads = (
                    back_product(
                        jnp.where(own, w, extra), jnp.where(own, values, one)
                    )
                    * table
                ).astype(jnp.bfloat16)
                total_q += dot(grads, own_keys)
                total_k += rows_product(grads, jnp.where(own, queries, zero))
                total_v += rows_product(scores, jnp.where(own, w, zero))
            return total_q, total_k, total_v

        total_q, total_k, total_v = half_block(now_b, mix[0])
        dq[:, span] = total_q
        dk[:, span] = total_k
        dv[:, span] = total_v

        @pl.when(slot == 0)
        def _():
            dk[:, span] += carry_k[:, span]
            dv[:, span] += carry_v[:, span]

        @pl.when(slot == 1)
        def _():
            far_q, far_k, far_v = half_block(old_b, mix[1])
            dq[:, span] += far_q
            carry_k[:, span] = far_k
            carry_v[:, span] = far_v

    def head_part(turn, i):
        slot = lax.rem(i, 2)

        @pl.when(turn >= 1)
        def _():
            right_done(turn - 1, 2)

        @pl.when(jnp.logical_and(first, jnp.logical_or(turn == 0, turn == half)))
        def _():
            w_copy(0).wait()

        now_b = keep_b.at[slot]
        grad_in = dn1[...]
        for n, (source, slope) in enumerate(((dq, "sq"), (dk, "sk"), (dv, None))):
            values = source[...]
            if slope:
                at = KEEP_B[slope]
                values = values * now_b[:, at : at + width].astype(jnp.float32)
            values = values.astype(jnp.bfloat16)
            right_blocks(18 + 3 * n, values)
            tally("bp", n * width, values)
            grad_in += back_product(values, wp[:, n * width : (n + 1) * width])
        right_go(turn, 2)

        @pl.when(first)
        def _():
            @pl.when(turn < half)
            def _():
                e_in[i] = grad_in.astype(jnp.bfloat16)

            @pl.when(turn >= half)
            def _():
                @pl.when(turn > half)
                def _():
                    res_copy(chunk_of(turn - 1)).wait()

                rows_out[...] = grad_in
                res_copy(i).start()

            @pl.when(turn + 2 < turns)
            def _():
                loads(turn + 2, (2, 3), lambda copy: copy.start())

            @pl.when(turn == half - 1)
            def _():
                w_copy(0).start()
                vec_sent[...] = vec[0:40, :]
                vec_push().start()
                vec[...] = jnp.zeros_like(vec)

        @pl.when(second)
        def _():
            handed[i] = grad_in.astype(jnp.bfloat16)
            hand_back(i).start()

    def one_turn(turn, carry):
        i = chunk_of(turn)
        tail_part(turn, i)

        @pl.when(jnp.logical_and(first, lax.rem(turn, 2) == 0))
        def _():
            loads(turn, (2, 3), lambda copy: copy.wait())
            loads(turn + 1, (2, 3), lambda copy: copy.wait())

        def one_pair(pair, inner):
            pair_part(i, pair)
            return inner

        lax.fori_loop(0, pairs, one_pair, 0)
        head_part(turn, i)
        return carry

    lax.fori_loop(0, turns, one_turn, 0)
    for n in range(3):
        right_copy(half, n).wait()

    @pl.when(first)
    def _():
        res_copy(half).wait()
        vec_push().wait_send()

    @pl.when(second)
    def _():
        for i in range(half, chunks):
            hand_back(i).wait_send()
        vec_push().wait_recv()
        vec[0:40, :] += vec_peer[...]
        for i in range(half):
            for n in range(3):
                right_push(i, n).wait_recv()

    vec_out[...] = vec[...]


def run_layers(ends, mats, rows_in, mix, dp_size):
    tokens, width = ends.shape
    chunks = tokens // CHUNK
    rows = sum_sizes(dp_size)[1]
    bf16, f32 = jnp.bfloat16, jnp.float32

    def kept(count):
        return [
            jax.ShapeDtypeStruct((count * CHUNK, columns), dtype)
            for columns, dtype in (
                (KEEP_A_WIDTH, bf16), (STAT_A_WIDTH, f32), (KEEP_B_WIDTH, bf16), (width, f32)
            )
        ]

    out_shape = (
        [
            jax.ShapeDtypeStruct((21, chunks, CHUNK, UNIT), bf16),
            jax.ShapeDtypeStruct((27, chunks, CHUNK, UNIT), bf16),
        ]
        + kept(chunks)
        + kept(chunks // 2)
        + [jax.ShapeDtypeStruct(mat.shape, mat.dtype) for mat in mats]
        + [
            jax.ShapeDtypeStruct((tokens, width), f32),
            jax.ShapeDtypeStruct((rows, UNIT), f32),
        ]
    )
    chunk_f32 = pltpu.VMEM((CHUNK, width), f32)
    all_rows = pltpu.VMEM((chunks, CHUNK, width), bf16)
    dma = pltpu.SemaphoreType.DMA
    outs = pl.pallas_call(
        partial(layers_kernel, chunks),
        out_shape=out_shape,
        in_specs=any_specs(5) + vmem_specs(9),
        out_specs=any_specs(15) + vmem_specs(1),
        scratch_shapes=[pltpu.VMEM(mat.shape, mat.dtype) for mat in mats]
        + [
            all_rows,
            all_rows,
            all_rows,
            pltpu.VMEM((18, CHUNK, UNIT), bf16),
            pltpu.VMEM((27, CHUNK, UNIT), bf16),
            pltpu.VMEM((2, CHUNK, KEEP_A_WIDTH), bf16),
            pltpu.VMEM((2, CHUNK, STAT_A_WIDTH), f32),
            pltpu.VMEM((2, CHUNK, KEEP_B_WIDTH), bf16),
            pltpu.VMEM((2, CHUNK, width), f32),
            chunk_f32,
            pltpu.VMEM((HEADS, CHUNK, 128), f32),
            chunk_f32,
            chunk_f32,
            chunk_f32,
            chunk_f32,
            chunk_f32,
            chunk_f32,
            pltpu.VMEM((CHUNK, width), bf16),
            pltpu.VMEM((rows, UNIT), f32),
            pltpu.VMEM((40, UNIT), f32),
            pltpu.VMEM((40, UNIT), f32),
            pltpu.VMEM((8, width), f32),
            pltpu.VMEM((8, width), f32),
            dma((4,)),
            dma((chunks,)),
            dma((chunks, 3)),
            dma((chunks,)),
            dma,
            dma((3,)),
            dma((2, 4)),
            dma,
            dma((chunks,)),
            dma((chunks,)),
            dma((chunks,)),
            dma((chunks,)),
            dma((4,)),
            dma((4,)),
            dma((chunks // 2,)),
            dma((chunks // 2,)),
            dma((chunks // 2, 4)),
            dma((chunks // 2, 4)),
            dma((3,)),
            dma((chunks // 2, 3)),
            dma,
            dma,
            dma,
            dma,
        ],
        compiler_params=pltpu.CompilerParams(
            collective_id=2, has_side_effects=True, vmem_limit_bytes=62 << 20
        ),
        name="layers",
    )(ends, *mats, *rows_in, mix)
    return outs[14], outs[0], outs[1], outs[15]


def widen_kernel(proj, out, up, down, small, *refs):
    sources = (proj, out, up, down)
    targets, vectors = refs[:4], refs[4:12]
    held, wide_held = refs[12:16], refs[16:20]
    in_sem, out_sem = refs[20:]
    blocks = []
    for which, source in enumerate(sources):
        step = 256 if source.shape[1] > 768 else 768
        for start in range(0, source.shape[0], step):
            blocks.append((which, pl.ds(start, step)))
    copies_in = [
        pltpu.make_async_copy(sources[which].at[span], held[which].at[span], in_sem.at[n])
        for n, (which, span) in enumerate(blocks)
    ]
    copies_out = [
        pltpu.make_async_copy(wide_held[which].at[span], targets[which].at[0, span], out_sem.at[n])
        for n, (which, span) in enumerate(blocks)
    ]
    for copy in copies_in:
        copy.start()
    for (start, count), vector in zip(VECTORS.values(), vectors):
        for n in range(count):
            vector[:, n * UNIT : (n + 1) * UNIT] = small[start + n : start + n + 1, :].astype(
                jnp.float32
            )
    for n, (which, span) in enumerate(blocks):
        copies_in[n].wait()
        wide_held[which][span, :] = held[which][span, :].astype(jnp.float32)
        copies_out[n].start()
    for copy in copies_out:
        copy.wait()


def widen(proj, out, up, down, small):
    mats = (proj, out, up, down)
    return pl.pallas_call(
        widen_kernel,
        out_shape=[jax.ShapeDtypeStruct((1,) + mat.shape, jnp.float32) for mat in mats]
        + [jax.ShapeDtypeStruct((1, count * UNIT), jnp.float32) for _, count in VECTORS.values()],
        in_specs=any_specs(4) + vmem_specs(1),
        out_specs=any_specs(4) + vmem_specs(8),
        scratch_shapes=[pltpu.VMEM(mat.shape, jnp.bfloat16) for mat in mats]
        + [pltpu.VMEM(mat.shape, jnp.float32) for mat in mats]
        + [pltpu.SemaphoreType.DMA((11,)), pltpu.SemaphoreType.DMA((11,))],
        compiler_params=pltpu.CompilerParams(vmem_limit_bytes=60 << 20),
        name="widen",
    )(proj, out, up, down, small)


def mix_tables(length):
    places = jnp.arange(2 * CHUNK, dtype=jnp.int32)
    angles = places.astype(jnp.float32) * ((0.5 * math.pi) / length.astype(jnp.float32))
    cosine, sine, document = lax.optimization_barrier(
        (jnp.cos(angles), jnp.sin(angles), places // length)
    )

    def table(start):
        later, earlier = slice(start, start + CHUNK), slice(0, CHUNK)
        seen = jnp.logical_and(
            document[later, None] == document[None, earlier],
            places[later, None] >= places[None, earlier],
        )
        near = cosine[later, None] * cosine[None, earlier] + sine[later, None] * sine[None, earlier]
        return jnp.where(seen, near, 0.0)

    return jnp.stack([table(0), table(CHUNK)])


def shards(
    endpoints,
    projection,
    projection_bias,
    output_weight,
    output_bias,
    first_gain,
    first_shift,
    up_weight,
    up_bias,
    down_weight,
    down_bias,
    second_gain,
    second_shift,
    segment_length,
):
    dp_size = lax.axis_size("dp")
    mats = (projection[0], output_weight[0], up_weight[0], down_weight[0])
    rows = (
        projection_bias, output_bias, first_gain, first_shift, up_bias, down_bias, second_gain,
        second_shift,
    )
    mix = mix_tables(segment_length[0])
    results, left, right, vec = run_layers(endpoints[0], mats, rows, mix, dp_size)
    sums = reduce_gradients(left, right, vec, dp_size)
    proj, out, up, down, bp, bo, g1, h1, bu, bd, g2, h2 = widen(*sums)
    return (results[None], proj, bp, out, bo, g1, h1, up, bu, down, bd, g2, h2)


def solution(mesh):
    in_specs = (
        P("section", "dp", None),
        P("section", None, None),
        P("section", None),
        P("section", None, None),
        P("section", None),
        P("section", None),
        P("section", None),
        P("section", None, None),
        P("section", None),
        P("section", None, None),
        P("section", None),
        P("section", None),
        P("section", None),
        P("dp"),
    )
    out_specs = (
        P("section", "dp", None),
        P("section", None, None),
        P("section", None),
        P("section", None, None),
        P("section", None),
        P("section", None),
        P("section", None),
        P("section", None, None),
        P("section", None),
        P("section", None, None),
        P("section", None),
        P("section", None),
        P("section", None),
    )
    return jax.shard_map(shards, mesh=mesh, in_specs=in_specs, out_specs=out_specs, check_vma=False)
```

```python
from functools import partial
import math

import jax
import jax.numpy as jnp
from jax import lax
from jax.experimental import pallas as pl
from jax.experimental.pallas import tpu as pltpu
from jax.sharding import PartitionSpec as P

HEADS = 12
EPSILON = 1e-05
MESH = pl.DeviceIdType.MESH


def rows_product(left_mat, right_mat):
    return lax.dot_general(
        left_mat, right_mat, (((0,), (0,)), ((), ())), preferred_element_type=jnp.float32
    )


def back_product(grad_mat, weight_mat):
    return lax.dot_general(
        grad_mat, weight_mat, (((1,), (1,)), ((), ())), preferred_element_type=jnp.float32
    )


def factor_dims(count):
    bits = count.bit_length() - 1
    return (1 << (bits // 3), 1 << ((bits + 1) // 3), 1 << ((bits + 2) // 3))


ORDERS = {"a": (0, 1, 2), "b": (1, 2, 0), "c": (2, 0, 1)}
PATTERN = "abacabc"
LAG = 3
END_LAG = 4
OUT_LAG = 4
UNIT = 256
UNITS = 108
PIECE_ROWS = 512
SEM_SLOTS = 35


def stage_list(order, dims, rows):
    stages, size, landing = [], rows, 0
    for level, ax in enumerate(order):
        part = size // dims[ax]
        for step in range(1, dims[ax]):
            stages.append(("reduce", level, ax, step, part, landing))
            landing += part if dims[ax] == 2 else 2 * part
        size = part
    for level in reversed(range(3)):
        ax = order[level]
        for step in range(1, dims[ax]):
            stages.append(("gather", level, ax, step, size, 0))
        size *= dims[ax]
    return stages, landing


def unit_blocks(unit):
    up, out, proj = unit - 36, unit - 72, unit - 81
    left = jnp.where(
        unit < 36,
        unit // 3,
        jnp.where(unit < 72, 12 + up // 12, jnp.where(unit < 81, 15 + out // 3, 18 + proj // 9)),
    )
    right = jnp.where(
        unit < 36,
        unit % 3,
        jnp.where(unit < 72, 3 + up % 12, jnp.where(unit < 81, 15 + out % 3, 18 + proj % 9)),
    )
    return left, right


def axis_places(dims):
    here = lax.axis_index("dp")
    strides = (1, dims[0], dims[0] * dims[1])
    return here, strides, [(here // strides[ax]) % dims[ax] for ax in range(3)]


def greet_axes(dims, semaphore):
    here, strides, place = axis_places(dims)
    around = 0
    for ax in range(3):
        for sign, can in ((1, place[ax] < dims[ax] - 1), (-1, place[ax] > 0)):
            @pl.when(can)
            def _():
                pl.semaphore_signal(
                    semaphore, inc=1, device_id={"dp": here + sign * strides[ax]},
                    device_id_type=MESH,
                )
            around = around + can.astype(jnp.int32)
    return around


def gather_sends(spot, count):
    found = {}
    for at in range(count):
        sent = (at + 1 if at < count - 1 else 0) + (count - at if at > 0 else 0)
        found.setdefault(sent, []).append(spot == at)
    options = []
    for sent, spots in found.items():
        can = spots[0]
        for other in spots[1:]:
            can = jnp.logical_or(can, other)
        options.append((can, sent))
    return options


def guarded(can, action):
    if can is None:
        action()
    else:
        pl.when(can)(action)


def summing(dims, pieces, rows, acc, acc_slots, full, full_slots, landing, land_slots, left_hbm,
            right_hbm, vec, outs, left_ring, right_ring, load_sem, out_sem, send_sem, recv_sem):
    here, strides, place = axis_places(dims)
    proj_hbm, out_hbm, up_hbm, down_hbm, small_hbm = outs
    ring, chunks = left_ring.shape[0], left_ring.shape[1]
    per_piece = rows // UNIT
    land_rows = landing.shape[0] // land_slots
    plans = {name: stage_list(order, dims, rows)[0] for name, order in ORDERS.items()}
    n_stages = len(plans["a"])
    shard = rows // (dims[0] * dims[1] * dims[2])
    period = len(PATTERN)

    bases = {}
    for name, order in ORDERS.items():
        base, size, found = 0, rows, []
        for ax in order:
            found.append(base)
            size = size // dims[ax]
            base = base + place[ax] * size
        bases[name] = found + [base]

    sent_rows = {}
    for name, plan in plans.items():
        sure, options = 0, [(None, 0)]
        for kind, _, ax, step, part, _ in plan:
            if dims[ax] == 2 or kind == "reduce":
                sure += part
            elif step == 1:
                options = [
                    (can if other is None else jnp.logical_and(can, other), more + part * count)
                    for other, more in options
                    for can, count in gather_sends(place[ax], dims[ax])
                ]
        sent_rows[name] = [(can, sure + more) for can, more in options]

    def view(ref, slot, start, size):
        across = ref.shape[1] // UNIT
        first = pl.multiple_of(slot // across * rows + start, 16)
        if across == 1:
            return ref.at[pl.ds(first, size)]
        return ref.at[pl.ds(first, size), pl.ds(pl.multiple_of(slot % across * UNIT, UNIT), UNIT)]

    def loads(unit):
        slot = unit % ring
        left, right = unit_blocks(unit)
        return (
            pltpu.make_async_copy(left_hbm.at[left], left_ring.at[slot], load_sem.at[slot, 0]),
            pltpu.make_async_copy(right_hbm.at[right], right_ring.at[slot], load_sem.at[slot, 1]),
        )

    def prime():
        for unit in range(ring):
            for copy in loads(jnp.int32(unit)):
                copy.start()

    def form(piece, sub):
        unit = piece * per_piece + sub
        target = view(acc, piece % acc_slots, sub * UNIT, UNIT)

        @pl.when(unit < UNITS)
        def _():
            for copy in loads(unit):
                copy.wait()
            slot = unit % ring
            tokens = chunks * left_ring.shape[2]
            target[...] = rows_product(
                left_ring[slot].reshape(tokens, UNIT), right_ring[slot].reshape(tokens, UNIT)
            ).astype(jnp.bfloat16)

            @pl.when(unit + ring < UNITS)
            def _():
                for copy in loads(unit + ring):
                    copy.start()

        @pl.when(unit >= UNITS)
        def _():
            target[...] = vec[sub * UNIT : (sub + 1) * UNIT, :].astype(jnp.bfloat16)

    def copies(name, stage, piece):
        kind, level, ax, step, part, land = plans[name][stage]
        count, spot = dims[ax], place[ax]
        slot = piece % SEM_SLOTS
        held, index = (acc, piece % acc_slots) if kind == "reduce" else (full, piece % full_slots)
        land_start = piece % land_slots * land_rows + land

        def chunk(q):
            return view(held, index, bases[name][level] + q * part, part)

        def landed(way):
            return landing.at[pl.ds(pl.multiple_of(land_start + way * part, 16), part)]

        def remote(src, dst, way, sign):
            return lambda: pltpu.make_async_remote_copy(
                src_ref=src, dst_ref=dst, send_sem=send_sem.at[slot],
                recv_sem=recv_sem.at[slot, stage, way],
                device_id={"dp": here + sign * strides[ax]}, device_id_type=MESH,
            )

        sends, receives = [], []
        if count == 2:
            sign = 1 - 2 * spot
            mine, other = spot, 1 - spot
            if kind == "reduce":
                sends.append((None, remote(chunk(other), landed(0), 0, sign)))
                receives.append((None, remote(chunk(mine), landed(0), 0, sign), mine, landed(0)))
            else:
                sends.append((None, remote(chunk(mine), chunk(mine), 0, sign)))
                receives.append((None, remote(chunk(other), chunk(other), 0, sign), other, None))
            return sends, receives, chunk
        back = count - 1 - spot
        if kind == "reduce":
            for way, sign, can, q in (
                (0, 1, spot < step, spot + count - step),
                (1, -1, back < step, step - 1 - back),
            ):
                q = jnp.clip(q, 0, count - 1)
                sends.append((can, remote(chunk(q), landed(way), way, sign)))
            for way, sign, can, q in (
                (0, 1, jnp.logical_and(spot >= 1, spot - 1 < step), spot - 1 + count - step),
                (1, -1, jnp.logical_and(back >= 1, back - 1 < step), step - back),
            ):
                q = jnp.clip(q, 0, count - 1)
                receives.append((can, remote(chunk(q), landed(way), way, sign), q, landed(way)))
        else:
            for way, sign, can, q in (
                (0, 1, jnp.logical_and(back >= 1, spot >= step - 1), spot - step + 1),
                (1, -1, jnp.logical_and(spot >= 1, back >= step - 1), spot + step - 1),
            ):
                q = jnp.clip(q, 0, count - 1)
                sends.append((can, remote(chunk(q), chunk(q), way, sign)))
            for way, sign, can, q in (
                (0, 1, spot >= step, spot - step),
                (1, -1, back >= step, spot + step),
            ):
                q = jnp.clip(q, 0, count - 1)
                receives.append((can, remote(chunk(q), chunk(q), way, sign), q, None))
        return sends, receives, chunk

    def out_copies(piece, action):
        for sub in range(per_piece):
            unit = piece * per_piece + sub
            source = view(full, piece % full_slots, sub * UNIT, UNIT)
            for begin, end, across, target in (
                (0, 36, 3, down_hbm), (36, 72, 12, up_hbm), (72, 81, 3, out_hbm),
                (81, 108, 9, proj_hbm), (108, 108 + per_piece, 1, small_hbm),
            ):
                @pl.when(jnp.logical_and(unit >= begin, unit < end))
                def _():
                    local = jnp.clip(unit - begin, 0, end - begin - 1)
                    place_in = target.at[
                        pl.ds(pl.multiple_of(local // across * UNIT, UNIT), UNIT),
                        pl.ds(pl.multiple_of(local % across * UNIT, UNIT), UNIT),
                    ]
                    action(pltpu.make_async_copy(source, place_in, out_sem.at[unit]))

    def work(name, stage, piece):
        if stage > 0:
            sends, receives, chunk = copies(name, stage - 1, piece)
            for can, copy, q, landed in receives:
                def finish():
                    copy().wait_recv()
                    if landed is not None:
                        block = chunk(q)
                        block[...] = block[...] + landed[...]
                guarded(can, finish)
        if stage == n_stages // 2:
            mine = bases[name][3]
            own = view(full, piece % full_slots, mine, shard)
            own[...] = view(acc, piece % acc_slots, mine, shard)[...]
        if stage < n_stages:
            for can, copy in copies(name, stage, piece)[0]:
                guarded(can, lambda: copy().start())
        else:
            out_copies(piece, lambda copy: copy.start())
        if stage == n_stages:
            for can, amount in sent_rows[name]:
                sent = landing.at[pl.ds(0, amount)]
                guarded(
                    can,
                    lambda: pltpu.make_async_copy(
                        sent, sent, send_sem.at[piece % SEM_SLOTS]
                    ).wait(),
                )

    starts = [0]
    for stage in range(n_stages):
        starts.append(starts[-1] + (END_LAG if stage in (0, n_stages - 1) else LAG))
    total_ticks = pieces + starts[-1] + OUT_LAG

    def run():
        prime()

        def some_ticks(turn, carry):
            for spot_in in range(period):
                now = turn * period + spot_in
                oldest = now - starts[-1] - OUT_LAG

                @pl.when(jnp.logical_and(oldest >= 0, oldest < pieces))
                def _():
                    out_copies(jnp.clip(oldest, 0, pieces - 1), lambda copy: copy.wait())

                for stage in reversed(range(n_stages + 1)):
                    piece = now - starts[stage]
                    name = PATTERN[(spot_in - starts[stage]) % period]

                    @pl.when(jnp.logical_and(piece >= 0, piece < pieces))
                    def _():
                        at = jnp.clip(piece, 0, pieces - 1)
                        if stage == 0:
                            for sub in range(per_piece):
                                form(at, sub)
                        work(name, stage, at)

            return carry

        lax.fori_loop(0, -(-total_ticks // period), some_ticks, 0)

    return run


def sum_sizes(dp_size):
    dims = factor_dims(dp_size)
    rows = max(PIECE_ROWS, 16 * dp_size)
    land = max(stage_list(order, dims, rows)[1] for order in ORDERS.values())
    return dims, rows, -(-(UNITS + 1) * UNIT // rows), land, 2 * (sum(dims) - 3)


def sum_out_shapes(rows):
    return [
        jax.ShapeDtypeStruct(shape, jnp.bfloat16)
        for shape in ((768, 2304), (768, 768), (768, 3072), (3072, 768), (rows, UNIT))
    ]


def sum_semaphores(ring, rows, pieces, stages):
    return [
        pltpu.SemaphoreType.DMA((ring, 2)),
        pltpu.SemaphoreType.DMA((pieces * rows // UNIT,)),
        pltpu.SemaphoreType.DMA((SEM_SLOTS,)),
        pltpu.SemaphoreType.DMA((SEM_SLOTS, stages, 2)),
    ]


def reduce_kernel(dims, pieces, rows, left_hbm, right_hbm, vec, proj_hbm, out_hbm, up_hbm, down_hbm,
                  small_hbm, acc, full, landing, left_ring, right_ring, load_sem, out_sem, send_sem,
                  recv_sem):
    barrier = pltpu.get_barrier_semaphore()
    around = greet_axes(dims, barrier)
    pl.semaphore_wait(barrier, around)
    slots = acc.shape[0] // rows
    summing(
        dims, pieces, rows, acc, slots, full, pieces, landing, slots, left_hbm, right_hbm, vec,
        (proj_hbm, out_hbm, up_hbm, down_hbm, small_hbm), left_ring, right_ring, load_sem, out_sem,
        send_sem, recv_sem,
    )()


def reduce_gradients(left, right, vec, dp_size):
    dims, rows, pieces, land, stages = sum_sizes(dp_size)
    ring = 4 if dp_size <= 16 else 2
    slots = min(SEM_SLOTS, pieces)
    return pl.pallas_call(
        partial(reduce_kernel, dims, pieces, rows),
        out_shape=sum_out_shapes(rows),
        in_specs=any_specs(2) + vmem_specs(1),
        out_specs=any_specs(5),
        scratch_shapes=[
            pltpu.VMEM((slots * rows, UNIT), jnp.bfloat16),
            pltpu.VMEM((pieces * rows, UNIT), jnp.bfloat16),
            pltpu.VMEM((slots * land, UNIT), jnp.bfloat16),
            pltpu.VMEM((ring,) + left.shape[1:], jnp.bfloat16),
            pltpu.VMEM((ring,) + left.shape[1:], jnp.bfloat16),
        ]
        + sum_semaphores(ring, rows, pieces, stages),
        compiler_params=pltpu.CompilerParams(
            collective_id=1, has_side_effects=True, vmem_limit_bytes=62 << 20
        ),
        name="reduce",
    )(left, right, vec)


CHUNK = 256
KEEP_A = {"slope": 0, "u1": 3072, "u2": 3840}
KEEP_A_WIDTH = 4608
STAT_A = {"rden": 0, "s1": 768, "s2": 896}
STAT_A_WIDTH = 1024
KEEP_B = {"q": 0, "k": 768, "sq": 1536, "sk": 2304, "v": 3072}
KEEP_B_WIDTH = 3840
VECTORS = {
    "bp": (0, 9), "bo": (9, 3), "g1": (12, 3), "h1": (15, 3), "bu": (18, 12), "bd": (30, 3), "g2": (33, 3),
    "h2": (36, 3),
}
TAIL_SCALE = 0.375
TAIL_POLY = (
    0.21141059805705423,
    0.21471795439954675,
    0.17184958530833144,
    0.26915459919947066,
    -0.10973686091480542,
    0.37354383408912983,
    -0.13093832475477368,
)


def dot(left_mat, right_mat):
    return jnp.dot(left_mat, right_mat, preferred_element_type=jnp.float32)


def inverse(value):
    rough = pl.reciprocal(value, approx=True)
    return rough * (2.0 - value * rough)


def gelu_pair(hidden):
    bell = jnp.exp(hidden * hidden * -0.5)
    t = inverse(1.0 + (TAIL_SCALE * math.sqrt(0.5)) * jnp.abs(hidden))
    poly = jnp.full_like(t, 0.5 * TAIL_POLY[-1])
    for coefficient in TAIL_POLY[-2::-1]:
        poly = poly * t + 0.5 * coefficient
    tail = poly * t * bell
    below = jnp.where(hidden >= 0, 1.0 - tail, tail)
    return hidden * below, below + hidden * (bell * (1.0 / math.sqrt(2.0 * math.pi)))


def softplus_pair(value):
    small = jnp.exp(-jnp.abs(value))
    whole = 1.0 + small
    log_whole = jnp.where(
        small < 1e-2, small * (1.0 - small * (0.5 - small * (1.0 / 3.0))), jnp.log(whole)
    )
    return (
        jnp.maximum(value, 0.0) + log_whole,
        jnp.where(value >= 0, 1.0, small) * inverse(whole),
    )


def centred(rows):
    centre = rows - jnp.mean(rows, axis=-1, keepdims=True)
    scaling = lax.rsqrt(jnp.mean(centre * centre, axis=-1, keepdims=True) + EPSILON)
    return centre * scaling, scaling


def wide(column, width=128):
    return jnp.broadcast_to(column, (column.shape[0], width))


def first_half(rows):
    return lax.broadcasted_iota(jnp.int32, (rows, 128), 1) < 64


def row(ref):
    return ref[...].astype(jnp.float32)


def any_specs(count):
    return [pl.BlockSpec(memory_space=pl.ANY)] * count


def vmem_specs(count):
    return [pl.BlockSpec(memory_space=pltpu.VMEM)] * count


def norm_back(grad, unit_rows, scaling):
    mean_grad = jnp.mean(grad, axis=-1, keepdims=True)
    mean_cross = jnp.mean(grad * unit_rows, axis=-1, keepdims=True)
    return scaling * (grad - mean_grad - unit_rows * mean_cross)


def layers_kernel(chunks, *refs):
    (ends_hbm, wp_hbm, wo_hbm, wu_hbm, wd_hbm, bp, bo, g1, h1, bu, bd, g2, h2, mix) = refs[:14]
    left_hbm, right_hbm = refs[14:16]
    own_hbm, peer_hbm, peer_w_hbm = refs[16:20], refs[20:24], refs[24:28]
    res_hbm, vec_out = refs[28:30]
    (wp, wo, wu, wd, x_in, e_in, handed, left, right, keep_a, stat_a, keep_b, stat_b, rows_out, nums, dq,
     dk, dv, carry_k, carry_v, dn1, weighed, vec, vec_sent, vec_peer, gains, gains_peer, w_sem, x_sem, xo_sem, e_sem, left_sem,
     right_sem, load_sem, res_sem, send_f, recv_f, send_b, recv_b, send_w, recv_w, send_e, recv_e,
     send_k, recv_k, send_r, recv_r, send_v, recv_v, send_g, recv_g) = refs[30:]

    section = lax.axis_index("section")
    first = section == 0
    second = jnp.logical_not(first)
    partner = {"section": 1 - section}
    width = ends_hbm.shape[1]
    pairs = width // 128
    half = chunks // 2
    mats_hbm, mats = (wp_hbm, wo_hbm, wu_hbm, wd_hbm), (wp, wo, wu, wd)
    kept_bufs = (keep_a, stat_a, keep_b, stat_b)

    def w_copy(which, sources=mats_hbm):
        return pltpu.make_async_copy(sources[which], mats[which], w_sem.at[which])

    def remote(src, dst, send, recv):
        return pltpu.make_async_remote_copy(
            src_ref=src, dst_ref=dst, send_sem=send, recv_sem=recv, device_id=partner,
            device_id_type=MESH,
        )

    def w_push(which):
        return remote(mats_hbm[which], peer_w_hbm[which], send_w.at[which], recv_w.at[which])

    def rows_of(i):
        return pl.ds(pl.multiple_of(i * CHUNK, CHUNK), CHUNK)

    def x_copy(i):
        return pltpu.make_async_copy(ends_hbm.at[rows_of(i)], x_in.at[i], x_sem.at[i])

    def x_out_copies(i):
        return [
            pltpu.make_async_copy(
                x_in.at[i, :, n * UNIT : (n + 1) * UNIT], left_hbm.at[18 + n, i], xo_sem.at[i, n]
            )
            for n in range(3)
        ]

    def e_copy(i):
        return pltpu.make_async_copy(ends_hbm.at[rows_of(i)], e_in.at[i], e_sem.at[i])

    def e_push(i):
        return remote(ends_hbm.at[rows_of(i)], e_in.at[i], send_e.at[i], recv_e.at[i])

    def hand_on(i):
        return remote(handed.at[i], x_in.at[i], send_f.at[i], recv_f.at[i])

    def hand_back(i):
        return remote(handed.at[i], e_in.at[i], send_b.at[i], recv_b.at[i])

    def left_copy(i):
        return pltpu.make_async_copy(left, left_hbm.at[0:18, i], left_sem)

    spans = ((0, 15), (15, 18), (18, 27))

    def right_copy(i, n):
        start, end = spans[n]
        return pltpu.make_async_copy(
            right.at[start:end], right_hbm.at[start:end, i], right_sem.at[n]
        )

    def right_push(i, n):
        start, end = spans[n]
        return remote(
            right.at[start:end], right_hbm.at[start:end, i], send_r.at[n], recv_r.at[i, n]
        )

    def save(i, slot, n):
        return pltpu.make_async_copy(
            kept_bufs[n].at[slot], own_hbm[n].at[rows_of(i)], load_sem.at[slot, n]
        )

    def push(i, slot, n):
        return remote(
            kept_bufs[n].at[slot], peer_hbm[n].at[rows_of(i)], send_k.at[i, n], recv_k.at[i, n]
        )

    def load(i, slot, n, source):
        return pltpu.make_async_copy(
            source[n].at[rows_of(i)], kept_bufs[n].at[slot], load_sem.at[slot, n]
        )

    def res_copy(i):
        return pltpu.make_async_copy(rows_out, res_hbm.at[rows_of(i)], res_sem)

    def own_gains():
        gains[0:1, :] = row(g1)
        gains[1:2, :] = row(g2)

    def gains_push():
        return remote(gains, gains_peer, send_g, recv_g)

    def vec_push():
        return remote(vec_sent, vec_peer, send_v, recv_v)

    @pl.when(first)
    def _():
        x_copy(0).start()

    for which in range(4):
        w_copy(which).start()

    @pl.when(first)
    def _():
        for i in range(1, chunks):
            x_copy(i).start()

    @pl.when(second)
    def _():
        for i in range(half, chunks):
            e_copy(i).start()

    barrier = pltpu.get_barrier_semaphore()
    pl.semaphore_signal(barrier, inc=1, device_id=partner, device_id_type=MESH)
    vec[...] = jnp.zeros_like(vec)
    gains[...] = jnp.zeros_like(gains)
    own_gains()
    pl.semaphore_wait(barrier, 1)

    @pl.when(second)
    def _():
        gains_push().start()
        for i in range(half):
            e_push(i).start()
        for which in (3, 2, 1, 0):
            w_push(which).start()

    def weights_ready(i, which):
        @pl.when(i == 0)
        def _():
            w_copy(which).wait()

    lanes = lax.broadcasted_iota(jnp.int32, (CHUNK, 128), 1)
    low = lanes < 64

    def forward_chunk(i, carry):
        slot = lax.rem(i, 2)

        @pl.when(i >= 2)
        def _():
            @pl.when(first)
            def _():
                for n in range(4):
                    save(i - 2, slot, n).wait()

            @pl.when(second)
            def _():
                for n in range(4):
                    push(i - 2, slot, n).wait_send()

        weights_ready(i, 0)

        @pl.when(first)
        def _():
            x_copy(i).wait()

        @pl.when(second)
        def _():
            hand_on(i).wait_recv()

        for copy in x_out_copies(i):
            copy.start()
        now_a, now_b, old_b = keep_a.at[slot], keep_b.at[slot], keep_b.at[1 - slot]

        def keep(ref, start, value):
            ref[:, start : start + value.shape[1]] = value.astype(jnp.bfloat16)

        def blocks(first_block, value):
            for n in range(value.shape[1] // UNIT):
                left[first_block + n] = value[:, n * UNIT : (n + 1) * UNIT]

        x = x_in[i]
        for part, (name, slope) in enumerate((("q", "sq"), ("k", "sk"))):
            cols = slice(part * width, (part + 1) * width)
            soft, sigma = softplus_pair(dot(x, wp[:, cols]) + row(bp)[:, cols])
            keep(now_b, KEEP_B[name], soft)
            keep(now_b, KEEP_B[slope], sigma)
        cols = slice(2 * width, 3 * width)
        keep(now_b, KEEP_B["v"], dot(x, wp[:, cols]) + row(bp)[:, cols])

        def mix_pair(pair, source, table, fresh):
            def cut(ref, name):
                return ref[:, KEEP_B[name] + pair * 128 : KEEP_B[name] + (pair + 1) * 128]

            queries, keys_in, values = cut(now_b, "q"), cut(source, "k"), cut(source, "v")
            zero, one = jnp.zeros_like(keys_in), jnp.ones_like(values)
            for half in range(2):
                own = low if half == 0 else jnp.logical_not(low)
                scores = back_product(queries, jnp.where(own, keys_in, zero)) * table
                num = dot(scores.astype(jnp.bfloat16), jnp.where(own, values, one))
                at = 2 * pair + half
                nums[at] = num if fresh else nums[at] + num

        for pair in range(pairs):
            mix_pair(pair, now_b, mix[0], True)

        @pl.when(slot == 1)
        def _():
            for pair in range(pairs):
                mix_pair(pair, old_b, mix[1], False)

        @pl.when(i >= 1)
        def _():
            left_copy(i - 1).wait()

        for pair in range(pairs):
            num_a, num_b = nums[2 * pair], nums[2 * pair + 1]
            inv = inverse(
                jnp.where(low, pltpu.roll(num_a, 64, 1), pltpu.roll(num_b, 64, 1))
            )
            span = slice(pair * 128, (pair + 1) * 128)
            stat_b[slot, :, span] = jnp.where(low, num_a, num_b) * inv
            stat_a[slot, :, span] = inv
        blocks(15, stat_b[slot].astype(jnp.bfloat16))
        weights_ready(i, 1)
        first_sum = x.astype(jnp.float32) + row(bo)
        for n in range(3):
            first_sum += dot(left[15 + n], wo[n * UNIT : (n + 1) * UNIT, :])
        unit_one, scale_one = centred(first_sum)
        keep(now_a, KEEP_A["u1"], unit_one)
        stat_a[slot, :, STAT_A["s1"] : STAT_A["s1"] + 128] = wide(scale_one)
        normed = unit_one * row(g1) + row(h1)
        resid = dn1
        resid[...] = normed + row(bd)
        up_in = normed.astype(jnp.bfloat16)
        blocks(12, up_in)
        weights_ready(i, 2)

        def hidden_of(n):
            cols = slice(n * width, (n + 1) * width)
            return dot(up_in, wu[:, cols]) + row(bu)[:, cols]

        hidden = hidden_of(0)
        for n in range(4):
            later = hidden_of(n + 1) if n < 3 else None
            active, slope = gelu_pair(hidden)
            active = active.astype(jnp.bfloat16)
            blocks(3 * n, active)
            keep(now_a, n * width, slope)
            if n == 0:
                weights_ready(i, 3)
            resid[...] += dot(active, wd[n * width : (n + 1) * width, :])
            hidden = later
        unit_two, scale_two = centred(resid[...])
        keep(now_a, KEEP_A["u2"], unit_two)
        stat_a[slot, :, STAT_A["s2"] : STAT_A["s2"] + 128] = wide(scale_two)
        result = unit_two * row(g2) + row(h2)

        @pl.when(first)
        def _():
            handed[i] = result.astype(jnp.bfloat16)
            hand_on(i).start()

        @pl.when(second)
        def _():
            @pl.when(i >= 1)
            def _():
                res_copy(i - 1).wait()

            rows_out[...] = result
            res_copy(i).start()

        left_copy(i).start()

        @pl.when(first)
        def _():
            for n in range(4):
                save(i, slot, n).start()

        @pl.when(jnp.logical_and(second, i < half))
        def _():
            for n in range(4):
                push(i, slot, n).start()

        return carry

    lax.fori_loop(0, chunks, forward_chunk, 0)
    left_copy(chunks - 1).wait()
    for i in range(chunks):
        for copy in x_out_copies(i):
            copy.wait()

    @pl.when(first)
    def _():
        for i in range(half, chunks):
            for n in range(4):
                save(i, i % 2, n).wait()
        for which in (3, 2, 1, 0):
            w_push(which).wait_recv()
            w_copy(which, peer_w_hbm).start()
        for i in (1, 0):
            for n in range(4):
                push(i, i, n).wait_recv()
                load(i, i, n, peer_hbm).start()
        for i in range(chunks):
            hand_on(i).wait_send()

    @pl.when(second)
    def _():
        res_copy(chunks - 1).wait()
        for i in range(half):
            e_push(i).wait_send()
        gains_push().wait_send()
        for which in range(4):
            w_push(which).wait_send()

    def tally(name, start, values):
        total = jnp.sum(values.astype(jnp.float32), axis=0, keepdims=True)
        at = VECTORS[name][0] + start // UNIT
        for n in range(values.shape[1] // UNIT):
            vec[at + n : at + n + 1, :] += total[:, n * UNIT : (n + 1) * UNIT]

    def right_blocks(first_block, value):
        for n in range(value.shape[1] // UNIT):
            right[first_block + n] = value[:, n * UNIT : (n + 1) * UNIT]

    turns = jnp.where(first, chunks + half, half)

    def chunk_of(turn):
        late = jnp.where(first, turn >= chunks, True)
        return 1 - lax.rem(turn, 2) + jnp.where(late, half, 0)

    def loads(turn, some, action):
        for peers in (True, False):
            @pl.when((turn < half) if peers else (turn >= half))
            def _():
                i = chunk_of(turn)
                for n in some:
                    action(load(i, lax.rem(i, 2), n, peer_hbm if peers else own_hbm))

    def right_done(turn, n):
        i = chunk_of(turn)

        @pl.when(jnp.logical_and(first, turn < half))
        def _():
            right_push(i, n).wait_send()

        @pl.when(jnp.logical_not(jnp.logical_and(first, turn < half)))
        def _():
            right_copy(i, n).wait()

    def right_go(turn, n):
        i = chunk_of(turn)

        @pl.when(jnp.logical_and(first, turn < half))
        def _():
            right_push(i, n).start()

        @pl.when(jnp.logical_not(jnp.logical_and(first, turn < half)))
        def _():
            right_copy(i, n).start()

    def tail_part(turn, i):
        slot = lax.rem(i, 2)

        @pl.when(first)
        def _():
            loads(turn, (0, 1), lambda copy: copy.wait())

            @pl.when(turn < half)
            def _():
                e_push(i).wait_recv()

            @pl.when(turn == 0)
            def _():
                gains_push().wait_recv()
                gains[...] = gains_peer[...]

            @pl.when(turn == half)
            def _():
                own_gains()

            @pl.when(turn >= chunks)
            def _():
                hand_back(i).wait_recv()

        @pl.when(second)
        def _():
            e_copy(i).wait()

        @pl.when(turn >= 1)
        def _():
            for n in range(2):
                right_done(turn - 1, n)

        def ready(which):
            @pl.when(jnp.logical_and(first, jnp.logical_or(turn == 0, turn == half)))
            def _():
                w_copy(which).wait()

        now_a, total = keep_a.at[slot], dn1

        def kept(name, start=0):
            at = KEEP_A[name] + start
            return now_a[:, at : at + width].astype(jnp.float32)

        e = e_in[i].astype(jnp.float32)
        unit_two = kept("u2")
        tally("g2", 0, e * unit_two)
        tally("h2", 0, e)
        second_full = norm_back(
            e * gains[1:2, :], unit_two, stat_a[slot, :, STAT_A["s2"] : STAT_A["s2"] + 1]
        )
        second_low = second_full.astype(jnp.bfloat16)
        right_blocks(0, second_low)
        tally("bd", 0, second_low)
        total[...] = second_full

        ready(3)

        def pulled(n):
            return back_product(second_low, wd[n * width : (n + 1) * width, :])

        grad = pulled(0)
        for n in range(4):
            later = pulled(n + 1) if n < 3 else None
            hidden_low = (grad * kept("slope", n * width)).astype(jnp.bfloat16)
            right_blocks(3 + 3 * n, hidden_low)
            tally("bu", n * width, hidden_low)
            if n == 0:
                ready(2)
            total[...] += back_product(hidden_low, wu[:, n * width : (n + 1) * width])
            grad = later
        right_go(turn, 0)
        grad_normed = total[...]
        unit_one = kept("u1")
        tally("g1", 0, grad_normed * unit_one)
        tally("h1", 0, grad_normed)
        grad_first = norm_back(
            grad_normed * gains[0:1, :], unit_one, stat_a[slot, :, STAT_A["s1"] : STAT_A["s1"] + 1]
        )
        total[...] = grad_first
        first_low = grad_first.astype(jnp.bfloat16)
        right_blocks(15, first_low)
        right_go(turn, 1)
        tally("bo", 0, first_low)
        ready(1)
        grad_mixed = back_product(first_low, wo[...]).astype(jnp.bfloat16).astype(jnp.float32)
        weighed[...] = (grad_mixed * stat_a[slot, :, 0:width]).astype(jnp.bfloat16)

        @pl.when(first)
        def _():
            @pl.when(turn + 2 < turns)
            def _():
                loads(turn + 2, (0, 1), lambda copy: copy.start())

            @pl.when(turn == half - 1)
            def _():
                for which in (3, 2, 1):
                    w_copy(which).start()

    def pair_part(i, pair):
        slot = lax.rem(i, 2)
        now_b, old_b = keep_b.at[slot], keep_b.at[1 - slot]
        span = pl.ds(pl.multiple_of(pair * 128, 128), 128)

        def cut(ref, name):
            return ref[:, pl.ds(pl.multiple_of(KEEP_B[name] + pair * 128, 128), 128)]

        def half_block(source, table):
            queries, keys_in, values = cut(now_b, "q"), cut(source, "k"), cut(source, "v")
            w = weighed[:, span]
            cross = w.astype(jnp.float32) * stat_b[slot, :, span]
            zero, one = jnp.zeros_like(keys_in), jnp.ones_like(values)
            total_q, total_k, total_v = 0.0, 0.0, 0.0
            for half in range(2):
                own = low if half == 0 else jnp.logical_not(low)
                spare = 64 * (1 - half)
                inner = jnp.sum(jnp.where(own, cross, 0.0), axis=-1, keepdims=True)
                rough = inner.astype(jnp.bfloat16).astype(jnp.float32)
                extra = jnp.where(
                    lanes == spare, -rough, jnp.where(lanes == spare + 1, rough - inner, 0.0)
                ).astype(jnp.bfloat16)
                own_keys = jnp.where(own, keys_in, zero)
                scores = (back_product(queries, own_keys) * table).astype(jnp.bfloat16)
                grads = (
                    back_product(
                        jnp.where(own, w, extra), jnp.where(own, values, one)
                    )
                    * table
                ).astype(jnp.bfloat16)
                total_q += dot(grads, own_keys)
                total_k += rows_product(grads, jnp.where(own, queries, zero))
                total_v += rows_product(scores, jnp.where(own, w, zero))
            return total_q, total_k, total_v

        total_q, total_k, total_v = half_block(now_b, mix[0])
        dq[:, span] = total_q
        dk[:, span] = total_k
        dv[:, span] = total_v

        @pl.when(slot == 0)
        def _():
            dk[:, span] += carry_k[:, span]
            dv[:, span] += carry_v[:, span]

        @pl.when(slot == 1)
        def _():
            far_q, far_k, far_v = half_block(old_b, mix[1])
            dq[:, span] += far_q
            carry_k[:, span] = far_k
            carry_v[:, span] = far_v

    def head_part(turn, i):
        slot = lax.rem(i, 2)

        @pl.when(turn >= 1)
        def _():
            right_done(turn - 1, 2)

        @pl.when(jnp.logical_and(first, jnp.logical_or(turn == 0, turn == half)))
        def _():
            w_copy(0).wait()

        now_b = keep_b.at[slot]
        grad_in = dn1[...]
        for n, (source, slope) in enumerate(((dq, "sq"), (dk, "sk"), (dv, None))):
            values = source[...]
            if slope:
                at = KEEP_B[slope]
                values = values * now_b[:, at : at + width].astype(jnp.float32)
            values = values.astype(jnp.bfloat16)
            right_blocks(18 + 3 * n, values)
            tally("bp", n * width, values)
            grad_in += back_product(values, wp[:, n * width : (n + 1) * width])
        right_go(turn, 2)

        @pl.when(first)
        def _():
            @pl.when(turn < half)
            def _():
                e_in[i] = grad_in.astype(jnp.bfloat16)

            @pl.when(turn >= half)
            def _():
                @pl.when(turn > half)
                def _():
                    res_copy(chunk_of(turn - 1)).wait()

                rows_out[...] = grad_in
                res_copy(i).start()

            @pl.when(turn + 2 < turns)
            def _():
                loads(turn + 2, (2, 3), lambda copy: copy.start())

            @pl.when(turn == half - 1)
            def _():
                w_copy(0).start()
                vec_sent[...] = vec[0:40, :]
                vec_push().start()
                vec[...] = jnp.zeros_like(vec)

        @pl.when(second)
        def _():
            handed[i] = grad_in.astype(jnp.bfloat16)
            hand_back(i).start()

    def one_turn(turn, carry):
        i = chunk_of(turn)
        tail_part(turn, i)

        @pl.when(jnp.logical_and(first, lax.rem(turn, 2) == 0))
        def _():
            loads(turn, (2, 3), lambda copy: copy.wait())
            loads(turn + 1, (2, 3), lambda copy: copy.wait())

        def one_pair(pair, inner):
            pair_part(i, pair)
            return inner

        lax.fori_loop(0, pairs, one_pair, 0)
        head_part(turn, i)
        return carry

    lax.fori_loop(0, turns, one_turn, 0)
    for n in range(3):
        right_copy(half, n).wait()

    @pl.when(first)
    def _():
        res_copy(half).wait()
        vec_push().wait_send()

    @pl.when(second)
    def _():
        for i in range(half, chunks):
            hand_back(i).wait_send()
        vec_push().wait_recv()
        vec[0:40, :] += vec_peer[...]
        for i in range(half):
            for n in range(3):
                right_push(i, n).wait_recv()

    vec_out[...] = vec[...]


def run_layers(ends, mats, rows_in, mix, dp_size):
    tokens, width = ends.shape
    chunks = tokens // CHUNK
    rows = sum_sizes(dp_size)[1]
    bf16, f32 = jnp.bfloat16, jnp.float32

    def kept(count):
        return [
            jax.ShapeDtypeStruct((count * CHUNK, columns), dtype)
            for columns, dtype in (
                (KEEP_A_WIDTH, bf16), (STAT_A_WIDTH, f32), (KEEP_B_WIDTH, bf16), (width, f32)
            )
        ]

    out_shape = (
        [
            jax.ShapeDtypeStruct((21, chunks, CHUNK, UNIT), bf16),
            jax.ShapeDtypeStruct((27, chunks, CHUNK, UNIT), bf16),
        ]
        + kept(chunks)
        + kept(chunks // 2)
        + [jax.ShapeDtypeStruct(mat.shape, mat.dtype) for mat in mats]
        + [
            jax.ShapeDtypeStruct((tokens, width), f32),
            jax.ShapeDtypeStruct((rows, UNIT), f32),
        ]
    )
    chunk_f32 = pltpu.VMEM((CHUNK, width), f32)
    all_rows = pltpu.VMEM((chunks, CHUNK, width), bf16)
    dma = pltpu.SemaphoreType.DMA
    outs = pl.pallas_call(
        partial(layers_kernel, chunks),
        out_shape=out_shape,
        in_specs=any_specs(5) + vmem_specs(9),
        out_specs=any_specs(15) + vmem_specs(1),
        scratch_shapes=[pltpu.VMEM(mat.shape, mat.dtype) for mat in mats]
        + [
            all_rows,
            all_rows,
            all_rows,
            pltpu.VMEM((18, CHUNK, UNIT), bf16),
            pltpu.VMEM((27, CHUNK, UNIT), bf16),
            pltpu.VMEM((2, CHUNK, KEEP_A_WIDTH), bf16),
            pltpu.VMEM((2, CHUNK, STAT_A_WIDTH), f32),
            pltpu.VMEM((2, CHUNK, KEEP_B_WIDTH), bf16),
            pltpu.VMEM((2, CHUNK, width), f32),
            chunk_f32,
            pltpu.VMEM((HEADS, CHUNK, 128), f32),
            chunk_f32,
            chunk_f32,
            chunk_f32,
            chunk_f32,
            chunk_f32,
            chunk_f32,
            pltpu.VMEM((CHUNK, width), bf16),
            pltpu.VMEM((rows, UNIT), f32),
            pltpu.VMEM((40, UNIT), f32),
            pltpu.VMEM((40, UNIT), f32),
            pltpu.VMEM((8, width), f32),
            pltpu.VMEM((8, width), f32),
            dma((4,)),
            dma((chunks,)),
            dma((chunks, 3)),
            dma((chunks,)),
            dma,
            dma((3,)),
            dma((2, 4)),
            dma,
            dma((chunks,)),
            dma((chunks,)),
            dma((chunks,)),
            dma((chunks,)),
            dma((4,)),
            dma((4,)),
            dma((chunks // 2,)),
            dma((chunks // 2,)),
            dma((chunks // 2, 4)),
            dma((chunks // 2, 4)),
            dma((3,)),
            dma((chunks // 2, 3)),
            dma,
            dma,
            dma,
            dma,
        ],
        compiler_params=pltpu.CompilerParams(
            collective_id=2, has_side_effects=True, vmem_limit_bytes=62 << 20
        ),
        name="layers",
    )(ends, *mats, *rows_in, mix)
    return outs[14], outs[0], outs[1], outs[15]


def widen_kernel(proj, out, up, down, small, *refs):
    sources = (proj, out, up, down)
    targets, vectors = refs[:4], refs[4:12]
    held, wide_held = refs[12:16], refs[16:20]
    in_sem, out_sem = refs[20:]
    blocks = []
    for which, source in enumerate(sources):
        step = 256 if source.shape[1] > 768 else 768
        for start in range(0, source.shape[0], step):
            blocks.append((which, pl.ds(start, step)))
    copies_in = [
        pltpu.make_async_copy(sources[which].at[span], held[which].at[span], in_sem.at[n])
        for n, (which, span) in enumerate(blocks)
    ]
    copies_out = [
        pltpu.make_async_copy(wide_held[which].at[span], targets[which].at[0, span], out_sem.at[n])
        for n, (which, span) in enumerate(blocks)
    ]
    for copy in copies_in:
        copy.start()
    for (start, count), vector in zip(VECTORS.values(), vectors):
        for n in range(count):
            vector[:, n * UNIT : (n + 1) * UNIT] = small[start + n : start + n + 1, :].astype(
                jnp.float32
            )
    for n, (which, span) in enumerate(blocks):
        copies_in[n].wait()
        wide_held[which][span, :] = held[which][span, :].astype(jnp.float32)
        copies_out[n].start()
    for copy in copies_out:
        copy.wait()


def widen(proj, out, up, down, small):
    mats = (proj, out, up, down)
    return pl.pallas_call(
        widen_kernel,
        out_shape=[jax.ShapeDtypeStruct((1,) + mat.shape, jnp.float32) for mat in mats]
        + [jax.ShapeDtypeStruct((1, count * UNIT), jnp.float32) for _, count in VECTORS.values()],
        in_specs=any_specs(4) + vmem_specs(1),
        out_specs=any_specs(4) + vmem_specs(8),
        scratch_shapes=[pltpu.VMEM(mat.shape, jnp.bfloat16) for mat in mats]
        + [pltpu.VMEM(mat.shape, jnp.float32) for mat in mats]
        + [pltpu.SemaphoreType.DMA((11,)), pltpu.SemaphoreType.DMA((11,))],
        compiler_params=pltpu.CompilerParams(vmem_limit_bytes=60 << 20),
        name="widen",
    )(proj, out, up, down, small)


def mix_tables(length):
    places = jnp.arange(2 * CHUNK, dtype=jnp.int32)
    angles = places.astype(jnp.float32) * ((0.5 * math.pi) / length.astype(jnp.float32))
    cosine, sine, document = lax.optimization_barrier(
        (jnp.cos(angles), jnp.sin(angles), places // length)
    )

    def table(start):
        later, earlier = slice(start, start + CHUNK), slice(0, CHUNK)
        seen = jnp.logical_and(
            document[later, None] == document[None, earlier],
            places[later, None] >= places[None, earlier],
        )
        near = cosine[later, None] * cosine[None, earlier] + sine[later, None] * sine[None, earlier]
        return jnp.where(seen, near, 0.0)

    return jnp.stack([table(0), table(CHUNK)])


def shards(
    endpoints,
    projection,
    projection_bias,
    output_weight,
    output_bias,
    first_gain,
    first_shift,
    up_weight,
    up_bias,
    down_weight,
    down_bias,
    second_gain,
    second_shift,
    segment_length,
):
    dp_size = lax.axis_size("dp")
    mats = (projection[0], output_weight[0], up_weight[0], down_weight[0])
    rows = (
        projection_bias, output_bias, first_gain, first_shift, up_bias, down_bias, second_gain,
        second_shift,
    )
    mix = mix_tables(segment_length[0])
    results, left, right, vec = run_layers(endpoints[0], mats, rows, mix, dp_size)
    sums = reduce_gradients(left, right, vec, dp_size)
    proj, out, up, down, bp, bo, g1, h1, bu, bd, g2, h2 = widen(*sums)
    return (results[None], proj, bp, out, bo, g1, h1, up, bu, down, bd, g2, h2)


def solution(mesh):
    in_specs = (
        P("section", "dp", None),
        P("section", None, None),
        P("section", None),
        P("section", None, None),
        P("section", None),
        P("section", None),
        P("section", None),
        P("section", None, None),
        P("section", None),
        P("section", None, None),
        P("section", None),
        P("section", None),
        P("section", None),
        P("dp"),
    )
    out_specs = (
        P("section", "dp", None),
        P("section", None, None),
        P("section", None),
        P("section", None, None),
        P("section", None),
        P("section", None),
        P("section", None),
        P("section", None, None),
        P("section", None),
        P("section", None, None),
        P("section", None),
        P("section", None),
        P("section", None),
    )
    return jax.shard_map(shards, mesh=mesh, in_specs=in_specs, out_specs=out_specs, check_vma=False)
```

```python
from functools import partial
import math

import jax
import jax.numpy as jnp
from jax import lax
from jax.experimental import pallas as pl
from jax.experimental.pallas import tpu as pltpu
from jax.sharding import PartitionSpec as P

HEADS = 12
EPSILON = 1e-05
MESH = pl.DeviceIdType.MESH


def rows_product(left_mat, right_mat):
    return lax.dot_general(
        left_mat, right_mat, (((0,), (0,)), ((), ())), preferred_element_type=jnp.float32
    )


def back_product(grad_mat, weight_mat):
    return lax.dot_general(
        grad_mat, weight_mat, (((1,), (1,)), ((), ())), preferred_element_type=jnp.float32
    )


def factor_dims(count):
    bits = count.bit_length() - 1
    return (1 << (bits // 3), 1 << ((bits + 1) // 3), 1 << ((bits + 2) // 3))


ORDERS = {"a": (0, 1, 2), "b": (1, 2, 0), "c": (2, 0, 1)}
PATTERN = "abacabc"
LAG = 3
END_LAG = 4
UNIT = 256
UNITS = 108
PIECE_ROWS = 512
SEM_SLOTS = 35


def stage_list(order, dims, rows):
    stages, size, landing = [], rows, 0
    for level, ax in enumerate(order):
        part = size // dims[ax]
        for step in range(1, dims[ax]):
            stages.append(("reduce", level, ax, step, part, landing))
            landing += part if dims[ax] == 2 else 2 * part
        size = part
    for level in reversed(range(3)):
        ax = order[level]
        for step in range(1, dims[ax]):
            stages.append(("gather", level, ax, step, size, 0))
        size *= dims[ax]
    return stages, landing


def unit_blocks(unit):
    up, out, proj = unit - 36, unit - 72, unit - 81
    left = jnp.where(
        unit < 36,
        unit // 3,
        jnp.where(unit < 72, 12 + up // 12, jnp.where(unit < 81, 15 + out // 3, 18 + proj // 9)),
    )
    right = jnp.where(
        unit < 36,
        unit % 3,
        jnp.where(unit < 72, 3 + up % 12, jnp.where(unit < 81, 15 + out % 3, 18 + proj % 9)),
    )
    return left, right


def axis_places(dims):
    here = lax.axis_index("dp")
    strides = (1, dims[0], dims[0] * dims[1])
    return here, strides, [(here // strides[ax]) % dims[ax] for ax in range(3)]


def greet_axes(dims, semaphore):
    here, strides, place = axis_places(dims)
    around = 0
    for ax in range(3):
        for sign, can in ((1, place[ax] < dims[ax] - 1), (-1, place[ax] > 0)):
            @pl.when(can)
            def _():
                pl.semaphore_signal(
                    semaphore, inc=1, device_id={"dp": here + sign * strides[ax]},
                    device_id_type=MESH,
                )
            around = around + can.astype(jnp.int32)
    return around


def gather_sends(spot, count):
    found = {}
    for at in range(count):
        sent = (at + 1 if at < count - 1 else 0) + (count - at if at > 0 else 0)
        found.setdefault(sent, []).append(spot == at)
    options = []
    for sent, spots in found.items():
        can = spots[0]
        for other in spots[1:]:
            can = jnp.logical_or(can, other)
        options.append((can, sent))
    return options


def guarded(can, action):
    if can is None:
        action()
    else:
        pl.when(can)(action)


def summing(dims, pieces, rows, acc, acc_slots, full, landing, land_slots, left_hbm,
            right_hbm, vec, left_ring, right_ring, load_sem, send_sem, recv_sem):
    here, strides, place = axis_places(dims)
    ring, chunks = left_ring.shape[0], left_ring.shape[1]
    per_piece = rows // UNIT
    land_rows = landing.shape[0] // land_slots
    plans = {name: stage_list(order, dims, rows)[0] for name, order in ORDERS.items()}
    n_stages = len(plans["a"])
    shard = rows // (dims[0] * dims[1] * dims[2])
    period = len(PATTERN)

    bases = {}
    for name, order in ORDERS.items():
        base, size, found = 0, rows, []
        for ax in order:
            found.append(base)
            size = size // dims[ax]
            base = base + place[ax] * size
        bases[name] = found + [base]

    sent_rows = {}
    for name, plan in plans.items():
        sure, options = 0, [(None, 0)]
        for kind, _, ax, step, part, _ in plan:
            if dims[ax] == 2 or kind == "reduce":
                sure += part
            elif step == 1:
                options = [
                    (can if other is None else jnp.logical_and(can, other), more + part * count)
                    for other, more in options
                    for can, count in gather_sends(place[ax], dims[ax])
                ]
        sent_rows[name] = [(can, sure + more) for can, more in options]

    def view(ref, slot, start, size):
        across = ref.shape[1] // UNIT
        first = pl.multiple_of(slot // across * rows + start, 16)
        if across == 1:
            return ref.at[pl.ds(first, size)]
        return ref.at[pl.ds(first, size), pl.ds(pl.multiple_of(slot % across * UNIT, UNIT), UNIT)]

    def loads(unit):
        slot = unit % ring
        left, right = unit_blocks(unit)
        return (
            pltpu.make_async_copy(left_hbm.at[left], left_ring.at[slot], load_sem.at[slot, 0]),
            pltpu.make_async_copy(right_hbm.at[right], right_ring.at[slot], load_sem.at[slot, 1]),
        )

    def prime():
        for unit in range(ring):
            for copy in loads(jnp.int32(unit)):
                copy.start()

    def form(piece, sub):
        unit = piece * per_piece + sub
        target = view(acc, piece % acc_slots, sub * UNIT, UNIT)

        @pl.when(unit < UNITS)
        def _():
            for copy in loads(unit):
                copy.wait()
            slot = unit % ring
            tokens = chunks * left_ring.shape[2]
            target[...] = rows_product(
                left_ring[slot].reshape(tokens, UNIT), right_ring[slot].reshape(tokens, UNIT)
            ).astype(jnp.bfloat16)

            @pl.when(unit + ring < UNITS)
            def _():
                for copy in loads(unit + ring):
                    copy.start()

        @pl.when(unit >= UNITS)
        def _():
            target[...] = vec[sub * UNIT : (sub + 1) * UNIT, :].astype(jnp.bfloat16)

    def copies(name, stage, piece):
        kind, level, ax, step, part, land = plans[name][stage]
        count, spot = dims[ax], place[ax]
        slot = piece % SEM_SLOTS
        held, index = (acc, piece % acc_slots) if kind == "reduce" else (full, piece)
        land_start = piece % land_slots * land_rows + land

        def chunk(q):
            return view(held, index, bases[name][level] + q * part, part)

        def landed(way):
            return landing.at[pl.ds(pl.multiple_of(land_start + way * part, 16), part)]

        def remote(src, dst, way, sign):
            return lambda: pltpu.make_async_remote_copy(
                src_ref=src, dst_ref=dst, send_sem=send_sem.at[slot],
                recv_sem=recv_sem.at[slot, stage, way],
                device_id={"dp": here + sign * strides[ax]}, device_id_type=MESH,
            )

        sends, receives = [], []
        if count == 2:
            sign = 1 - 2 * spot
            mine, other = spot, 1 - spot
            if kind == "reduce":
                sends.append((None, remote(chunk(other), landed(0), 0, sign)))
                receives.append((None, remote(chunk(mine), landed(0), 0, sign), mine, landed(0)))
            else:
                sends.append((None, remote(chunk(mine), chunk(mine), 0, sign)))
                receives.append((None, remote(chunk(other), chunk(other), 0, sign), other, None))
            return sends, receives, chunk
        back = count - 1 - spot
        if kind == "reduce":
            for way, sign, can, q in (
                (0, 1, spot < step, spot + count - step),
                (1, -1, back < step, step - 1 - back),
            ):
                q = jnp.clip(q, 0, count - 1)
                sends.append((can, remote(chunk(q), landed(way), way, sign)))
            for way, sign, can, q in (
                (0, 1, jnp.logical_and(spot >= 1, spot - 1 < step), spot - 1 + count - step),
                (1, -1, jnp.logical_and(back >= 1, back - 1 < step), step - back),
            ):
                q = jnp.clip(q, 0, count - 1)
                receives.append((can, remote(chunk(q), landed(way), way, sign), q, landed(way)))
        else:
            for way, sign, can, q in (
                (0, 1, jnp.logical_and(back >= 1, spot >= step - 1), spot - step + 1),
                (1, -1, jnp.logical_and(spot >= 1, back >= step - 1), spot + step - 1),
            ):
                q = jnp.clip(q, 0, count - 1)
                sends.append((can, remote(chunk(q), chunk(q), way, sign)))
            for way, sign, can, q in (
                (0, 1, spot >= step, spot - step),
                (1, -1, back >= step, spot + step),
            ):
                q = jnp.clip(q, 0, count - 1)
                receives.append((can, remote(chunk(q), chunk(q), way, sign), q, None))
        return sends, receives, chunk

    def work(name, stage, piece):
        if stage > 0:
            sends, receives, chunk = copies(name, stage - 1, piece)
            for can, copy, q, landed in receives:
                def finish():
                    copy().wait_recv()
                    if landed is not None:
                        block = chunk(q)
                        block[...] = block[...] + landed[...]
                guarded(can, finish)
        if stage == n_stages // 2:
            mine = bases[name][3]
            own = view(full, piece, mine, shard)
            own[...] = view(acc, piece % acc_slots, mine, shard)[...]
        if stage < n_stages:
            for can, copy in copies(name, stage, piece)[0]:
                guarded(can, lambda: copy().start())
        if stage == n_stages:
            for can, amount in sent_rows[name]:
                sent = landing.at[pl.ds(0, amount)]
                guarded(
                    can,
                    lambda: pltpu.make_async_copy(
                        sent, sent, send_sem.at[piece % SEM_SLOTS]
                    ).wait(),
                )

    starts = [0]
    for stage in range(n_stages):
        starts.append(starts[-1] + (END_LAG if stage in (0, n_stages - 1) else LAG))
    total_ticks = pieces + starts[-1]

    def run():
        prime()

        def some_ticks(turn, carry):
            for spot_in in range(period):
                now = turn * period + spot_in
                for stage in reversed(range(n_stages + 1)):
                    piece = now - starts[stage]
                    name = PATTERN[(spot_in - starts[stage]) % period]

                    @pl.when(jnp.logical_and(piece >= 0, piece < pieces))
                    def _():
                        at = jnp.clip(piece, 0, pieces - 1)
                        if stage == 0:
                            for sub in range(per_piece):
                                form(at, sub)
                        work(name, stage, at)

            return carry

        lax.fori_loop(0, -(-total_ticks // period), some_ticks, 0)

    return run


def sum_sizes(dp_size):
    dims = factor_dims(dp_size)
    rows = max(PIECE_ROWS, 16 * dp_size)
    land = max(stage_list(order, dims, rows)[1] for order in ORDERS.values())
    return dims, rows, -(-(UNITS + 1) * UNIT // rows), land, 2 * (sum(dims) - 3)


def sum_semaphores(ring, stages):
    return [
        pltpu.SemaphoreType.DMA((ring, 2)),
        pltpu.SemaphoreType.DMA((SEM_SLOTS,)),
        pltpu.SemaphoreType.DMA((SEM_SLOTS, stages, 2)),
    ]


def reduce_kernel(dims, pieces, rows, left_hbm, right_hbm, vec, full, acc, landing, left_ring, right_ring,
                  load_sem, send_sem, recv_sem):
    barrier = pltpu.get_barrier_semaphore()
    around = greet_axes(dims, barrier)
    pl.semaphore_wait(barrier, around)
    slots = acc.shape[0] // rows
    summing(
        dims, pieces, rows, acc, slots, full, landing, slots, left_hbm, right_hbm, vec, left_ring,
        right_ring, load_sem, send_sem, recv_sem,
    )()


def reduce_gradients(left, right, vec, dp_size):
    dims, rows, pieces, land, stages = sum_sizes(dp_size)
    ring = 4 if dp_size <= 16 else 2
    slots = min(SEM_SLOTS, pieces)
    return pl.pallas_call(
        partial(reduce_kernel, dims, pieces, rows),
        out_shape=pltpu.VMEM((pieces * rows, UNIT), jnp.bfloat16),
        in_specs=any_specs(2) + vmem_specs(1),
        out_specs=pl.BlockSpec(memory_space=pltpu.VMEM),
        scratch_shapes=[
            pltpu.VMEM((slots * rows, UNIT), jnp.bfloat16),
            pltpu.VMEM((slots * land, UNIT), jnp.bfloat16),
            pltpu.VMEM((ring,) + left.shape[1:], jnp.bfloat16),
            pltpu.VMEM((ring,) + left.shape[1:], jnp.bfloat16),
        ]
        + sum_semaphores(ring, stages),
        compiler_params=pltpu.CompilerParams(
            collective_id=1, has_side_effects=True, vmem_limit_bytes=47 << 20
        ),
        name="reduce",
    )(left, right, vec)


CHUNK = 256
KEEP_A = {"slope": 0, "u1": 3072, "u2": 3840}
KEEP_A_WIDTH = 4608
STAT_A = {"rden": 0, "s1": 768, "s2": 896}
STAT_A_WIDTH = 1024
KEEP_B = {"q": 0, "k": 768, "sq": 1536, "sk": 2304, "v": 3072}
KEEP_B_WIDTH = 3840
VECTORS = {
    "bp": (0, 9), "bo": (9, 3), "g1": (12, 3), "h1": (15, 3), "bu": (18, 12), "bd": (30, 3), "g2": (33, 3),
    "h2": (36, 3),
}
TAIL_SCALE = 0.375
TAIL_POLY = (
    0.21141059805705423,
    0.21471795439954675,
    0.17184958530833144,
    0.26915459919947066,
    -0.10973686091480542,
    0.37354383408912983,
    -0.13093832475477368,
)


def dot(left_mat, right_mat):
    return jnp.dot(left_mat, right_mat, preferred_element_type=jnp.float32)


def inverse(value):
    rough = pl.reciprocal(value, approx=True)
    return rough * (2.0 - value * rough)


def gelu_pair(hidden):
    bell = jnp.exp(hidden * hidden * -0.5)
    t = inverse(1.0 + (TAIL_SCALE * math.sqrt(0.5)) * jnp.abs(hidden))
    poly = jnp.full_like(t, 0.5 * TAIL_POLY[-1])
    for coefficient in TAIL_POLY[-2::-1]:
        poly = poly * t + 0.5 * coefficient
    tail = poly * t * bell
    below = jnp.where(hidden >= 0, 1.0 - tail, tail)
    return hidden * below, below + hidden * (bell * (1.0 / math.sqrt(2.0 * math.pi)))


def softplus_pair(value):
    small = jnp.exp(-jnp.abs(value))
    whole = 1.0 + small
    log_whole = jnp.where(
        small < 1e-2, small * (1.0 - small * (0.5 - small * (1.0 / 3.0))), jnp.log(whole)
    )
    return (
        jnp.maximum(value, 0.0) + log_whole,
        jnp.where(value >= 0, 1.0, small) * inverse(whole),
    )


def centred(rows):
    centre = rows - jnp.mean(rows, axis=-1, keepdims=True)
    scaling = lax.rsqrt(jnp.mean(centre * centre, axis=-1, keepdims=True) + EPSILON)
    return centre * scaling, scaling


def wide(column, width=128):
    return jnp.broadcast_to(column, (column.shape[0], width))


def first_half(rows):
    return lax.broadcasted_iota(jnp.int32, (rows, 128), 1) < 64


def row(ref):
    return ref[...].astype(jnp.float32)


def any_specs(count):
    return [pl.BlockSpec(memory_space=pl.ANY)] * count


def vmem_specs(count):
    return [pl.BlockSpec(memory_space=pltpu.VMEM)] * count


def norm_back(grad, unit_rows, scaling):
    mean_grad = jnp.mean(grad, axis=-1, keepdims=True)
    mean_cross = jnp.mean(grad * unit_rows, axis=-1, keepdims=True)
    return scaling * (grad - mean_grad - unit_rows * mean_cross)


def layers_kernel(chunks, *refs):
    (ends_hbm, wp_hbm, wo_hbm, wu_hbm, wd_hbm, bp, bo, g1, h1, bu, bd, g2, h2, mix) = refs[:14]
    left_hbm, right_hbm = refs[14:16]
    own_hbm, peer_hbm, peer_w_hbm = refs[16:20], refs[20:24], refs[24:28]
    res_hbm, vec_out = refs[28:30]
    (wp, wo, wu, wd, x_in, e_in, handed, left, right, keep_a, stat_a, keep_b, stat_b, rows_out, nums, dq,
     dk, dv, carry_k, carry_v, dn1, weighed, vec, vec_sent, vec_peer, gains, gains_peer, w_sem, x_sem, xo_sem, e_sem, left_sem,
     right_sem, load_sem, res_sem, send_f, recv_f, send_b, recv_b, send_w, recv_w, send_e, recv_e,
     send_k, recv_k, send_r, recv_r, send_v, recv_v, send_g, recv_g) = refs[30:]

    section = lax.axis_index("section")
    first = section == 0
    second = jnp.logical_not(first)
    partner = {"section": 1 - section}
    width = ends_hbm.shape[1]
    pairs = width // 128
    half = chunks // 2
    mats_hbm, mats = (wp_hbm, wo_hbm, wu_hbm, wd_hbm), (wp, wo, wu, wd)
    kept_bufs = (keep_a, stat_a, keep_b, stat_b)

    def w_copy(which, sources=mats_hbm):
        return pltpu.make_async_copy(sources[which], mats[which], w_sem.at[which])

    def remote(src, dst, send, recv):
        return pltpu.make_async_remote_copy(
            src_ref=src, dst_ref=dst, send_sem=send, recv_sem=recv, device_id=partner,
            device_id_type=MESH,
        )

    def w_push(which):
        return remote(mats_hbm[which], peer_w_hbm[which], send_w.at[which], recv_w.at[which])

    def rows_of(i):
        return pl.ds(pl.multiple_of(i * CHUNK, CHUNK), CHUNK)

    def x_copy(i):
        return pltpu.make_async_copy(ends_hbm.at[rows_of(i)], x_in.at[i], x_sem.at[i])

    def x_out_copies(i):
        return [
            pltpu.make_async_copy(
                x_in.at[i, :, n * UNIT : (n + 1) * UNIT], left_hbm.at[18 + n, i], xo_sem.at[i, n]
            )
            for n in range(3)
        ]

    def e_copy(i):
        return pltpu.make_async_copy(ends_hbm.at[rows_of(i)], e_in.at[i], e_sem.at[i])

    def e_push(i):
        return remote(ends_hbm.at[rows_of(i)], e_in.at[i], send_e.at[i], recv_e.at[i])

    def hand_on(i):
        return remote(handed.at[i], x_in.at[i], send_f.at[i], recv_f.at[i])

    def hand_back(i):
        return remote(handed.at[i], e_in.at[i], send_b.at[i], recv_b.at[i])

    def left_copy(i):
        return pltpu.make_async_copy(left, left_hbm.at[0:18, i], left_sem)

    spans = ((0, 15), (15, 18), (18, 27))

    def right_copy(i, n):
        start, end = spans[n]
        return pltpu.make_async_copy(
            right.at[start:end], right_hbm.at[start:end, i], right_sem.at[n]
        )

    def right_push(i, n):
        start, end = spans[n]
        return remote(
            right.at[start:end], right_hbm.at[start:end, i], send_r.at[n], recv_r.at[i, n]
        )

    def save(i, slot, n):
        return pltpu.make_async_copy(
            kept_bufs[n].at[slot], own_hbm[n].at[rows_of(i)], load_sem.at[slot, n]
        )

    def push(i, slot, n):
        return remote(
            kept_bufs[n].at[slot], peer_hbm[n].at[rows_of(i)], send_k.at[i, n], recv_k.at[i, n]
        )

    def load(i, slot, n, source):
        return pltpu.make_async_copy(
            source[n].at[rows_of(i)], kept_bufs[n].at[slot], load_sem.at[slot, n]
        )

    def res_copy(i):
        return pltpu.make_async_copy(rows_out, res_hbm.at[rows_of(i)], res_sem)

    def own_gains():
        gains[0:1, :] = row(g1)
        gains[1:2, :] = row(g2)

    def gains_push():
        return remote(gains, gains_peer, send_g, recv_g)

    def vec_push():
        return remote(vec_sent, vec_peer, send_v, recv_v)

    @pl.when(first)
    def _():
        x_copy(0).start()

    for which in range(4):
        w_copy(which).start()

    @pl.when(first)
    def _():
        for i in range(1, chunks):
            x_copy(i).start()

    @pl.when(second)
    def _():
        for i in range(half, chunks):
            e_copy(i).start()

    barrier = pltpu.get_barrier_semaphore()
    pl.semaphore_signal(barrier, inc=1, device_id=partner, device_id_type=MESH)
    vec[...] = jnp.zeros_like(vec)
    gains[...] = jnp.zeros_like(gains)
    own_gains()
    pl.semaphore_wait(barrier, 1)

    @pl.when(second)
    def _():
        gains_push().start()
        for i in range(half):
            e_push(i).start()
        for which in (3, 2, 1, 0):
            w_push(which).start()

    def weights_ready(i, which):
        @pl.when(i == 0)
        def _():
            w_copy(which).wait()

    lanes = lax.broadcasted_iota(jnp.int32, (CHUNK, 128), 1)
    low = lanes < 64

    def forward_chunk(i, carry):
        slot = lax.rem(i, 2)

        @pl.when(i >= 2)
        def _():
            @pl.when(first)
            def _():
                for n in range(4):
                    save(i - 2, slot, n).wait()

            @pl.when(second)
            def _():
                for n in range(4):
                    push(i - 2, slot, n).wait_send()

        weights_ready(i, 0)

        @pl.when(first)
        def _():
            x_copy(i).wait()

        @pl.when(second)
        def _():
            hand_on(i).wait_recv()

        for copy in x_out_copies(i):
            copy.start()
        now_a, now_b, old_b = keep_a.at[slot], keep_b.at[slot], keep_b.at[1 - slot]

        def keep(ref, start, value):
            ref[:, start : start + value.shape[1]] = value.astype(jnp.bfloat16)

        def blocks(first_block, value):
            for n in range(value.shape[1] // UNIT):
                left[first_block + n] = value[:, n * UNIT : (n + 1) * UNIT]

        x = x_in[i]
        for part, (name, slope) in enumerate((("q", "sq"), ("k", "sk"))):
            cols = slice(part * width, (part + 1) * width)
            soft, sigma = softplus_pair(dot(x, wp[:, cols]) + row(bp)[:, cols])
            keep(now_b, KEEP_B[name], soft)
            keep(now_b, KEEP_B[slope], sigma)
        cols = slice(2 * width, 3 * width)
        keep(now_b, KEEP_B["v"], dot(x, wp[:, cols]) + row(bp)[:, cols])

        def mix_pair(pair, source, table, fresh):
            def cut(ref, name):
                return ref[:, KEEP_B[name] + pair * 128 : KEEP_B[name] + (pair + 1) * 128]

            queries, keys_in, values = cut(now_b, "q"), cut(source, "k"), cut(source, "v")
            zero, one = jnp.zeros_like(keys_in), jnp.ones_like(values)
            for half in range(2):
                own = low if half == 0 else jnp.logical_not(low)
                scores = back_product(queries, jnp.where(own, keys_in, zero)) * table
                num = dot(scores.astype(jnp.bfloat16), jnp.where(own, values, one))
                at = 2 * pair + half
                nums[at] = num if fresh else nums[at] + num

        for pair in range(pairs):
            mix_pair(pair, now_b, mix[0], True)

        @pl.when(slot == 1)
        def _():
            for pair in range(pairs):
                mix_pair(pair, old_b, mix[1], False)

        @pl.when(i >= 1)
        def _():
            left_copy(i - 1).wait()

        for pair in range(pairs):
            num_a, num_b = nums[2 * pair], nums[2 * pair + 1]
            inv = inverse(
                jnp.where(low, pltpu.roll(num_a, 64, 1), pltpu.roll(num_b, 64, 1))
            )
            span = slice(pair * 128, (pair + 1) * 128)
            stat_b[slot, :, span] = jnp.where(low, num_a, num_b) * inv
            stat_a[slot, :, span] = inv
        blocks(15, stat_b[slot].astype(jnp.bfloat16))
        weights_ready(i, 1)
        first_sum = x.astype(jnp.float32) + row(bo)
        for n in range(3):
            first_sum += dot(left[15 + n], wo[n * UNIT : (n + 1) * UNIT, :])
        unit_one, scale_one = centred(first_sum)
        keep(now_a, KEEP_A["u1"], unit_one)
        stat_a[slot, :, STAT_A["s1"] : STAT_A["s1"] + 128] = wide(scale_one)
        normed = unit_one * row(g1) + row(h1)
        resid = dn1
        resid[...] = normed + row(bd)
        up_in = normed.astype(jnp.bfloat16)
        blocks(12, up_in)
        weights_ready(i, 2)

        def hidden_of(n):
            cols = slice(n * width, (n + 1) * width)
            return dot(up_in, wu[:, cols]) + row(bu)[:, cols]

        hidden = hidden_of(0)
        for n in range(4):
            later = hidden_of(n + 1) if n < 3 else None
            active, slope = gelu_pair(hidden)
            active = active.astype(jnp.bfloat16)
            blocks(3 * n, active)
            keep(now_a, n * width, slope)
            if n == 0:
                weights_ready(i, 3)
            resid[...] += dot(active, wd[n * width : (n + 1) * width, :])
            hidden = later
        unit_two, scale_two = centred(resid[...])
        keep(now_a, KEEP_A["u2"], unit_two)
        stat_a[slot, :, STAT_A["s2"] : STAT_A["s2"] + 128] = wide(scale_two)
        result = unit_two * row(g2) + row(h2)

        @pl.when(first)
        def _():
            handed[i] = result.astype(jnp.bfloat16)
            hand_on(i).start()

        @pl.when(second)
        def _():
            @pl.when(i >= 1)
            def _():
                res_copy(i - 1).wait()

            rows_out[...] = result
            res_copy(i).start()

        left_copy(i).start()

        @pl.when(first)
        def _():
            for n in range(4):
                save(i, slot, n).start()

        @pl.when(jnp.logical_and(second, i < half))
        def _():
            for n in range(4):
                push(i, slot, n).start()

        return carry

    lax.fori_loop(0, chunks, forward_chunk, 0)
    left_copy(chunks - 1).wait()
    for i in range(chunks):
        for copy in x_out_copies(i):
            copy.wait()

    @pl.when(first)
    def _():
        for i in range(half, chunks):
            for n in range(4):
                save(i, i % 2, n).wait()
        for which in (3, 2, 1, 0):
            w_push(which).wait_recv()
            w_copy(which, peer_w_hbm).start()
        for i in (1, 0):
            for n in range(4):
                push(i, i, n).wait_recv()
                load(i, i, n, peer_hbm).start()
        for i in range(chunks):
            hand_on(i).wait_send()

    @pl.when(second)
    def _():
        res_copy(chunks - 1).wait()
        for i in range(half):
            e_push(i).wait_send()
        gains_push().wait_send()
        for which in range(4):
            w_push(which).wait_send()

    def tally(name, start, values):
        total = jnp.sum(values.astype(jnp.float32), axis=0, keepdims=True)
        at = VECTORS[name][0] + start // UNIT
        for n in range(values.shape[1] // UNIT):
            vec[at + n : at + n + 1, :] += total[:, n * UNIT : (n + 1) * UNIT]

    def right_blocks(first_block, value):
        for n in range(value.shape[1] // UNIT):
            right[first_block + n] = value[:, n * UNIT : (n + 1) * UNIT]

    turns = jnp.where(first, chunks + half, half)

    def chunk_of(turn):
        late = jnp.where(first, turn >= chunks, True)
        return 1 - lax.rem(turn, 2) + jnp.where(late, half, 0)

    def loads(turn, some, action):
        for peers in (True, False):
            @pl.when((turn < half) if peers else (turn >= half))
            def _():
                i = chunk_of(turn)
                for n in some:
                    action(load(i, lax.rem(i, 2), n, peer_hbm if peers else own_hbm))

    def right_done(turn, n):
        i = chunk_of(turn)

        @pl.when(jnp.logical_and(first, turn < half))
        def _():
            right_push(i, n).wait_send()

        @pl.when(jnp.logical_not(jnp.logical_and(first, turn < half)))
        def _():
            right_copy(i, n).wait()

    def right_go(turn, n):
        i = chunk_of(turn)

        @pl.when(jnp.logical_and(first, turn < half))
        def _():
            right_push(i, n).start()

        @pl.when(jnp.logical_not(jnp.logical_and(first, turn < half)))
        def _():
            right_copy(i, n).start()

    def tail_part(turn, i):
        slot = lax.rem(i, 2)

        @pl.when(first)
        def _():
            loads(turn, (0, 1), lambda copy: copy.wait())

            @pl.when(turn < half)
            def _():
                e_push(i).wait_recv()

            @pl.when(turn == 0)
            def _():
                gains_push().wait_recv()
                gains[...] = gains_peer[...]

            @pl.when(turn == half)
            def _():
                own_gains()

            @pl.when(turn >= chunks)
            def _():
                hand_back(i).wait_recv()

        @pl.when(second)
        def _():
            e_copy(i).wait()

        @pl.when(turn >= 1)
        def _():
            for n in range(2):
                right_done(turn - 1, n)

        def ready(which):
            @pl.when(jnp.logical_and(first, jnp.logical_or(turn == 0, turn == half)))
            def _():
                w_copy(which).wait()

        now_a, total = keep_a.at[slot], dn1

        def kept(name, start=0):
            at = KEEP_A[name] + start
            return now_a[:, at : at + width].astype(jnp.float32)

        e = e_in[i].astype(jnp.float32)
        unit_two = kept("u2")
        tally("g2", 0, e * unit_two)
        tally("h2", 0, e)
        second_full = norm_back(
            e * gains[1:2, :], unit_two, stat_a[slot, :, STAT_A["s2"] : STAT_A["s2"] + 1]
        )
        second_low = second_full.astype(jnp.bfloat16)
        right_blocks(0, second_low)
        tally("bd", 0, second_low)
        total[...] = second_full

        ready(3)

        def pulled(n):
            return back_product(second_low, wd[n * width : (n + 1) * width, :])

        grad = pulled(0)
        for n in range(4):
            later = pulled(n + 1) if n < 3 else None
            hidden_low = (grad * kept("slope", n * width)).astype(jnp.bfloat16)
            right_blocks(3 + 3 * n, hidden_low)
            tally("bu", n * width, hidden_low)
            if n == 0:
                ready(2)
            total[...] += back_product(hidden_low, wu[:, n * width : (n + 1) * width])
            grad = later
        right_go(turn, 0)
        grad_normed = total[...]
        unit_one = kept("u1")
        tally("g1", 0, grad_normed * unit_one)
        tally("h1", 0, grad_normed)
        grad_first = norm_back(
            grad_normed * gains[0:1, :], unit_one, stat_a[slot, :, STAT_A["s1"] : STAT_A["s1"] + 1]
        )
        total[...] = grad_first
        first_low = grad_first.astype(jnp.bfloat16)
        right_blocks(15, first_low)
        right_go(turn, 1)
        tally("bo", 0, first_low)
        ready(1)
        grad_mixed = back_product(first_low, wo[...]).astype(jnp.bfloat16).astype(jnp.float32)
        weighed[...] = (grad_mixed * stat_a[slot, :, 0:width]).astype(jnp.bfloat16)

        @pl.when(first)
        def _():
            @pl.when(turn + 2 < turns)
            def _():
                loads(turn + 2, (0, 1), lambda copy: copy.start())

            @pl.when(turn == half - 1)
            def _():
                for which in (3, 2, 1):
                    w_copy(which).start()

    def pair_part(i, pair):
        slot = lax.rem(i, 2)
        now_b, old_b = keep_b.at[slot], keep_b.at[1 - slot]
        span = pl.ds(pl.multiple_of(pair * 128, 128), 128)

        def cut(ref, name):
            return ref[:, pl.ds(pl.multiple_of(KEEP_B[name] + pair * 128, 128), 128)]

        def half_block(source, table):
            queries, keys_in, values = cut(now_b, "q"), cut(source, "k"), cut(source, "v")
            w = weighed[:, span]
            cross = w.astype(jnp.float32) * stat_b[slot, :, span]
            zero, one = jnp.zeros_like(keys_in), jnp.ones_like(values)
            total_q, total_k, total_v = 0.0, 0.0, 0.0
            for half in range(2):
                own = low if half == 0 else jnp.logical_not(low)
                spare = 64 * (1 - half)
                inner = jnp.sum(jnp.where(own, cross, 0.0), axis=-1, keepdims=True)
                rough = inner.astype(jnp.bfloat16).astype(jnp.float32)
                extra = jnp.where(
                    lanes == spare, -rough, jnp.where(lanes == spare + 1, rough - inner, 0.0)
                ).astype(jnp.bfloat16)
                own_keys = jnp.where(own, keys_in, zero)
                scores = (back_product(queries, own_keys) * table).astype(jnp.bfloat16)
                grads = (
                    back_product(
                        jnp.where(own, w, extra), jnp.where(own, values, one)
                    )
                    * table
                ).astype(jnp.bfloat16)
                total_q += dot(grads, own_keys)
                total_k += rows_product(grads, jnp.where(own, queries, zero))
                total_v += rows_product(scores, jnp.where(own, w, zero))
            return total_q, total_k, total_v

        total_q, total_k, total_v = half_block(now_b, mix[0])
        dq[:, span] = total_q
        dk[:, span] = total_k
        dv[:, span] = total_v

        @pl.when(slot == 0)
        def _():
            dk[:, span] += carry_k[:, span]
            dv[:, span] += carry_v[:, span]

        @pl.when(slot == 1)
        def _():
            far_q, far_k, far_v = half_block(old_b, mix[1])
            dq[:, span] += far_q
            carry_k[:, span] = far_k
            carry_v[:, span] = far_v

    def head_part(turn, i):
        slot = lax.rem(i, 2)

        @pl.when(turn >= 1)
        def _():
            right_done(turn - 1, 2)

        @pl.when(jnp.logical_and(first, jnp.logical_or(turn == 0, turn == half)))
        def _():
            w_copy(0).wait()

        now_b = keep_b.at[slot]
        grad_in = dn1[...]
        for n, (source, slope) in enumerate(((dq, "sq"), (dk, "sk"), (dv, None))):
            values = source[...]
            if slope:
                at = KEEP_B[slope]
                values = values * now_b[:, at : at + width].astype(jnp.float32)
            values = values.astype(jnp.bfloat16)
            right_blocks(18 + 3 * n, values)
            tally("bp", n * width, values)
            grad_in += back_product(values, wp[:, n * width : (n + 1) * width])
        right_go(turn, 2)

        @pl.when(first)
        def _():
            @pl.when(turn < half)
            def _():
                e_in[i] = grad_in.astype(jnp.bfloat16)

            @pl.when(turn >= half)
            def _():
                @pl.when(turn > half)
                def _():
                    res_copy(chunk_of(turn - 1)).wait()

                rows_out[...] = grad_in
                res_copy(i).start()

            @pl.when(turn + 2 < turns)
            def _():
                loads(turn + 2, (2, 3), lambda copy: copy.start())

            @pl.when(turn == half - 1)
            def _():
                w_copy(0).start()
                vec_sent[...] = vec[0:40, :]
                vec_push().start()
                vec[...] = jnp.zeros_like(vec)

        @pl.when(second)
        def _():
            handed[i] = grad_in.astype(jnp.bfloat16)
            hand_back(i).start()

    def one_turn(turn, carry):
        i = chunk_of(turn)
        tail_part(turn, i)

        @pl.when(jnp.logical_and(first, lax.rem(turn, 2) == 0))
        def _():
            loads(turn, (2, 3), lambda copy: copy.wait())
            loads(turn + 1, (2, 3), lambda copy: copy.wait())

        def one_pair(pair, inner):
            pair_part(i, pair)
            return inner

        lax.fori_loop(0, pairs, one_pair, 0)
        head_part(turn, i)
        return carry

    lax.fori_loop(0, turns, one_turn, 0)
    for n in range(3):
        right_copy(half, n).wait()

    @pl.when(first)
    def _():
        res_copy(half).wait()
        vec_push().wait_send()

    @pl.when(second)
    def _():
        for i in range(half, chunks):
            hand_back(i).wait_send()
        vec_push().wait_recv()
        vec[0:40, :] += vec_peer[...]
        for i in range(half):
            for n in range(3):
                right_push(i, n).wait_recv()

    vec_out[...] = vec[...]


def run_layers(ends, mats, rows_in, mix, dp_size):
    tokens, width = ends.shape
    chunks = tokens // CHUNK
    rows = sum_sizes(dp_size)[1]
    bf16, f32 = jnp.bfloat16, jnp.float32

    def kept(count):
        return [
            jax.ShapeDtypeStruct((count * CHUNK, columns), dtype)
            for columns, dtype in (
                (KEEP_A_WIDTH, bf16), (STAT_A_WIDTH, f32), (KEEP_B_WIDTH, bf16), (width, f32)
            )
        ]

    out_shape = (
        [
            jax.ShapeDtypeStruct((21, chunks, CHUNK, UNIT), bf16),
            jax.ShapeDtypeStruct((27, chunks, CHUNK, UNIT), bf16),
        ]
        + kept(chunks)
        + kept(chunks // 2)
        + [jax.ShapeDtypeStruct(mat.shape, mat.dtype) for mat in mats]
        + [
            jax.ShapeDtypeStruct((tokens, width), f32),
            jax.ShapeDtypeStruct((rows, UNIT), f32),
        ]
    )
    chunk_f32 = pltpu.VMEM((CHUNK, width), f32)
    all_rows = pltpu.VMEM((chunks, CHUNK, width), bf16)
    dma = pltpu.SemaphoreType.DMA
    outs = pl.pallas_call(
        partial(layers_kernel, chunks),
        out_shape=out_shape,
        in_specs=any_specs(5) + vmem_specs(9),
        out_specs=any_specs(15) + vmem_specs(1),
        scratch_shapes=[pltpu.VMEM(mat.shape, mat.dtype) for mat in mats]
        + [
            all_rows,
            all_rows,
            all_rows,
            pltpu.VMEM((18, CHUNK, UNIT), bf16),
            pltpu.VMEM((27, CHUNK, UNIT), bf16),
            pltpu.VMEM((2, CHUNK, KEEP_A_WIDTH), bf16),
            pltpu.VMEM((2, CHUNK, STAT_A_WIDTH), f32),
            pltpu.VMEM((2, CHUNK, KEEP_B_WIDTH), bf16),
            pltpu.VMEM((2, CHUNK, width), f32),
            chunk_f32,
            pltpu.VMEM((HEADS, CHUNK, 128), f32),
            chunk_f32,
            chunk_f32,
            chunk_f32,
            chunk_f32,
            chunk_f32,
            chunk_f32,
            pltpu.VMEM((CHUNK, width), bf16),
            pltpu.VMEM((rows, UNIT), f32),
            pltpu.VMEM((40, UNIT), f32),
            pltpu.VMEM((40, UNIT), f32),
            pltpu.VMEM((8, width), f32),
            pltpu.VMEM((8, width), f32),
            dma((4,)),
            dma((chunks,)),
            dma((chunks, 3)),
            dma((chunks,)),
            dma,
            dma((3,)),
            dma((2, 4)),
            dma,
            dma((chunks,)),
            dma((chunks,)),
            dma((chunks,)),
            dma((chunks,)),
            dma((4,)),
            dma((4,)),
            dma((chunks // 2,)),
            dma((chunks // 2,)),
            dma((chunks // 2, 4)),
            dma((chunks // 2, 4)),
            dma((3,)),
            dma((chunks // 2, 3)),
            dma,
            dma,
            dma,
            dma,
        ],
        compiler_params=pltpu.CompilerParams(
            collective_id=2, has_side_effects=True, vmem_limit_bytes=62 << 20
        ),
        name="layers",
    )(ends, *mats, *rows_in, mix)
    return outs[14], outs[0], outs[1], outs[15]


MATRICES = ((81, 9, 3), (72, 3, 3), (36, 12, 3), (0, 3, 12))


def widen_kernel(full, *refs):
    targets, vectors, held, out_sem = refs[:4], refs[4:12], refs[12:16], refs[16]
    copies, turn = [], 0
    for which, (begin, across, down) in enumerate(MATRICES):
        for block in range(down):
            span = pl.ds(block * UNIT, UNIT)
            copy = pltpu.make_async_copy(
                held[which].at[span], targets[which].at[0, span], out_sem.at[turn]
            )

            def one(n, carry):
                start = pl.multiple_of((begin + block * across + n) * UNIT, UNIT)
                held[which][span, pl.ds(pl.multiple_of(n * UNIT, UNIT), UNIT)] = full[
                    pl.ds(start, UNIT), :
                ].astype(jnp.float32)
                return carry

            lax.fori_loop(0, across, one, 0)
            copy.start()
            copies.append(copy)
            turn += 1
    for (start, count), vector in zip(VECTORS.values(), vectors):
        for n in range(count):
            at = UNITS * UNIT + start + n
            vector[:, n * UNIT : (n + 1) * UNIT] = full[at : at + 1, :].astype(jnp.float32)
    for copy in copies:
        copy.wait()


def widen(full):
    shapes = [(down * UNIT, across * UNIT) for _, across, down in MATRICES]
    return pl.pallas_call(
        widen_kernel,
        out_shape=[jax.ShapeDtypeStruct((1,) + shape, jnp.float32) for shape in shapes]
        + [jax.ShapeDtypeStruct((1, count * UNIT), jnp.float32) for _, count in VECTORS.values()],
        in_specs=[pl.BlockSpec(memory_space=pltpu.VMEM)],
        out_specs=any_specs(4) + vmem_specs(8),
        scratch_shapes=[pltpu.VMEM(shape, jnp.float32) for shape in shapes]
        + [pltpu.SemaphoreType.DMA((sum(down for _, _, down in MATRICES),))],
        compiler_params=pltpu.CompilerParams(vmem_limit_bytes=36 << 20),
        name="widen",
    )(full)


def mix_tables(length):
    places = jnp.arange(2 * CHUNK, dtype=jnp.int32)
    angles = places.astype(jnp.float32) * ((0.5 * math.pi) / length.astype(jnp.float32))
    cosine, sine, document = lax.optimization_barrier(
        (jnp.cos(angles), jnp.sin(angles), places // length)
    )

    def table(start):
        later, earlier = slice(start, start + CHUNK), slice(0, CHUNK)
        seen = jnp.logical_and(
            document[later, None] == document[None, earlier],
            places[later, None] >= places[None, earlier],
        )
        near = cosine[later, None] * cosine[None, earlier] + sine[later, None] * sine[None, earlier]
        return jnp.where(seen, near, 0.0)

    return jnp.stack([table(0), table(CHUNK)])


def shards(
    endpoints,
    projection,
    projection_bias,
    output_weight,
    output_bias,
    first_gain,
    first_shift,
    up_weight,
    up_bias,
    down_weight,
    down_bias,
    second_gain,
    second_shift,
    segment_length,
):
    dp_size = lax.axis_size("dp")
    mats = (projection[0], output_weight[0], up_weight[0], down_weight[0])
    rows = (
        projection_bias, output_bias, first_gain, first_shift, up_bias, down_bias, second_gain,
        second_shift,
    )
    mix = mix_tables(segment_length[0])
    results, left, right, vec = run_layers(endpoints[0], mats, rows, mix, dp_size)
    full = reduce_gradients(left, right, vec, dp_size)
    proj, out, up, down, bp, bo, g1, h1, bu, bd, g2, h2 = widen(full)
    return (results[None], proj, bp, out, bo, g1, h1, up, bu, down, bd, g2, h2)


def solution(mesh):
    in_specs = (
        P("section", "dp", None),
        P("section", None, None),
        P("section", None),
        P("section", None, None),
        P("section", None),
        P("section", None),
        P("section", None),
        P("section", None, None),
        P("section", None),
        P("section", None, None),
        P("section", None),
        P("section", None),
        P("section", None),
        P("dp"),
    )
    out_specs = (
        P("section", "dp", None),
        P("section", None, None),
        P("section", None),
        P("section", None, None),
        P("section", None),
        P("section", None),
        P("section", None),
        P("section", None, None),
        P("section", None),
        P("section", None, None),
        P("section", None),
        P("section", None),
        P("section", None),
    )
    return jax.shard_map(shards, mesh=mesh, in_specs=in_specs, out_specs=out_specs, check_vma=False)
```

```python
from functools import partial
import math

import jax
import jax.numpy as jnp
from jax import lax
from jax.experimental import pallas as pl
from jax.experimental.pallas import tpu as pltpu
from jax.sharding import PartitionSpec as P

HEADS = 12
EPSILON = 1e-05
MESH = pl.DeviceIdType.MESH


def rows_product(left_mat, right_mat):
    return lax.dot_general(
        left_mat, right_mat, (((0,), (0,)), ((), ())), preferred_element_type=jnp.float32
    )


def back_product(grad_mat, weight_mat):
    return lax.dot_general(
        grad_mat, weight_mat, (((1,), (1,)), ((), ())), preferred_element_type=jnp.float32
    )


def factor_dims(count):
    bits = count.bit_length() - 1
    return (1 << (bits // 3), 1 << ((bits + 1) // 3), 1 << ((bits + 2) // 3))


ORDERS = {"a": (0, 1, 2), "b": (1, 2, 0), "c": (2, 0, 1)}
PATTERN = "abacabc"
LAG = 3
END_LAG = 4
UNIT = 256
UNITS = 108
PIECE_ROWS = 512
SEM_SLOTS = 35


def stage_list(order, dims, rows):
    stages, size, landing = [], rows, 0
    for level, ax in enumerate(order):
        part = size // dims[ax]
        for step in range(1, dims[ax]):
            stages.append(("reduce", level, ax, step, part, landing))
            landing += part if dims[ax] == 2 else 2 * part
        size = part
    for level in reversed(range(3)):
        ax = order[level]
        for step in range(1, dims[ax]):
            stages.append(("gather", level, ax, step, size, 0))
        size *= dims[ax]
    return stages, landing


def unit_blocks(unit):
    up, out, proj = unit - 36, unit - 72, unit - 81
    left = jnp.where(
        unit < 36,
        unit // 3,
        jnp.where(unit < 72, 12 + up // 12, jnp.where(unit < 81, 15 + out // 3, 18 + proj // 9)),
    )
    right = jnp.where(
        unit < 36,
        unit % 3,
        jnp.where(unit < 72, 3 + up % 12, jnp.where(unit < 81, 15 + out % 3, 18 + proj % 9)),
    )
    return left, right


def axis_places(dims):
    here = lax.axis_index("dp")
    strides = (1, dims[0], dims[0] * dims[1])
    return here, strides, [(here // strides[ax]) % dims[ax] for ax in range(3)]


def greet_axes(dims, semaphore):
    here, strides, place = axis_places(dims)
    around = 0
    for ax in range(3):
        for sign, can in ((1, place[ax] < dims[ax] - 1), (-1, place[ax] > 0)):
            @pl.when(can)
            def _():
                pl.semaphore_signal(
                    semaphore, inc=1, device_id={"dp": here + sign * strides[ax]},
                    device_id_type=MESH,
                )
            around = around + can.astype(jnp.int32)
    return around


def gather_sends(spot, count):
    found = {}
    for at in range(count):
        sent = (at + 1 if at < count - 1 else 0) + (count - at if at > 0 else 0)
        found.setdefault(sent, []).append(spot == at)
    options = []
    for sent, spots in found.items():
        can = spots[0]
        for other in spots[1:]:
            can = jnp.logical_or(can, other)
        options.append((can, sent))
    return options


def guarded(can, action):
    if can is None:
        action()
    else:
        pl.when(can)(action)


def summing(dims, pieces, rows, acc, acc_slots, full, landing, land_slots, left_hbm,
            right_hbm, vec_hbm, vec, left_ring, right_ring, load_sem, vec_sem, send_sem, recv_sem):
    here, strides, place = axis_places(dims)
    ring, chunks = left_ring.shape[0], left_ring.shape[1]
    per_piece = rows // UNIT
    land_rows = landing.shape[0] // land_slots
    plans = {name: stage_list(order, dims, rows)[0] for name, order in ORDERS.items()}
    n_stages = len(plans["a"])
    shard = rows // (dims[0] * dims[1] * dims[2])
    period = len(PATTERN)

    bases = {}
    for name, order in ORDERS.items():
        base, size, found = 0, rows, []
        for ax in order:
            found.append(base)
            size = size // dims[ax]
            base = base + place[ax] * size
        bases[name] = found + [base]

    sent_rows = {}
    for name, plan in plans.items():
        sure, options = 0, [(None, 0)]
        for kind, _, ax, step, part, _ in plan:
            if dims[ax] == 2 or kind == "reduce":
                sure += part
            elif step == 1:
                options = [
                    (can if other is None else jnp.logical_and(can, other), more + part * count)
                    for other, more in options
                    for can, count in gather_sends(place[ax], dims[ax])
                ]
        sent_rows[name] = [(can, sure + more) for can, more in options]

    def view(ref, slot, start, size):
        across = ref.shape[1] // UNIT
        first = pl.multiple_of(slot // across * rows + start, 16)
        if across == 1:
            return ref.at[pl.ds(first, size)]
        return ref.at[pl.ds(first, size), pl.ds(pl.multiple_of(slot % across * UNIT, UNIT), UNIT)]

    def loads(unit):
        slot = unit % ring
        left, right = unit_blocks(unit)
        return (
            pltpu.make_async_copy(left_hbm.at[left], left_ring.at[slot], load_sem.at[slot, 0]),
            pltpu.make_async_copy(right_hbm.at[right], right_ring.at[slot], load_sem.at[slot, 1]),
        )

    def prime():
        for unit in range(ring):
            for copy in loads(jnp.int32(unit)):
                copy.start()

    vec_copy = pltpu.make_async_copy(vec_hbm, vec.at[pl.ds(0, vec_hbm.shape[0])], vec_sem)

    def form(piece, sub):
        unit = piece * per_piece + sub
        target = view(acc, piece % acc_slots, sub * UNIT, UNIT)

        @pl.when(unit < UNITS)
        def _():
            for copy in loads(unit):
                copy.wait()
            slot = unit % ring
            tokens = chunks * left_ring.shape[2]
            target[...] = rows_product(
                left_ring[slot].reshape(tokens, UNIT), right_ring[slot].reshape(tokens, UNIT)
            ).astype(jnp.bfloat16)

            @pl.when(unit + ring < UNITS)
            def _():
                for copy in loads(unit + ring):
                    copy.start()

        @pl.when(unit >= UNITS)
        def _():
            if sub == 0:
                vec_copy.wait()
            target[...] = vec[sub * UNIT : (sub + 1) * UNIT, :].astype(jnp.bfloat16)

    def copies(name, stage, piece):
        kind, level, ax, step, part, land = plans[name][stage]
        count, spot = dims[ax], place[ax]
        slot = piece % SEM_SLOTS
        held, index = (acc, piece % acc_slots) if kind == "reduce" else (full, piece)
        land_start = piece % land_slots * land_rows + land

        def chunk(q):
            return view(held, index, bases[name][level] + q * part, part)

        def landed(way):
            return landing.at[pl.ds(pl.multiple_of(land_start + way * part, 16), part)]

        def remote(src, dst, way, sign):
            return lambda: pltpu.make_async_remote_copy(
                src_ref=src, dst_ref=dst, send_sem=send_sem.at[slot],
                recv_sem=recv_sem.at[slot, stage, way],
                device_id={"dp": here + sign * strides[ax]}, device_id_type=MESH,
            )

        sends, receives = [], []
        if count == 2:
            sign = 1 - 2 * spot
            mine, other = spot, 1 - spot
            if kind == "reduce":
                sends.append((None, remote(chunk(other), landed(0), 0, sign)))
                receives.append((None, remote(chunk(mine), landed(0), 0, sign), mine, landed(0)))
            else:
                sends.append((None, remote(chunk(mine), chunk(mine), 0, sign)))
                receives.append((None, remote(chunk(other), chunk(other), 0, sign), other, None))
            return sends, receives, chunk
        back = count - 1 - spot
        if kind == "reduce":
            for way, sign, can, q in (
                (0, 1, spot < step, spot + count - step),
                (1, -1, back < step, step - 1 - back),
            ):
                q = jnp.clip(q, 0, count - 1)
                sends.append((can, remote(chunk(q), landed(way), way, sign)))
            for way, sign, can, q in (
                (0, 1, jnp.logical_and(spot >= 1, spot - 1 < step), spot - 1 + count - step),
                (1, -1, jnp.logical_and(back >= 1, back - 1 < step), step - back),
            ):
                q = jnp.clip(q, 0, count - 1)
                receives.append((can, remote(chunk(q), landed(way), way, sign), q, landed(way)))
        else:
            for way, sign, can, q in (
                (0, 1, jnp.logical_and(back >= 1, spot >= step - 1), spot - step + 1),
                (1, -1, jnp.logical_and(spot >= 1, back >= step - 1), spot + step - 1),
            ):
                q = jnp.clip(q, 0, count - 1)
                sends.append((can, remote(chunk(q), chunk(q), way, sign)))
            for way, sign, can, q in (
                (0, 1, spot >= step, spot - step),
                (1, -1, back >= step, spot + step),
            ):
                q = jnp.clip(q, 0, count - 1)
                receives.append((can, remote(chunk(q), chunk(q), way, sign), q, None))
        return sends, receives, chunk

    def work(name, stage, piece):
        if stage > 0:
            sends, receives, chunk = copies(name, stage - 1, piece)
            for can, copy, q, landed in receives:
                def finish():
                    copy().wait_recv()
                    if landed is not None:
                        block = chunk(q)
                        block[...] = block[...] + landed[...]
                guarded(can, finish)
        if stage == n_stages // 2:
            mine = bases[name][3]
            own = view(full, piece, mine, shard)
            own[...] = view(acc, piece % acc_slots, mine, shard)[...]
        if stage < n_stages:
            for can, copy in copies(name, stage, piece)[0]:
                guarded(can, lambda: copy().start())
        if stage == n_stages:
            for can, amount in sent_rows[name]:
                sent = landing.at[pl.ds(0, amount)]
                guarded(
                    can,
                    lambda: pltpu.make_async_copy(
                        sent, sent, send_sem.at[piece % SEM_SLOTS]
                    ).wait(),
                )

    starts = [0]
    for stage in range(n_stages):
        starts.append(starts[-1] + (END_LAG if stage in (0, n_stages - 1) else LAG))
    total_ticks = pieces + starts[-1]

    def run(meet):
        prime()
        vec[...] = jnp.zeros_like(vec)
        vec_copy.start()
        meet()

        def some_ticks(turn, carry):
            for spot_in in range(period):
                now = turn * period + spot_in
                for stage in range(n_stages + 1):
                    piece = now - starts[stage]
                    name = PATTERN[(spot_in - starts[stage]) % period]

                    @pl.when(jnp.logical_and(piece >= 0, piece < pieces))
                    def _():
                        at = jnp.clip(piece, 0, pieces - 1)
                        if stage == 0:
                            for sub in range(per_piece):
                                form(at, sub)
                        work(name, stage, at)

            return carry

        lax.fori_loop(0, -(-total_ticks // period), some_ticks, 0)

    return run


def sum_sizes(dp_size):
    dims = factor_dims(dp_size)
    rows = max(PIECE_ROWS, 16 * dp_size)
    land = max(stage_list(order, dims, rows)[1] for order in ORDERS.values())
    return dims, rows, -(-(UNITS + 1) * UNIT // rows), land, 2 * (sum(dims) - 3)


def sum_semaphores(ring, stages):
    return [
        pltpu.SemaphoreType.DMA((ring, 2)),
        pltpu.SemaphoreType.DMA,
        pltpu.SemaphoreType.DMA((SEM_SLOTS,)),
        pltpu.SemaphoreType.DMA((SEM_SLOTS, stages, 2)),
    ]


def reduce_kernel(dims, pieces, rows, left_hbm, right_hbm, vec_hbm, full, acc, landing, vec, left_ring,
                  right_ring, load_sem, vec_sem, send_sem, recv_sem):
    barrier = pltpu.get_barrier_semaphore()
    around = greet_axes(dims, barrier)
    slots = acc.shape[0] // rows
    run = summing(
        dims, pieces, rows, acc, slots, full, landing, slots, left_hbm, right_hbm, vec_hbm, vec,
        left_ring, right_ring, load_sem, vec_sem, send_sem, recv_sem,
    )
    run(lambda: pl.semaphore_wait(barrier, around))


def reduce_gradients(left, right, vec, dp_size):
    dims, rows, pieces, land, stages = sum_sizes(dp_size)
    ring = 4 if dp_size <= 16 else 2
    slots = min(SEM_SLOTS, pieces)
    return pl.pallas_call(
        partial(reduce_kernel, dims, pieces, rows),
        out_shape=pltpu.VMEM((pieces * rows, UNIT), jnp.bfloat16),
        in_specs=any_specs(3),
        out_specs=pl.BlockSpec(memory_space=pltpu.VMEM),
        scratch_shapes=[
            pltpu.VMEM((slots * rows, UNIT), jnp.bfloat16),
            pltpu.VMEM((slots * land, UNIT), jnp.bfloat16),
            pltpu.VMEM((rows, UNIT), jnp.float32),
            pltpu.VMEM((ring,) + left.shape[1:], jnp.bfloat16),
            pltpu.VMEM((ring,) + left.shape[1:], jnp.bfloat16),
        ]
        + sum_semaphores(ring, stages),
        compiler_params=pltpu.CompilerParams(
            collective_id=1, has_side_effects=True, vmem_limit_bytes=47 << 20
        ),
        name="reduce",
    )(left, right, vec)


CHUNK = 256
KEEP_A = {"slope": 0, "u1": 3072, "u2": 3840}
KEEP_A_WIDTH = 4608
STAT_A = {"rden": 0, "s1": 768, "s2": 896}
STAT_A_WIDTH = 1024
KEEP_B = {"q": 0, "k": 768, "sq": 1536, "sk": 2304, "v": 3072}
KEEP_B_WIDTH = 3840
VECTORS = {
    "bp": (0, 9), "bo": (9, 3), "g1": (12, 3), "h1": (15, 3), "bu": (18, 12), "bd": (30, 3), "g2": (33, 3),
    "h2": (36, 3),
}
TAIL_SCALE = 0.45
TAIL_POLY = (
    0.25396798653159114,
    0.25170428274474826,
    0.24846812412232888,
    0.08947906819608953,
    0.2922223682202733,
    -0.13585125317877522,
)


def dot(left_mat, right_mat):
    return jnp.dot(left_mat, right_mat, preferred_element_type=jnp.float32)


def inverse(value):
    rough = pl.reciprocal(value, approx=True)
    return rough * (2.0 - value * rough)


def gelu_pair(hidden):
    bell = jnp.exp2(hidden * hidden * (-0.5 * math.log2(math.e)))
    t = inverse(1.0 + (TAIL_SCALE * math.sqrt(0.5)) * jnp.abs(hidden))
    poly = jnp.full_like(t, 0.5 * TAIL_POLY[-1])
    for coefficient in TAIL_POLY[-2::-1]:
        poly = poly * t + 0.5 * coefficient
    tail = poly * t * bell
    below = jnp.where(hidden >= 0, 1.0 - tail, tail)
    return hidden * below, below + hidden * (bell * (1.0 / math.sqrt(2.0 * math.pi)))


def softplus_pair(value):
    small = jnp.exp(-jnp.abs(value))
    whole = 1.0 + small
    log_whole = jnp.where(
        small < 1e-2, small * (1.0 - small * (0.5 - small * (1.0 / 3.0))), jnp.log(whole)
    )
    return (
        jnp.maximum(value, 0.0) + log_whole,
        jnp.where(value >= 0, 1.0, small) * inverse(whole),
    )


def centred(rows):
    centre = rows - jnp.mean(rows, axis=-1, keepdims=True)
    scaling = lax.rsqrt(jnp.mean(centre * centre, axis=-1, keepdims=True) + EPSILON)
    return centre * scaling, scaling


def wide(column, width=128):
    return jnp.broadcast_to(column, (column.shape[0], width))


def first_half(rows):
    return lax.broadcasted_iota(jnp.int32, (rows, 128), 1) < 64


def row(ref):
    return ref[...].astype(jnp.float32)


def any_specs(count):
    return [pl.BlockSpec(memory_space=pl.ANY)] * count


def vmem_specs(count):
    return [pl.BlockSpec(memory_space=pltpu.VMEM)] * count


def norm_back(grad, unit_rows, scaling):
    mean_grad = jnp.mean(grad, axis=-1, keepdims=True)
    mean_cross = jnp.mean(grad * unit_rows, axis=-1, keepdims=True)
    return scaling * (grad - mean_grad - unit_rows * mean_cross)


def layers_kernel(chunks, *refs):
    (ends_hbm, wp_hbm, wo_hbm, wu_hbm, wd_hbm, bp, bo, g1, h1, bu, bd, g2, h2, mix) = refs[:14]
    left_hbm, right_hbm = refs[14:16]
    own_hbm, peer_hbm, peer_w_hbm = refs[16:20], refs[20:24], refs[24:28]
    res_hbm, vec_out = refs[28:30]
    (wp, wo, wu, wd, x_in, e_in, handed, left, right, keep_a, stat_a, keep_b, stat_b, rows_out, nums, dq,
     dk, dv, carry_k, carry_v, dn1, weighed, vec, vec_sent, vec_peer, gains, gains_peer, w_sem, x_sem, xo_sem, e_sem, left_sem,
     right_sem, load_sem, res_sem, send_f, recv_f, send_b, recv_b, send_w, recv_w, send_e, recv_e,
     send_k, recv_k, send_r, recv_r, send_v, recv_v, send_g, recv_g) = refs[30:]

    section = lax.axis_index("section")
    first = section == 0
    second = jnp.logical_not(first)
    partner = {"section": 1 - section}
    width = ends_hbm.shape[1]
    pairs = width // 128
    half = chunks // 2
    mats_hbm, mats = (wp_hbm, wo_hbm, wu_hbm, wd_hbm), (wp, wo, wu, wd)
    kept_bufs = (keep_a, stat_a, keep_b, stat_b)

    def w_copy(which, sources=mats_hbm):
        return pltpu.make_async_copy(sources[which], mats[which], w_sem.at[which])

    def remote(src, dst, send, recv):
        return pltpu.make_async_remote_copy(
            src_ref=src, dst_ref=dst, send_sem=send, recv_sem=recv, device_id=partner,
            device_id_type=MESH,
        )

    def w_push(which):
        return remote(mats_hbm[which], peer_w_hbm[which], send_w.at[which], recv_w.at[which])

    def rows_of(i):
        return pl.ds(pl.multiple_of(i * CHUNK, CHUNK), CHUNK)

    def x_copy(i):
        return pltpu.make_async_copy(ends_hbm.at[rows_of(i)], x_in.at[i], x_sem.at[i])

    def x_out_copies(i):
        return [
            pltpu.make_async_copy(
                x_in.at[i, :, n * UNIT : (n + 1) * UNIT], left_hbm.at[18 + n, i], xo_sem.at[i, n]
            )
            for n in range(3)
        ]

    def e_copy(i):
        return pltpu.make_async_copy(ends_hbm.at[rows_of(i)], e_in.at[i], e_sem.at[i])

    def e_push(i):
        return remote(ends_hbm.at[rows_of(i)], e_in.at[i], send_e.at[i], recv_e.at[i])

    def hand_on(i):
        return remote(handed.at[i], x_in.at[i], send_f.at[i], recv_f.at[i])

    def hand_back(i):
        return remote(handed.at[i], e_in.at[i], send_b.at[i], recv_b.at[i])

    def left_copy(i):
        return pltpu.make_async_copy(left, left_hbm.at[0:18, i], left_sem)

    spans = ((0, 15), (15, 18), (18, 27))

    def right_copy(i, n):
        start, end = spans[n]
        return pltpu.make_async_copy(
            right.at[start:end], right_hbm.at[start:end, i], right_sem.at[n]
        )

    def right_push(i, n):
        start, end = spans[n]
        return remote(
            right.at[start:end], right_hbm.at[start:end, i], send_r.at[n], recv_r.at[i, n]
        )

    def save(i, slot, n):
        return pltpu.make_async_copy(
            kept_bufs[n].at[slot], own_hbm[n].at[rows_of(i)], load_sem.at[slot, n]
        )

    def push(i, slot, n):
        return remote(
            kept_bufs[n].at[slot], peer_hbm[n].at[rows_of(i)], send_k.at[i, n], recv_k.at[i, n]
        )

    def load(i, slot, n, source):
        return pltpu.make_async_copy(
            source[n].at[rows_of(i)], kept_bufs[n].at[slot], load_sem.at[slot, n]
        )

    def res_copy(i):
        return pltpu.make_async_copy(rows_out, res_hbm.at[rows_of(i)], res_sem)

    def own_gains():
        gains[0:1, :] = row(g1)
        gains[1:2, :] = row(g2)

    def gains_push():
        return remote(gains, gains_peer, send_g, recv_g)

    def vec_push():
        return remote(vec_sent, vec_peer, send_v, recv_v)

    @pl.when(first)
    def _():
        x_copy(0).start()

    for which in range(4):
        w_copy(which).start()

    @pl.when(first)
    def _():
        for i in range(1, chunks):
            x_copy(i).start()

    @pl.when(second)
    def _():
        for i in range(half, chunks):
            e_copy(i).start()

    barrier = pltpu.get_barrier_semaphore()
    pl.semaphore_signal(barrier, inc=1, device_id=partner, device_id_type=MESH)
    vec[...] = jnp.zeros_like(vec)
    gains[...] = jnp.zeros_like(gains)
    own_gains()
    pl.semaphore_wait(barrier, 1)

    @pl.when(second)
    def _():
        gains_push().start()
        for i in range(half):
            e_push(i).start()
        for which in (3, 2, 1, 0):
            w_push(which).start()

    def weights_ready(i, which):
        @pl.when(i == 0)
        def _():
            w_copy(which).wait()

    lanes = lax.broadcasted_iota(jnp.int32, (CHUNK, 128), 1)
    low = lanes < 64

    def forward_chunk(i, carry):
        slot = lax.rem(i, 2)

        @pl.when(i >= 2)
        def _():
            @pl.when(first)
            def _():
                for n in range(4):
                    save(i - 2, slot, n).wait()

            @pl.when(second)
            def _():
                for n in range(4):
                    push(i - 2, slot, n).wait_send()

        weights_ready(i, 0)

        @pl.when(first)
        def _():
            x_copy(i).wait()

        @pl.when(second)
        def _():
            hand_on(i).wait_recv()

        for copy in x_out_copies(i):
            copy.start()
        now_a, now_b, old_b = keep_a.at[slot], keep_b.at[slot], keep_b.at[1 - slot]

        def keep(ref, start, value):
            ref[:, start : start + value.shape[1]] = value.astype(jnp.bfloat16)

        def blocks(first_block, value):
            for n in range(value.shape[1] // UNIT):
                left[first_block + n] = value[:, n * UNIT : (n + 1) * UNIT]

        x = x_in[i]
        for part, (name, slope) in enumerate((("q", "sq"), ("k", "sk"))):
            cols = slice(part * width, (part + 1) * width)
            soft, sigma = softplus_pair(dot(x, wp[:, cols]) + row(bp)[:, cols])
            keep(now_b, KEEP_B[name], soft)
            keep(now_b, KEEP_B[slope], sigma)
        cols = slice(2 * width, 3 * width)
        keep(now_b, KEEP_B["v"], dot(x, wp[:, cols]) + row(bp)[:, cols])

        def mix_pair(pair, source, table, fresh):
            def cut(ref, name):
                return ref[:, KEEP_B[name] + pair * 128 : KEEP_B[name] + (pair + 1) * 128]

            queries, keys_in, values = cut(now_b, "q"), cut(source, "k"), cut(source, "v")
            zero, one = jnp.zeros_like(keys_in), jnp.ones_like(values)
            for half in range(2):
                own = low if half == 0 else jnp.logical_not(low)
                scores = back_product(queries, jnp.where(own, keys_in, zero)) * table
                num = dot(scores.astype(jnp.bfloat16), jnp.where(own, values, one))
                at = 2 * pair + half
                nums[at] = num if fresh else nums[at] + num

        for pair in range(pairs):
            mix_pair(pair, now_b, mix[0], True)

        @pl.when(slot == 1)
        def _():
            for pair in range(pairs):
                mix_pair(pair, old_b, mix[1], False)

        @pl.when(i >= 1)
        def _():
            left_copy(i - 1).wait()

        for pair in range(pairs):
            num_a, num_b = nums[2 * pair], nums[2 * pair + 1]
            inv = inverse(
                jnp.where(low, pltpu.roll(num_a, 64, 1), pltpu.roll(num_b, 64, 1))
            )
            span = slice(pair * 128, (pair + 1) * 128)
            stat_b[slot, :, span] = jnp.where(low, num_a, num_b) * inv
            stat_a[slot, :, span] = inv
        mixed_low = stat_b[slot].astype(jnp.bfloat16)
        blocks(15, mixed_low)
        weights_ready(i, 1)
        first_sum = x.astype(jnp.float32) + row(bo) + dot(mixed_low, wo[...])

        @pl.when(jnp.logical_and(first, i == chunks - 1))
        def _():
            for which in (1, 0):
                w_push(which).wait_recv()
                w_copy(which, peer_w_hbm).start()

        unit_one, scale_one = centred(first_sum)
        keep(now_a, KEEP_A["u1"], unit_one)
        stat_a[slot, :, STAT_A["s1"] : STAT_A["s1"] + 128] = wide(scale_one)
        normed = unit_one * row(g1) + row(h1)
        resid = dn1
        resid[...] = normed + row(bd)
        up_in = normed.astype(jnp.bfloat16)
        blocks(12, up_in)
        weights_ready(i, 2)

        def hidden_of(n):
            cols = slice(n * width, (n + 1) * width)
            return dot(up_in, wu[:, cols]) + row(bu)[:, cols]

        hidden = hidden_of(0)
        for n in range(4):
            later = hidden_of(n + 1) if n < 3 else None
            active, slope = gelu_pair(hidden)
            active = active.astype(jnp.bfloat16)
            blocks(3 * n, active)
            keep(now_a, n * width, slope)
            if n == 0:
                weights_ready(i, 3)
            resid[...] += dot(active, wd[n * width : (n + 1) * width, :])
            hidden = later
        unit_two, scale_two = centred(resid[...])
        keep(now_a, KEEP_A["u2"], unit_two)
        stat_a[slot, :, STAT_A["s2"] : STAT_A["s2"] + 128] = wide(scale_two)
        result = unit_two * row(g2) + row(h2)

        @pl.when(first)
        def _():
            handed[i] = result.astype(jnp.bfloat16)
            hand_on(i).start()

        @pl.when(second)
        def _():
            @pl.when(i >= 1)
            def _():
                res_copy(i - 1).wait()

            rows_out[...] = result
            res_copy(i).start()

        left_copy(i).start()

        @pl.when(first)
        def _():
            for n in range(4):
                save(i, slot, n).start()

        @pl.when(jnp.logical_and(second, i < half))
        def _():
            for n in range(4):
                push(i, slot, n).start()

        return carry

    lax.fori_loop(0, chunks, forward_chunk, 0)
    @pl.when(first)
    def _():
        def fetch(i, some):
            for n in some:
                save(i + half, i, n).wait()
                push(i, i, n).wait_recv()
                load(i, i, n, peer_hbm).start()

        fetch(1, (0, 1))
        for which in (3, 2):
            w_push(which).wait_recv()
            w_copy(which, peer_w_hbm).start()
        fetch(1, (2, 3))
        fetch(0, (2, 3, 0, 1))
        for i in range(chunks):
            hand_on(i).wait_send()

    left_copy(chunks - 1).wait()
    for i in range(chunks):
        for copy in x_out_copies(i):
            copy.wait()

    @pl.when(second)
    def _():
        res_copy(chunks - 1).wait()
        for i in range(half):
            e_push(i).wait_send()
        gains_push().wait_send()
        for which in range(4):
            w_push(which).wait_send()

    def tally(name, start, values):
        total = jnp.sum(values.astype(jnp.float32), axis=0, keepdims=True)
        at = VECTORS[name][0] + start // UNIT
        for n in range(values.shape[1] // UNIT):
            vec[at + n : at + n + 1, :] += total[:, n * UNIT : (n + 1) * UNIT]

    def right_blocks(first_block, value):
        for n in range(value.shape[1] // UNIT):
            right[first_block + n] = value[:, n * UNIT : (n + 1) * UNIT]

    turns = jnp.where(first, chunks + half, half)

    def chunk_of(turn):
        late = jnp.where(first, turn >= chunks, True)
        return 1 - lax.rem(turn, 2) + jnp.where(late, half, 0)

    def loads(turn, some, action):
        for peers in (True, False):
            @pl.when((turn < half) if peers else (turn >= half))
            def _():
                i = chunk_of(turn)
                for n in some:
                    action(load(i, lax.rem(i, 2), n, peer_hbm if peers else own_hbm))

    def right_done(turn, n):
        i = chunk_of(turn)

        @pl.when(jnp.logical_and(first, turn < half))
        def _():
            right_push(i, n).wait_send()

        @pl.when(jnp.logical_not(jnp.logical_and(first, turn < half)))
        def _():
            right_copy(i, n).wait()

    def right_go(turn, n):
        i = chunk_of(turn)

        @pl.when(jnp.logical_and(first, turn < half))
        def _():
            right_push(i, n).start()

        @pl.when(jnp.logical_not(jnp.logical_and(first, turn < half)))
        def _():
            right_copy(i, n).start()

    def tail_part(turn, i):
        slot = lax.rem(i, 2)

        @pl.when(first)
        def _():
            loads(turn, (0, 1), lambda copy: copy.wait())

            @pl.when(turn < half)
            def _():
                e_push(i).wait_recv()

            @pl.when(turn == 0)
            def _():
                gains_push().wait_recv()
                gains[...] = gains_peer[...]

            @pl.when(turn == half)
            def _():
                own_gains()

            @pl.when(turn >= chunks)
            def _():
                hand_back(i).wait_recv()

        @pl.when(second)
        def _():
            e_copy(i).wait()

        @pl.when(turn >= 1)
        def _():
            for n in range(2):
                right_done(turn - 1, n)

        def ready(which):
            @pl.when(jnp.logical_and(first, jnp.logical_or(turn == 0, turn == half)))
            def _():
                w_copy(which).wait()

        now_a, total = keep_a.at[slot], dn1

        def kept(name, start=0):
            at = KEEP_A[name] + start
            return now_a[:, at : at + width].astype(jnp.float32)

        e = e_in[i].astype(jnp.float32)
        unit_two = kept("u2")
        tally("g2", 0, e * unit_two)
        tally("h2", 0, e)
        second_full = norm_back(
            e * gains[1:2, :], unit_two, stat_a[slot, :, STAT_A["s2"] : STAT_A["s2"] + 1]
        )
        second_low = second_full.astype(jnp.bfloat16)
        right_blocks(0, second_low)
        tally("bd", 0, second_low)
        total[...] = second_full

        ready(3)

        def pulled(n):
            return back_product(second_low, wd[n * width : (n + 1) * width, :])

        grad = pulled(0)
        for n in range(4):
            later = pulled(n + 1) if n < 3 else None
            hidden_low = (grad * kept("slope", n * width)).astype(jnp.bfloat16)
            right_blocks(3 + 3 * n, hidden_low)
            tally("bu", n * width, hidden_low)
            if n == 0:
                ready(2)
            total[...] += back_product(hidden_low, wu[:, n * width : (n + 1) * width])
            grad = later
        right_go(turn, 0)
        grad_normed = total[...]
        unit_one = kept("u1")
        tally("g1", 0, grad_normed * unit_one)
        tally("h1", 0, grad_normed)
        grad_first = norm_back(
            grad_normed * gains[0:1, :], unit_one, stat_a[slot, :, STAT_A["s1"] : STAT_A["s1"] + 1]
        )
        total[...] = grad_first
        first_low = grad_first.astype(jnp.bfloat16)
        right_blocks(15, first_low)
        right_go(turn, 1)
        tally("bo", 0, first_low)
        ready(1)
        grad_mixed = back_product(first_low, wo[...]).astype(jnp.bfloat16).astype(jnp.float32)
        weighed[...] = (grad_mixed * stat_a[slot, :, 0:width]).astype(jnp.bfloat16)

        @pl.when(first)
        def _():
            @pl.when(turn + 2 < turns)
            def _():
                loads(turn + 2, (0, 1), lambda copy: copy.start())

            @pl.when(turn == half - 1)
            def _():
                for which in (3, 2, 1):
                    w_copy(which).start()

    def pair_part(i, pair):
        slot = lax.rem(i, 2)
        now_b, old_b = keep_b.at[slot], keep_b.at[1 - slot]
        span = pl.ds(pl.multiple_of(pair * 128, 128), 128)

        def cut(ref, name):
            return ref[:, pl.ds(pl.multiple_of(KEEP_B[name] + pair * 128, 128), 128)]

        def half_block(source, table):
            queries, keys_in, values = cut(now_b, "q"), cut(source, "k"), cut(source, "v")
            w = weighed[:, span]
            cross = w.astype(jnp.float32) * stat_b[slot, :, span]
            zero, one = jnp.zeros_like(keys_in), jnp.ones_like(values)
            total_q, total_k, total_v = 0.0, 0.0, 0.0
            for half in range(2):
                own = low if half == 0 else jnp.logical_not(low)
                spare = 64 * (1 - half)
                inner = jnp.sum(jnp.where(own, cross, 0.0), axis=-1, keepdims=True)
                rough = inner.astype(jnp.bfloat16).astype(jnp.float32)
                extra = jnp.where(
                    lanes == spare, -rough, jnp.where(lanes == spare + 1, rough - inner, 0.0)
                ).astype(jnp.bfloat16)
                own_keys = jnp.where(own, keys_in, zero)
                scores = (back_product(queries, own_keys) * table).astype(jnp.bfloat16)
                grads = (
                    back_product(
                        jnp.where(own, w, extra), jnp.where(own, values, one)
                    )
                    * table
                ).astype(jnp.bfloat16)
                total_q += dot(grads, own_keys)
                total_k += rows_product(grads, jnp.where(own, queries, zero))
                total_v += rows_product(scores, jnp.where(own, w, zero))
            return total_q, total_k, total_v

        total_q, total_k, total_v = half_block(now_b, mix[0])
        dq[:, span] = total_q
        dk[:, span] = total_k
        dv[:, span] = total_v

        @pl.when(slot == 0)
        def _():
            dk[:, span] += carry_k[:, span]
            dv[:, span] += carry_v[:, span]

        @pl.when(slot == 1)
        def _():
            far_q, far_k, far_v = half_block(old_b, mix[1])
            dq[:, span] += far_q
            carry_k[:, span] = far_k
            carry_v[:, span] = far_v

    def head_part(turn, i):
        slot = lax.rem(i, 2)

        @pl.when(turn >= 1)
        def _():
            right_done(turn - 1, 2)

        @pl.when(jnp.logical_and(first, jnp.logical_or(turn == 0, turn == half)))
        def _():
            w_copy(0).wait()

        now_b = keep_b.at[slot]
        grad_in = dn1[...]
        for n, (source, slope) in enumerate(((dq, "sq"), (dk, "sk"), (dv, None))):
            values = source[...]
            if slope:
                at = KEEP_B[slope]
                values = values * now_b[:, at : at + width].astype(jnp.float32)
            values = values.astype(jnp.bfloat16)
            right_blocks(18 + 3 * n, values)
            tally("bp", n * width, values)
            grad_in += back_product(values, wp[:, n * width : (n + 1) * width])
        right_go(turn, 2)

        @pl.when(first)
        def _():
            @pl.when(turn < half)
            def _():
                e_in[i] = grad_in.astype(jnp.bfloat16)

            @pl.when(turn >= half)
            def _():
                @pl.when(turn > half)
                def _():
                    res_copy(chunk_of(turn - 1)).wait()

                rows_out[...] = grad_in
                res_copy(i).start()

            @pl.when(turn + 2 < turns)
            def _():
                loads(turn + 2, (2, 3), lambda copy: copy.start())

            @pl.when(turn == half - 1)
            def _():
                w_copy(0).start()
                vec_sent[...] = vec[...]
                vec_push().start()
                vec[...] = jnp.zeros_like(vec)

        @pl.when(second)
        def _():
            handed[i] = grad_in.astype(jnp.bfloat16)
            hand_back(i).start()

    def one_turn(turn, carry):
        i = chunk_of(turn)
        tail_part(turn, i)

        @pl.when(jnp.logical_and(first, lax.rem(turn, 2) == 0))
        def _():
            loads(turn, (2, 3), lambda copy: copy.wait())
            loads(turn + 1, (2, 3), lambda copy: copy.wait())

        def one_pair(pair, inner):
            pair_part(i, pair)
            return inner

        lax.fori_loop(0, pairs, one_pair, 0)
        head_part(turn, i)
        return carry

    lax.fori_loop(0, turns, one_turn, 0)
    for n in range(3):
        right_copy(half, n).wait()

    @pl.when(first)
    def _():
        res_copy(half).wait()
        vec_push().wait_send()

    @pl.when(second)
    def _():
        for i in range(half, chunks):
            hand_back(i).wait_send()
        vec_push().wait_recv()
        vec[...] += vec_peer[...]
        for i in range(half):
            for n in range(3):
                right_push(i, n).wait_recv()

    out_copy = pltpu.make_async_copy(vec, vec_out, w_sem.at[0])
    out_copy.start()
    out_copy.wait()


def run_layers(ends, mats, rows_in, mix):
    tokens, width = ends.shape
    chunks = tokens // CHUNK
    bf16, f32 = jnp.bfloat16, jnp.float32

    def kept(count):
        return [
            jax.ShapeDtypeStruct((count * CHUNK, columns), dtype)
            for columns, dtype in (
                (KEEP_A_WIDTH, bf16), (STAT_A_WIDTH, f32), (KEEP_B_WIDTH, bf16), (width, f32)
            )
        ]

    out_shape = (
        [
            jax.ShapeDtypeStruct((21, chunks, CHUNK, UNIT), bf16),
            jax.ShapeDtypeStruct((27, chunks, CHUNK, UNIT), bf16),
        ]
        + kept(chunks)
        + kept(chunks // 2)
        + [jax.ShapeDtypeStruct(mat.shape, mat.dtype) for mat in mats]
        + [
            jax.ShapeDtypeStruct((tokens, width), f32),
            jax.ShapeDtypeStruct((40, UNIT), f32),
        ]
    )
    chunk_f32 = pltpu.VMEM((CHUNK, width), f32)
    all_rows = pltpu.VMEM((chunks, CHUNK, width), bf16)
    dma = pltpu.SemaphoreType.DMA
    outs = pl.pallas_call(
        partial(layers_kernel, chunks),
        out_shape=out_shape,
        in_specs=any_specs(5) + vmem_specs(9),
        out_specs=any_specs(16),
        scratch_shapes=[pltpu.VMEM(mat.shape, mat.dtype) for mat in mats]
        + [
            all_rows,
            all_rows,
            all_rows,
            pltpu.VMEM((18, CHUNK, UNIT), bf16),
            pltpu.VMEM((27, CHUNK, UNIT), bf16),
            pltpu.VMEM((2, CHUNK, KEEP_A_WIDTH), bf16),
            pltpu.VMEM((2, CHUNK, STAT_A_WIDTH), f32),
            pltpu.VMEM((2, CHUNK, KEEP_B_WIDTH), bf16),
            pltpu.VMEM((2, CHUNK, width), f32),
            chunk_f32,
            pltpu.VMEM((HEADS, CHUNK, 128), f32),
            chunk_f32,
            chunk_f32,
            chunk_f32,
            chunk_f32,
            chunk_f32,
            chunk_f32,
            pltpu.VMEM((CHUNK, width), bf16),
            pltpu.VMEM((40, UNIT), f32),
            pltpu.VMEM((40, UNIT), f32),
            pltpu.VMEM((40, UNIT), f32),
            pltpu.VMEM((8, width), f32),
            pltpu.VMEM((8, width), f32),
            dma((4,)),
            dma((chunks,)),
            dma((chunks, 3)),
            dma((chunks,)),
            dma,
            dma((3,)),
            dma((2, 4)),
            dma,
            dma((chunks,)),
            dma((chunks,)),
            dma((chunks,)),
            dma((chunks,)),
            dma((4,)),
            dma((4,)),
            dma((chunks // 2,)),
            dma((chunks // 2,)),
            dma((chunks // 2, 4)),
            dma((chunks // 2, 4)),
            dma((3,)),
            dma((chunks // 2, 3)),
            dma,
            dma,
            dma,
            dma,
        ],
        compiler_params=pltpu.CompilerParams(
            collective_id=2, has_side_effects=True, vmem_limit_bytes=62 << 20
        ),
        name="layers",
    )(ends, *mats, *rows_in, mix)
    return outs[14], outs[0], outs[1], outs[15]


MATRICES = ((81, 9, 3), (72, 3, 3), (36, 12, 3), (0, 3, 12))


def widen_kernel(full, *refs):
    targets, vectors, held, out_sem = refs[:4], refs[4:12], refs[12:16], refs[16]
    copies, turn = [], 0
    for which, (begin, across, down) in enumerate(MATRICES):
        for block in range(down):
            span = pl.ds(block * UNIT, UNIT)
            copy = pltpu.make_async_copy(
                held[which].at[span], targets[which].at[0, span], out_sem.at[turn]
            )

            def one(n, carry):
                start = pl.multiple_of((begin + block * across + n) * UNIT, UNIT)
                held[which][span, pl.ds(pl.multiple_of(n * UNIT, UNIT), UNIT)] = full[
                    pl.ds(start, UNIT), :
                ].astype(jnp.float32)
                return carry

            lax.fori_loop(0, across, one, 0)
            copy.start()
            copies.append(copy)
            turn += 1
    for (start, count), vector in zip(VECTORS.values(), vectors):
        for n in range(count):
            at = UNITS * UNIT + start + n
            vector[:, n * UNIT : (n + 1) * UNIT] = full[at : at + 1, :].astype(jnp.float32)
    for copy in copies:
        copy.wait()


def widen(full):
    shapes = [(down * UNIT, across * UNIT) for _, across, down in MATRICES]
    return pl.pallas_call(
        widen_kernel,
        out_shape=[jax.ShapeDtypeStruct((1,) + shape, jnp.float32) for shape in shapes]
        + [jax.ShapeDtypeStruct((1, count * UNIT), jnp.float32) for _, count in VECTORS.values()],
        in_specs=[pl.BlockSpec(memory_space=pltpu.VMEM)],
        out_specs=any_specs(4) + vmem_specs(8),
        scratch_shapes=[pltpu.VMEM(shape, jnp.float32) for shape in shapes]
        + [pltpu.SemaphoreType.DMA((sum(down for _, _, down in MATRICES),))],
        compiler_params=pltpu.CompilerParams(vmem_limit_bytes=36 << 20),
        name="widen",
    )(full)


def mix_tables(length):
    places = jnp.arange(2 * CHUNK, dtype=jnp.int32)
    angles = places.astype(jnp.float32) * ((0.5 * math.pi) / length.astype(jnp.float32))
    cosine, sine, document = lax.optimization_barrier(
        (jnp.cos(angles), jnp.sin(angles), places // length)
    )

    def table(start):
        later, earlier = slice(start, start + CHUNK), slice(0, CHUNK)
        seen = jnp.logical_and(
            document[later, None] == document[None, earlier],
            places[later, None] >= places[None, earlier],
        )
        near = cosine[later, None] * cosine[None, earlier] + sine[later, None] * sine[None, earlier]
        return jnp.where(seen, near, 0.0)

    return jnp.stack([table(0), table(CHUNK)])


def shards(
    endpoints,
    projection,
    projection_bias,
    output_weight,
    output_bias,
    first_gain,
    first_shift,
    up_weight,
    up_bias,
    down_weight,
    down_bias,
    second_gain,
    second_shift,
    segment_length,
):
    dp_size = lax.axis_size("dp")
    mats = (projection[0], output_weight[0], up_weight[0], down_weight[0])
    rows = (
        projection_bias, output_bias, first_gain, first_shift, up_bias, down_bias, second_gain,
        second_shift,
    )
    mix = mix_tables(segment_length[0])
    results, left, right, vec = run_layers(endpoints[0], mats, rows, mix)
    full = reduce_gradients(left, right, vec, dp_size)
    proj, out, up, down, bp, bo, g1, h1, bu, bd, g2, h2 = widen(full)
    return (results[None], proj, bp, out, bo, g1, h1, up, bu, down, bd, g2, h2)


def solution(mesh):
    in_specs = (
        P("section", "dp", None),
        P("section", None, None),
        P("section", None),
        P("section", None, None),
        P("section", None),
        P("section", None),
        P("section", None),
        P("section", None, None),
        P("section", None),
        P("section", None, None),
        P("section", None),
        P("section", None),
        P("section", None),
        P("dp"),
    )
    out_specs = (
        P("section", "dp", None),
        P("section", None, None),
        P("section", None),
        P("section", None, None),
        P("section", None),
        P("section", None),
        P("section", None),
        P("section", None, None),
        P("section", None),
        P("section", None, None),
        P("section", None),
        P("section", None),
        P("section", None),
    )
    return jax.shard_map(shards, mesh=mesh, in_specs=in_specs, out_specs=out_specs, check_vma=False)
```

```python
from functools import partial
import math

import jax
import jax.numpy as jnp
from jax import lax
from jax.experimental import pallas as pl
from jax.experimental.pallas import tpu as pltpu
from jax.sharding import PartitionSpec as P

HEADS = 12
EPSILON = 1e-05
MESH = pl.DeviceIdType.MESH


def rows_product(left_mat, right_mat):
    return lax.dot_general(
        left_mat, right_mat, (((0,), (0,)), ((), ())), preferred_element_type=jnp.float32
    )


def back_product(grad_mat, weight_mat):
    return lax.dot_general(
        grad_mat, weight_mat, (((1,), (1,)), ((), ())), preferred_element_type=jnp.float32
    )


def factor_dims(count):
    bits = count.bit_length() - 1
    return (1 << (bits // 3), 1 << ((bits + 1) // 3), 1 << ((bits + 2) // 3))


ORDERS = {"a": (0, 1, 2), "b": (1, 2, 0), "c": (2, 0, 1)}
PATTERN = "abacabc"
LAG = 3
END_LAG = 4
UNIT = 256
UNITS = 108
PIECE_ROWS = 512
SEM_SLOTS = 35


def stage_list(order, dims, rows):
    stages, size, landing = [], rows, 0
    for level, ax in enumerate(order):
        part = size // dims[ax]
        for step in range(1, dims[ax]):
            stages.append(("reduce", level, ax, step, part, landing))
            landing += part if dims[ax] == 2 else 2 * part
        size = part
    for level in reversed(range(3)):
        ax = order[level]
        for step in range(1, dims[ax]):
            stages.append(("gather", level, ax, step, size, 0))
        size *= dims[ax]
    return stages, landing


def unit_blocks(unit):
    up, out, proj = unit - 36, unit - 72, unit - 81
    left = jnp.where(
        unit < 36,
        unit // 3,
        jnp.where(unit < 72, 12 + up // 12, jnp.where(unit < 81, 15 + out // 3, 18 + proj // 9)),
    )
    right = jnp.where(
        unit < 36,
        unit % 3,
        jnp.where(unit < 72, 3 + up % 12, jnp.where(unit < 81, 15 + out % 3, 18 + proj % 9)),
    )
    return left, right


def axis_places(dims):
    here = lax.axis_index("dp")
    strides = (1, dims[0], dims[0] * dims[1])
    return here, strides, [(here // strides[ax]) % dims[ax] for ax in range(3)]


def greet_axes(dims, semaphore):
    here, strides, place = axis_places(dims)
    around = 0
    for ax in range(3):
        for sign, can in ((1, place[ax] < dims[ax] - 1), (-1, place[ax] > 0)):
            @pl.when(can)
            def _():
                pl.semaphore_signal(
                    semaphore, inc=1, device_id={"dp": here + sign * strides[ax]},
                    device_id_type=MESH,
                )
            around = around + can.astype(jnp.int32)
    return around


def gather_sends(spot, count):
    found = {}
    for at in range(count):
        sent = (at + 1 if at < count - 1 else 0) + (count - at if at > 0 else 0)
        found.setdefault(sent, []).append(spot == at)
    options = []
    for sent, spots in found.items():
        can = spots[0]
        for other in spots[1:]:
            can = jnp.logical_or(can, other)
        options.append((can, sent))
    return options


def guarded(can, action):
    if can is None:
        action()
    else:
        pl.when(can)(action)


def summing(dims, pieces, rows, acc, acc_slots, full, landing, land_slots, left_hbm,
            right_hbm, vec_hbm, vec, left_ring, right_ring, load_sem, vec_sem, send_sem, recv_sem):
    here, strides, place = axis_places(dims)
    ring, chunks = left_ring.shape[0], left_ring.shape[1]
    per_piece = rows // UNIT
    land_rows = landing.shape[0] // land_slots
    plans = {name: stage_list(order, dims, rows)[0] for name, order in ORDERS.items()}
    n_stages = len(plans["a"])
    shard = rows // (dims[0] * dims[1] * dims[2])
    period = len(PATTERN)

    bases = {}
    for name, order in ORDERS.items():
        base, size, found = 0, rows, []
        for ax in order:
            found.append(base)
            size = size // dims[ax]
            base = base + place[ax] * size
        bases[name] = found + [base]

    sent_rows = {}
    for name, plan in plans.items():
        sure, options = 0, [(None, 0)]
        for kind, _, ax, step, part, _ in plan:
            if dims[ax] == 2 or kind == "reduce":
                sure += part
            elif step == 1:
                options = [
                    (can if other is None else jnp.logical_and(can, other), more + part * count)
                    for other, more in options
                    for can, count in gather_sends(place[ax], dims[ax])
                ]
        sent_rows[name] = [(can, sure + more) for can, more in options]

    def view(ref, slot, start, size):
        across = ref.shape[1] // UNIT
        first = pl.multiple_of(slot // across * rows + start, 16)
        if across == 1:
            return ref.at[pl.ds(first, size)]
        return ref.at[pl.ds(first, size), pl.ds(pl.multiple_of(slot % across * UNIT, UNIT), UNIT)]

    def loads(unit):
        slot = unit % ring
        left, right = unit_blocks(unit)
        return (
            pltpu.make_async_copy(left_hbm.at[left], left_ring.at[slot], load_sem.at[slot, 0]),
            pltpu.make_async_copy(right_hbm.at[right], right_ring.at[slot], load_sem.at[slot, 1]),
        )

    def prime():
        for unit in range(ring):
            for copy in loads(jnp.int32(unit)):
                copy.start()

    vec_copy = pltpu.make_async_copy(vec_hbm, vec.at[pl.ds(0, vec_hbm.shape[0])], vec_sem)

    def form(piece, sub):
        unit = piece * per_piece + sub
        target = view(acc, piece % acc_slots, sub * UNIT, UNIT)

        @pl.when(unit < UNITS)
        def _():
            for copy in loads(unit):
                copy.wait()
            slot = unit % ring
            tokens = chunks * left_ring.shape[2]
            target[...] = rows_product(
                left_ring[slot].reshape(tokens, UNIT), right_ring[slot].reshape(tokens, UNIT)
            ).astype(jnp.bfloat16)

            @pl.when(unit + ring < UNITS)
            def _():
                for copy in loads(unit + ring):
                    copy.start()

        @pl.when(unit >= UNITS)
        def _():
            if sub == 0:
                vec_copy.wait()
            target[...] = vec[sub * UNIT : (sub + 1) * UNIT, :].astype(jnp.bfloat16)

    def copies(name, stage, piece):
        kind, level, ax, step, part, land = plans[name][stage]
        count, spot = dims[ax], place[ax]
        slot = piece % SEM_SLOTS
        held, index = (acc, piece % acc_slots) if kind == "reduce" else (full, piece)
        land_start = piece % land_slots * land_rows + land

        def chunk(q):
            return view(held, index, bases[name][level] + q * part, part)

        def landed(way):
            return landing.at[pl.ds(pl.multiple_of(land_start + way * part, 16), part)]

        def remote(src, dst, way, sign):
            return lambda: pltpu.make_async_remote_copy(
                src_ref=src, dst_ref=dst, send_sem=send_sem.at[slot],
                recv_sem=recv_sem.at[slot, stage, way],
                device_id={"dp": here + sign * strides[ax]}, device_id_type=MESH,
            )

        sends, receives = [], []
        if count == 2:
            sign = 1 - 2 * spot
            mine, other = spot, 1 - spot
            if kind == "reduce":
                sends.append((None, remote(chunk(other), landed(0), 0, sign)))
                receives.append((None, remote(chunk(mine), landed(0), 0, sign), mine, landed(0)))
            else:
                sends.append((None, remote(chunk(mine), chunk(mine), 0, sign)))
                receives.append((None, remote(chunk(other), chunk(other), 0, sign), other, None))
            return sends, receives, chunk
        back = count - 1 - spot
        if kind == "reduce":
            for way, sign, can, q in (
                (0, 1, spot < step, spot + count - step),
                (1, -1, back < step, step - 1 - back),
            ):
                q = jnp.clip(q, 0, count - 1)
                sends.append((can, remote(chunk(q), landed(way), way, sign)))
            for way, sign, can, q in (
                (0, 1, jnp.logical_and(spot >= 1, spot - 1 < step), spot - 1 + count - step),
                (1, -1, jnp.logical_and(back >= 1, back - 1 < step), step - back),
            ):
                q = jnp.clip(q, 0, count - 1)
                receives.append((can, remote(chunk(q), landed(way), way, sign), q, landed(way)))
        else:
            for way, sign, can, q in (
                (0, 1, jnp.logical_and(back >= 1, spot >= step - 1), spot - step + 1),
                (1, -1, jnp.logical_and(spot >= 1, back >= step - 1), spot + step - 1),
            ):
                q = jnp.clip(q, 0, count - 1)
                sends.append((can, remote(chunk(q), chunk(q), way, sign)))
            for way, sign, can, q in (
                (0, 1, spot >= step, spot - step),
                (1, -1, back >= step, spot + step),
            ):
                q = jnp.clip(q, 0, count - 1)
                receives.append((can, remote(chunk(q), chunk(q), way, sign), q, None))
        return sends, receives, chunk

    def work(name, stage, piece):
        if stage > 0:
            sends, receives, chunk = copies(name, stage - 1, piece)
            for can, copy, q, landed in receives:
                def finish():
                    copy().wait_recv()
                    if landed is not None:
                        block = chunk(q)
                        block[...] = block[...] + landed[...]
                guarded(can, finish)
        if stage == n_stages // 2:
            mine = bases[name][3]
            own = view(full, piece, mine, shard)
            own[...] = view(acc, piece % acc_slots, mine, shard)[...]
        if stage < n_stages:
            for can, copy in copies(name, stage, piece)[0]:
                guarded(can, lambda: copy().start())
        if stage == n_stages:
            for can, amount in sent_rows[name]:
                sent = landing.at[pl.ds(0, amount)]
                guarded(
                    can,
                    lambda: pltpu.make_async_copy(
                        sent, sent, send_sem.at[piece % SEM_SLOTS]
                    ).wait(),
                )

    starts = [0]
    for stage in range(n_stages):
        starts.append(starts[-1] + (END_LAG if stage in (0, n_stages - 1) else LAG))
    total_ticks = pieces + starts[-1]

    def run(meet):
        prime()
        vec[...] = jnp.zeros_like(vec)
        vec_copy.start()
        meet()

        def some_ticks(turn, carry):
            for spot_in in range(period):
                now = turn * period + spot_in
                for stage in range(n_stages + 1):
                    piece = now - starts[stage]
                    name = PATTERN[(spot_in - starts[stage]) % period]

                    @pl.when(jnp.logical_and(piece >= 0, piece < pieces))
                    def _():
                        at = jnp.clip(piece, 0, pieces - 1)
                        if stage == 0:
                            for sub in range(per_piece):
                                form(at, sub)
                        work(name, stage, at)

            return carry

        lax.fori_loop(0, -(-total_ticks // period), some_ticks, 0)

    return run


def sum_sizes(dp_size):
    dims = factor_dims(dp_size)
    rows = max(PIECE_ROWS, 16 * dp_size)
    land = max(stage_list(order, dims, rows)[1] for order in ORDERS.values())
    return dims, rows, -(-(UNITS + 1) * UNIT // rows), land, 2 * (sum(dims) - 3)


def sum_semaphores(ring, stages):
    return [
        pltpu.SemaphoreType.DMA((ring, 2)),
        pltpu.SemaphoreType.DMA,
        pltpu.SemaphoreType.DMA((SEM_SLOTS,)),
        pltpu.SemaphoreType.DMA((SEM_SLOTS, stages, 2)),
    ]


def reduce_kernel(dims, pieces, rows, left_hbm, right_hbm, vec_hbm, full, acc, landing, vec, left_ring,
                  right_ring, load_sem, vec_sem, send_sem, recv_sem):
    barrier = pltpu.get_barrier_semaphore()
    around = greet_axes(dims, barrier)
    slots = acc.shape[0] // rows
    run = summing(
        dims, pieces, rows, acc, slots, full, landing, slots, left_hbm, right_hbm, vec_hbm, vec,
        left_ring, right_ring, load_sem, vec_sem, send_sem, recv_sem,
    )
    run(lambda: pl.semaphore_wait(barrier, around))


def reduce_gradients(left, right, vec, dp_size):
    dims, rows, pieces, land, stages = sum_sizes(dp_size)
    ring = 4 if dp_size <= 16 else 2
    slots = min(SEM_SLOTS, pieces)
    return pl.pallas_call(
        partial(reduce_kernel, dims, pieces, rows),
        out_shape=pltpu.VMEM((pieces * rows, UNIT), jnp.bfloat16),
        in_specs=any_specs(3),
        out_specs=pl.BlockSpec(memory_space=pltpu.VMEM),
        scratch_shapes=[
            pltpu.VMEM((slots * rows, UNIT), jnp.bfloat16),
            pltpu.VMEM((slots * land, UNIT), jnp.bfloat16),
            pltpu.VMEM((rows, UNIT), jnp.float32),
            pltpu.VMEM((ring,) + left.shape[1:], jnp.bfloat16),
            pltpu.VMEM((ring,) + left.shape[1:], jnp.bfloat16),
        ]
        + sum_semaphores(ring, stages),
        compiler_params=pltpu.CompilerParams(
            collective_id=1, has_side_effects=True, vmem_limit_bytes=47 << 20
        ),
        name="reduce",
    )(left, right, vec)


CHUNK = 256
KEEP_A = {"slope": 0, "u1": 3072, "u2": 3840}
KEEP_A_WIDTH = 4608
STAT_A = {"rden": 0, "s1": 768, "s2": 896}
STAT_A_WIDTH = 1024
KEEP_B = {"q": 0, "k": 768, "sq": 1536, "sk": 2304, "v": 3072}
KEEP_B_WIDTH = 3840
VECTORS = {
    "bp": (0, 9), "bo": (9, 3), "g1": (12, 3), "h1": (15, 3), "bu": (18, 12), "bd": (30, 3), "g2": (33, 3),
    "h2": (36, 3),
}
TAIL_SCALE = 0.45
TAIL_POLY = (
    0.25396798653159114,
    0.25170428274474826,
    0.24846812412232888,
    0.08947906819608953,
    0.2922223682202733,
    -0.13585125317877522,
)


def dot(left_mat, right_mat):
    return jnp.dot(left_mat, right_mat, preferred_element_type=jnp.float32)


def inverse(value):
    return pl.reciprocal(value, approx=True)


def gelu_pair(hidden):
    bell = jnp.exp2(hidden * hidden * (-0.5 * math.log2(math.e)))
    t = inverse(1.0 + (TAIL_SCALE * math.sqrt(0.5)) * jnp.abs(hidden))
    poly = jnp.full_like(t, 0.5 * TAIL_POLY[-1])
    for coefficient in TAIL_POLY[-2::-1]:
        poly = poly * t + 0.5 * coefficient
    tail = poly * t * bell
    below = jnp.where(hidden >= 0, 1.0 - tail, tail)
    return hidden * below, below + hidden * (bell * (1.0 / math.sqrt(2.0 * math.pi)))


def softplus_pair(value):
    small = jnp.exp2(jnp.abs(value) * -math.log2(math.e))
    whole = 1.0 + small
    log_whole = jnp.where(small < 2e-3, small * (1.0 - 0.5 * small), jnp.log(whole))
    return (
        jnp.maximum(value, 0.0) + log_whole,
        jnp.where(value >= 0, 1.0, small) * inverse(whole),
    )


def centred(rows):
    centre = rows - jnp.mean(rows, axis=-1, keepdims=True)
    scaling = lax.rsqrt(jnp.mean(centre * centre, axis=-1, keepdims=True) + EPSILON)
    return centre * scaling, scaling


def wide(column, width=128):
    return jnp.broadcast_to(column, (column.shape[0], width))


def first_half(rows):
    return lax.broadcasted_iota(jnp.int32, (rows, 128), 1) < 64


def row(ref):
    return ref[...].astype(jnp.float32)


def any_specs(count):
    return [pl.BlockSpec(memory_space=pl.ANY)] * count


def vmem_specs(count):
    return [pl.BlockSpec(memory_space=pltpu.VMEM)] * count


def norm_back(grad, unit_rows, scaling):
    mean_grad = jnp.mean(grad, axis=-1, keepdims=True)
    mean_cross = jnp.mean(grad * unit_rows, axis=-1, keepdims=True)
    return scaling * (grad - mean_grad - unit_rows * mean_cross)


def layers_kernel(chunks, *refs):
    (ends_hbm, wp_hbm, wo_hbm, wu_hbm, wd_hbm, bp, bo, g1, h1, bu, bd, g2, h2, mix) = refs[:14]
    left_hbm, right_hbm = refs[14:16]
    own_hbm, peer_hbm, peer_w_hbm = refs[16:20], refs[20:24], refs[24:28]
    res_hbm, vec_out = refs[28:30]
    (wp, wo, wu, wd, x_in, e_in, handed, left, right, keep_a, stat_a, keep_b, stat_b, rows_out, nums, dq,
     dk, dv, carry_k, carry_v, dn1, weighed, vec, vec_sent, vec_peer, gains, gains_peer, cut_in, rest_in, rest, w_sem, x_sem, xo_sem, e_sem, left_sem,
     right_sem, load_sem, res_sem, send_f, recv_f, send_b, recv_b, send_w, recv_w, send_e, recv_e,
     send_k, recv_k, send_r, recv_r, send_v, recv_v, send_g, recv_g) = refs[30:]

    section = lax.axis_index("section")
    first = section == 0
    second = jnp.logical_not(first)
    partner = {"section": 1 - section}
    width = ends_hbm.shape[1]
    pairs = width // 128
    half = chunks // 2
    mats_hbm, mats = (wp_hbm, wo_hbm, wu_hbm, wd_hbm), (wp, wo, wu, wd)
    kept_bufs = (keep_a, stat_a, keep_b, stat_b)

    def w_copy(which, sources=mats_hbm):
        return pltpu.make_async_copy(sources[which], mats[which], w_sem.at[which])

    def remote(src, dst, send, recv):
        return pltpu.make_async_remote_copy(
            src_ref=src, dst_ref=dst, send_sem=send, recv_sem=recv, device_id=partner,
            device_id_type=MESH,
        )

    def w_push(which):
        return remote(mats_hbm[which], peer_w_hbm[which], send_w.at[which], recv_w.at[which])

    def rows_of(i):
        return pl.ds(pl.multiple_of(i * CHUNK, CHUNK), CHUNK)

    def x_copy(i):
        return pltpu.make_async_copy(ends_hbm.at[rows_of(i)], x_in.at[i], x_sem.at[i])

    def x_out_copies(i):
        return [
            pltpu.make_async_copy(
                x_in.at[i, :, n * UNIT : (n + 1) * UNIT], left_hbm.at[18 + n, i], xo_sem.at[i, n]
            )
            for n in range(3)
        ]

    def e_copy(i):
        return pltpu.make_async_copy(ends_hbm.at[rows_of(i)], e_in.at[i], e_sem.at[i])

    def e_push(i):
        return remote(ends_hbm.at[rows_of(i)], e_in.at[i], send_e.at[i], recv_e.at[i])

    def hand_on(i):
        return remote(handed.at[i], x_in.at[i], send_f.at[i], recv_f.at[i])

    def hand_back(i):
        at = i - half
        return [
            remote(
                right.at[18 + 3 * n : 21 + 3 * n], cut_in.at[at, 3 * n : 3 * n + 3],
                send_b.at[at, n], recv_b.at[at, n],
            )
            for n in range(3)
        ] + [remote(rest.at[at], rest_in.at[at], send_b.at[at, 3], recv_b.at[at, 3])]

    def left_copy(i):
        return pltpu.make_async_copy(left, left_hbm.at[0:18, i], left_sem)

    spans = ((0, 15), (15, 18), (18, 27))

    def right_copy(i, n):
        start, end = spans[n]
        return pltpu.make_async_copy(
            right.at[start:end], right_hbm.at[start:end, i], right_sem.at[n]
        )

    def right_push(i, n):
        start, end = spans[n]
        return remote(
            right.at[start:end], right_hbm.at[start:end, i], send_r.at[n], recv_r.at[i, n]
        )

    def save(i, slot, n):
        return pltpu.make_async_copy(
            kept_bufs[n].at[slot], own_hbm[n].at[rows_of(i)], load_sem.at[slot, n]
        )

    def push(i, slot, n):
        return remote(
            kept_bufs[n].at[slot], peer_hbm[n].at[rows_of(i)], send_k.at[i, n], recv_k.at[i, n]
        )

    def load(i, slot, n, source):
        return pltpu.make_async_copy(
            source[n].at[rows_of(i)], kept_bufs[n].at[slot], load_sem.at[slot, n]
        )

    def res_copy(i):
        return pltpu.make_async_copy(rows_out, res_hbm.at[rows_of(i)], res_sem)

    def own_gains():
        gains[0:1, :] = row(g1)
        gains[1:2, :] = row(g2)

    def gains_push():
        return remote(gains, gains_peer, send_g, recv_g)

    def vec_push():
        return remote(vec_sent, vec_peer, send_v, recv_v)

    @pl.when(first)
    def _():
        x_copy(0).start()

    for which in range(4):
        w_copy(which).start()

    @pl.when(first)
    def _():
        for i in range(1, chunks):
            x_copy(i).start()

    @pl.when(second)
    def _():
        for i in range(half, chunks):
            e_copy(i).start()

    barrier = pltpu.get_barrier_semaphore()
    pl.semaphore_signal(barrier, inc=1, device_id=partner, device_id_type=MESH)
    vec[...] = jnp.zeros_like(vec)
    gains[...] = jnp.zeros_like(gains)
    own_gains()
    pl.semaphore_wait(barrier, 1)

    @pl.when(second)
    def _():
        gains_push().start()
        for i in range(half):
            e_push(i).start()
        for which in (3, 2, 1, 0):
            w_push(which).start()

    def weights_ready(i, which):
        @pl.when(i == 0)
        def _():
            w_copy(which).wait()

    lanes = lax.broadcasted_iota(jnp.int32, (CHUNK, 128), 1)
    low = lanes < 64

    def forward_chunk(i, carry):
        slot = lax.rem(i, 2)

        @pl.when(i >= 2)
        def _():
            @pl.when(first)
            def _():
                for n in range(4):
                    save(i - 2, slot, n).wait()

            @pl.when(second)
            def _():
                for n in range(4):
                    push(i - 2, slot, n).wait_send()

        weights_ready(i, 0)

        @pl.when(first)
        def _():
            x_copy(i).wait()

        @pl.when(second)
        def _():
            hand_on(i).wait_recv()

        for copy in x_out_copies(i):
            copy.start()
        now_a, now_b, old_b = keep_a.at[slot], keep_b.at[slot], keep_b.at[1 - slot]

        def keep(ref, start, value):
            ref[:, start : start + value.shape[1]] = value.astype(jnp.bfloat16)

        def blocks(first_block, value):
            for n in range(value.shape[1] // UNIT):
                left[first_block + n] = value[:, n * UNIT : (n + 1) * UNIT]

        x = x_in[i]
        for part, (name, slope) in enumerate((("q", "sq"), ("k", "sk"))):
            cols = slice(part * width, (part + 1) * width)
            soft, sigma = softplus_pair(dot(x, wp[:, cols]) + row(bp)[:, cols])
            keep(now_b, KEEP_B[name], soft)
            keep(now_b, KEEP_B[slope], sigma)
        cols = slice(2 * width, 3 * width)
        keep(now_b, KEEP_B["v"], dot(x, wp[:, cols]) + row(bp)[:, cols])

        def mix_pair(pair, source, table, fresh):
            def cut(ref, name):
                return ref[:, KEEP_B[name] + pair * 128 : KEEP_B[name] + (pair + 1) * 128]

            queries, keys_in, values = cut(now_b, "q"), cut(source, "k"), cut(source, "v")
            zero, one = jnp.zeros_like(keys_in), jnp.ones_like(values)
            for half in range(2):
                own = low if half == 0 else jnp.logical_not(low)
                scores = back_product(queries, jnp.where(own, keys_in, zero)) * table
                num = dot(scores.astype(jnp.bfloat16), jnp.where(own, values, one))
                at = 2 * pair + half
                nums[at] = num if fresh else nums[at] + num

        for pair in range(pairs):
            mix_pair(pair, now_b, mix[0], True)

        @pl.when(slot == 1)
        def _():
            for pair in range(pairs):
                mix_pair(pair, old_b, mix[1], False)

        @pl.when(i >= 1)
        def _():
            left_copy(i - 1).wait()

        for pair in range(pairs):
            num_a, num_b = nums[2 * pair], nums[2 * pair + 1]
            inv = inverse(
                jnp.where(low, pltpu.roll(num_a, 64, 1), pltpu.roll(num_b, 64, 1))
            )
            span = slice(pair * 128, (pair + 1) * 128)
            stat_b[slot, :, span] = jnp.where(low, num_a, num_b) * inv
            stat_a[slot, :, span] = inv
        mixed_low = stat_b[slot].astype(jnp.bfloat16)
        blocks(15, mixed_low)
        weights_ready(i, 1)
        first_sum = x.astype(jnp.float32) + row(bo) + dot(mixed_low, wo[...])

        @pl.when(jnp.logical_and(first, i == chunks - 1))
        def _():
            for which in (1, 0):
                w_push(which).wait_recv()
                w_copy(which, peer_w_hbm).start()

        unit_one, scale_one = centred(first_sum)
        keep(now_a, KEEP_A["u1"], unit_one)
        stat_a[slot, :, STAT_A["s1"] : STAT_A["s1"] + 128] = wide(scale_one)
        normed = unit_one * row(g1) + row(h1)
        resid = dn1
        resid[...] = normed + row(bd)
        up_in = normed.astype(jnp.bfloat16)
        blocks(12, up_in)
        weights_ready(i, 2)

        def hidden_of(n):
            cols = slice(n * width, (n + 1) * width)
            return dot(up_in, wu[:, cols]) + row(bu)[:, cols]

        hidden = hidden_of(0)
        for n in range(4):
            later = hidden_of(n + 1) if n < 3 else None
            active, slope = gelu_pair(hidden)
            active = active.astype(jnp.bfloat16)
            blocks(3 * n, active)
            keep(now_a, n * width, slope)
            if n == 0:
                weights_ready(i, 3)
            resid[...] += dot(active, wd[n * width : (n + 1) * width, :])
            hidden = later

            @pl.when(jnp.logical_and(first, i == chunks - 1))
            def _():
                if n == 0:
                    w_push(3).wait_recv()
                    w_push(2).wait_recv()
                quarter = pl.ds(n * width, width)
                pltpu.make_async_copy(
                    peer_w_hbm[3].at[quarter], wd.at[quarter], w_sem.at[3]
                ).start()
                pltpu.make_async_copy(
                    peer_w_hbm[2].at[:, quarter], wu.at[:, quarter], w_sem.at[2]
                ).start()
        unit_two, scale_two = centred(resid[...])
        keep(now_a, KEEP_A["u2"], unit_two)
        stat_a[slot, :, STAT_A["s2"] : STAT_A["s2"] + 128] = wide(scale_two)
        result = unit_two * row(g2) + row(h2)

        @pl.when(first)
        def _():
            handed[i] = result.astype(jnp.bfloat16)
            hand_on(i).start()

        @pl.when(second)
        def _():
            @pl.when(i >= 1)
            def _():
                res_copy(i - 1).wait()

            rows_out[...] = result
            res_copy(i).start()

        left_copy(i).start()

        @pl.when(first)
        def _():
            for n in range(4):
                save(i, slot, n).start()

        @pl.when(jnp.logical_and(second, i < half))
        def _():
            for n in range(4):
                push(i, slot, n).start()

        return carry

    lax.fori_loop(0, chunks, forward_chunk, 0)
    @pl.when(first)
    def _():
        def fetch(i, some):
            for n in some:
                save(i + half, i, n).wait()
                push(i, i, n).wait_recv()
                load(i, i, n, peer_hbm).start()

        fetch(1, (0, 1))
        fetch(1, (2, 3))
        fetch(0, (2, 3, 0, 1))
        for i in range(chunks):
            hand_on(i).wait_send()

    left_copy(chunks - 1).wait()
    for i in range(chunks):
        for copy in x_out_copies(i):
            copy.wait()

    @pl.when(second)
    def _():
        res_copy(chunks - 1).wait()
        for i in range(half):
            e_push(i).wait_send()
        gains_push().wait_send()
        for which in range(4):
            w_push(which).wait_send()

    def tally(name, start, values):
        total = jnp.sum(values.astype(jnp.float32), axis=0, keepdims=True)
        at = VECTORS[name][0] + start // UNIT
        for n in range(values.shape[1] // UNIT):
            vec[at + n : at + n + 1, :] += total[:, n * UNIT : (n + 1) * UNIT]

    def right_blocks(first_block, value):
        for n in range(value.shape[1] // UNIT):
            right[first_block + n] = value[:, n * UNIT : (n + 1) * UNIT]

    turns = jnp.where(first, chunks + half, half)

    def chunk_of(turn):
        late = jnp.where(first, turn >= chunks, True)
        return 1 - lax.rem(turn, 2) + jnp.where(late, half, 0)

    def loads(turn, some, action):
        for peers in (True, False):
            @pl.when((turn < half) if peers else (turn >= half))
            def _():
                i = chunk_of(turn)
                for n in some:
                    action(load(i, lax.rem(i, 2), n, peer_hbm if peers else own_hbm))

    def right_done(turn, n):
        i = chunk_of(turn)

        @pl.when(jnp.logical_and(first, turn < half))
        def _():
            right_push(i, n).wait_send()

        @pl.when(jnp.logical_not(jnp.logical_and(first, turn < half)))
        def _():
            right_copy(i, n).wait()

    def right_go(turn, n):
        i = chunk_of(turn)

        @pl.when(jnp.logical_and(first, turn < half))
        def _():
            right_push(i, n).start()

        @pl.when(jnp.logical_not(jnp.logical_and(first, turn < half)))
        def _():
            right_copy(i, n).start()

    def tail_part(turn, i):
        slot = lax.rem(i, 2)

        @pl.when(first)
        def _():
            loads(turn, (0, 1), lambda copy: copy.wait())

            @pl.when(turn < half)
            def _():
                e_push(i).wait_recv()

            @pl.when(turn == 0)
            def _():
                gains_push().wait_recv()
                gains[...] = gains_peer[...]

            @pl.when(turn == half)
            def _():
                own_gains()

        @pl.when(second)
        def _():
            e_copy(i).wait()

        @pl.when(turn >= 1)
        def _():
            for n in range(2):
                right_done(turn - 1, n)

        def ready(which):
            @pl.when(jnp.logical_and(first, jnp.logical_or(turn == 0, turn == half)))
            def _():
                w_copy(which).wait()

        now_a, total = keep_a.at[slot], dn1

        def kept(name, start=0):
            at = KEEP_A[name] + start
            return now_a[:, at : at + width].astype(jnp.float32)

        e = e_in[i].astype(jnp.float32)
        unit_two = kept("u2")
        tally("g2", 0, e * unit_two)
        tally("h2", 0, e)
        second_full = norm_back(
            e * gains[1:2, :], unit_two, stat_a[slot, :, STAT_A["s2"] : STAT_A["s2"] + 1]
        )
        second_low = second_full.astype(jnp.bfloat16)
        right_blocks(0, second_low)
        tally("bd", 0, second_low)
        total[...] = second_full

        ready(3)

        def pulled(n):
            return back_product(second_low, wd[n * width : (n + 1) * width, :])

        grad = pulled(0)
        for n in range(4):
            later = pulled(n + 1) if n < 3 else None
            hidden_low = (grad * kept("slope", n * width)).astype(jnp.bfloat16)
            right_blocks(3 + 3 * n, hidden_low)
            tally("bu", n * width, hidden_low)
            if n == 0:
                ready(2)
            total[...] += back_product(hidden_low, wu[:, n * width : (n + 1) * width])
            grad = later
        right_go(turn, 0)
        grad_normed = total[...]
        unit_one = kept("u1")
        tally("g1", 0, grad_normed * unit_one)
        tally("h1", 0, grad_normed)
        grad_first = norm_back(
            grad_normed * gains[0:1, :], unit_one, stat_a[slot, :, STAT_A["s1"] : STAT_A["s1"] + 1]
        )
        total[...] = grad_first
        first_low = grad_first.astype(jnp.bfloat16)
        right_blocks(15, first_low)
        right_go(turn, 1)
        tally("bo", 0, first_low)
        ready(1)
        grad_mixed = back_product(first_low, wo[...]).astype(jnp.bfloat16).astype(jnp.float32)
        weighed[...] = (grad_mixed * stat_a[slot, :, 0:width]).astype(jnp.bfloat16)

        @pl.when(second)
        def _():
            rest[i - half] = total[...]
            hand_back(i)[3].start()

        @pl.when(first)
        def _():
            @pl.when(turn + 2 < turns)
            def _():
                loads(turn + 2, (0, 1), lambda copy: copy.start())

            @pl.when(turn == half - 1)
            def _():
                for which in (3, 2, 1):
                    w_copy(which).start()

    def pair_part(i, pair):
        slot = lax.rem(i, 2)
        now_b, old_b = keep_b.at[slot], keep_b.at[1 - slot]
        span = pl.ds(pl.multiple_of(pair * 128, 128), 128)

        def cut(ref, name):
            return ref[:, pl.ds(pl.multiple_of(KEEP_B[name] + pair * 128, 128), 128)]

        queries = cut(now_b, "q")
        w = weighed[:, span]
        cross = w.astype(jnp.float32) * stat_b[slot, :, span]
        zero, one = jnp.zeros_like(w), jnp.ones_like(w)
        halves = []
        for part in range(2):
            own = low if part == 0 else jnp.logical_not(low)
            spare = 64 * (1 - part)
            inner = jnp.sum(jnp.where(own, cross, 0.0), axis=-1, keepdims=True)
            rough = inner.astype(jnp.bfloat16).astype(jnp.float32)
            extra = jnp.where(
                lanes == spare, -rough, jnp.where(lanes == spare + 1, rough - inner, 0.0)
            ).astype(jnp.bfloat16)
            halves.append(
                (own, jnp.where(own, w, extra), jnp.where(own, queries, zero), jnp.where(own, w, zero))
            )

        def half_block(source, table):
            keys_in, values = cut(source, "k"), cut(source, "v")
            total_q, total_k, total_v = 0.0, 0.0, 0.0
            for own, w_extra, own_queries, own_w in halves:
                own_keys = jnp.where(own, keys_in, zero)
                scores = (back_product(queries, own_keys) * table).astype(jnp.bfloat16)
                grads = (back_product(w_extra, jnp.where(own, values, one)) * table).astype(
                    jnp.bfloat16
                )
                total_q += dot(grads, own_keys)
                total_k += rows_product(grads, own_queries)
                total_v += rows_product(scores, own_w)
            return total_q, total_k, total_v

        total_q, total_k, total_v = half_block(now_b, mix[0])
        dq[:, span] = total_q
        dk[:, span] = total_k
        dv[:, span] = total_v

        @pl.when(slot == 0)
        def _():
            dk[:, span] += carry_k[:, span]
            dv[:, span] += carry_v[:, span]

        @pl.when(slot == 1)
        def _():
            far_q, far_k, far_v = half_block(old_b, mix[1])
            dq[:, span] += far_q
            carry_k[:, span] = far_k
            carry_v[:, span] = far_v

    def head_part(turn, i):
        slot = lax.rem(i, 2)

        @pl.when(turn >= 1)
        def _():
            right_done(turn - 1, 2)

            @pl.when(second)
            def _():
                for copy in hand_back(chunk_of(turn - 1))[:3]:
                    copy.wait_send()

        @pl.when(jnp.logical_and(first, jnp.logical_or(turn == 0, turn == half)))
        def _():
            w_copy(0).wait()

        now_b = keep_b.at[slot]
        for n, (source, slope) in enumerate(((dq, "sq"), (dk, "sk"), (dv, None))):
            values = source[...]
            if slope:
                at = KEEP_B[slope]
                values = values * now_b[:, at : at + width].astype(jnp.float32)
            values = values.astype(jnp.bfloat16)
            right_blocks(18 + 3 * n, values)

            @pl.when(second)
            def _():
                hand_back(i)[n].start()

            tally("bp", n * width, values)
        right_go(turn, 2)

        def through(blocks_of, start):
            for n in range(3):
                values = jnp.concatenate([blocks_of[3 * n + m] for m in range(3)], axis=1)
                start += back_product(values, wp[:, n * width : (n + 1) * width])
            return start

        @pl.when(first)
        def _():
            grad_in = through(right.at[18:27], dn1[...])

            @pl.when(turn < half)
            def _():
                e_in[i] = grad_in.astype(jnp.bfloat16)

            @pl.when(turn >= half)
            def _():
                @pl.when(turn > half)
                def _():
                    res_copy(chunk_of(turn - 1)).wait()

                rows_out[...] = grad_in
                res_copy(i).start()

            @pl.when(turn + 2 < turns)
            def _():
                loads(turn + 2, (2, 3), lambda copy: copy.start())

            @pl.when(turn == half - 1)
            def _():
                vec_sent[...] = vec[...]
                vec_push().start()
                vec[...] = jnp.zeros_like(vec)
                for late in (chunks - 1, chunks - 2):
                    for copy in hand_back(late):
                        copy.wait_recv()
                    e_in[late] = through(cut_in.at[late - half], rest_in[late - half]).astype(
                        jnp.bfloat16
                    )
                w_copy(0).start()

    def one_turn(turn, carry):
        i = chunk_of(turn)
        tail_part(turn, i)

        @pl.when(jnp.logical_and(first, lax.rem(turn, 2) == 0))
        def _():
            loads(turn, (2, 3), lambda copy: copy.wait())
            loads(turn + 1, (2, 3), lambda copy: copy.wait())

        def one_pair(pair, inner):
            pair_part(i, pair)
            return inner

        lax.fori_loop(0, pairs, one_pair, 0)
        head_part(turn, i)
        return carry

    lax.fori_loop(0, turns, one_turn, 0)
    for n in range(3):
        right_copy(half, n).wait()

    @pl.when(first)
    def _():
        res_copy(half).wait()
        vec_push().wait_send()

    @pl.when(second)
    def _():
        for copy in hand_back(half)[:3]:
            copy.wait_send()
        for i in range(half, chunks):
            hand_back(i)[3].wait_send()
        vec_push().wait_recv()
        vec[...] += vec_peer[...]
        for i in range(half):
            for n in range(3):
                right_push(i, n).wait_recv()

    out_copy = pltpu.make_async_copy(vec, vec_out, w_sem.at[0])
    out_copy.start()
    out_copy.wait()


def run_layers(ends, mats, rows_in, mix):
    tokens, width = ends.shape
    chunks = tokens // CHUNK
    bf16, f32 = jnp.bfloat16, jnp.float32

    def kept(count):
        return [
            jax.ShapeDtypeStruct((count * CHUNK, columns), dtype)
            for columns, dtype in (
                (KEEP_A_WIDTH, bf16), (STAT_A_WIDTH, f32), (KEEP_B_WIDTH, bf16), (width, f32)
            )
        ]

    out_shape = (
        [
            jax.ShapeDtypeStruct((21, chunks, CHUNK, UNIT), bf16),
            jax.ShapeDtypeStruct((27, chunks, CHUNK, UNIT), bf16),
        ]
        + kept(chunks)
        + kept(chunks // 2)
        + [jax.ShapeDtypeStruct(mat.shape, mat.dtype) for mat in mats]
        + [
            jax.ShapeDtypeStruct((tokens, width), f32),
            jax.ShapeDtypeStruct((40, UNIT), f32),
        ]
    )
    chunk_f32 = pltpu.VMEM((CHUNK, width), f32)
    all_rows = pltpu.VMEM((chunks, CHUNK, width), bf16)
    dma = pltpu.SemaphoreType.DMA
    outs = pl.pallas_call(
        partial(layers_kernel, chunks),
        out_shape=out_shape,
        in_specs=any_specs(5) + vmem_specs(9),
        out_specs=any_specs(16),
        scratch_shapes=[pltpu.VMEM(mat.shape, mat.dtype) for mat in mats]
        + [
            all_rows,
            all_rows,
            all_rows,
            pltpu.VMEM((18, CHUNK, UNIT), bf16),
            pltpu.VMEM((27, CHUNK, UNIT), bf16),
            pltpu.VMEM((2, CHUNK, KEEP_A_WIDTH), bf16),
            pltpu.VMEM((2, CHUNK, STAT_A_WIDTH), f32),
            pltpu.VMEM((2, CHUNK, KEEP_B_WIDTH), bf16),
            pltpu.VMEM((2, CHUNK, width), f32),
            chunk_f32,
            pltpu.VMEM((HEADS, CHUNK, 128), f32),
            chunk_f32,
            chunk_f32,
            chunk_f32,
            chunk_f32,
            chunk_f32,
            chunk_f32,
            pltpu.VMEM((CHUNK, width), bf16),
            pltpu.VMEM((40, UNIT), f32),
            pltpu.VMEM((40, UNIT), f32),
            pltpu.VMEM((40, UNIT), f32),
            pltpu.VMEM((8, width), f32),
            pltpu.VMEM((8, width), f32),
            pltpu.VMEM((chunks // 2, 9, CHUNK, UNIT), bf16),
            pltpu.VMEM((chunks // 2, CHUNK, width), f32),
            pltpu.VMEM((chunks // 2, CHUNK, width), f32),
            dma((4,)),
            dma((chunks,)),
            dma((chunks, 3)),
            dma((chunks,)),
            dma,
            dma((3,)),
            dma((2, 4)),
            dma,
            dma((chunks,)),
            dma((chunks,)),
            dma((chunks // 2, 4)),
            dma((chunks // 2, 4)),
            dma((4,)),
            dma((4,)),
            dma((chunks // 2,)),
            dma((chunks // 2,)),
            dma((chunks // 2, 4)),
            dma((chunks // 2, 4)),
            dma((3,)),
            dma((chunks // 2, 3)),
            dma,
            dma,
            dma,
            dma,
        ],
        compiler_params=pltpu.CompilerParams(
            collective_id=2, has_side_effects=True, vmem_limit_bytes=62 << 20
        ),
        name="layers",
    )(ends, *mats, *rows_in, mix)
    return outs[14], outs[0], outs[1], outs[15]


MATRICES = ((81, 9, 3), (72, 3, 3), (36, 12, 3), (0, 3, 12))


def widen_kernel(full, *refs):
    targets, vectors, held, out_sem = refs[:4], refs[4:12], refs[12:16], refs[16]
    copies, turn = [], 0
    for which, (begin, across, down) in enumerate(MATRICES):
        for block in range(down):
            span = pl.ds(block * UNIT, UNIT)
            copy = pltpu.make_async_copy(
                held[which].at[span], targets[which].at[0, span], out_sem.at[turn]
            )

            def one(n, carry):
                start = pl.multiple_of((begin + block * across + n) * UNIT, UNIT)
                held[which][span, pl.ds(pl.multiple_of(n * UNIT, UNIT), UNIT)] = full[
                    pl.ds(start, UNIT), :
                ].astype(jnp.float32)
                return carry

            lax.fori_loop(0, across, one, 0)
            copy.start()
            copies.append(copy)
            turn += 1
    for (start, count), vector in zip(VECTORS.values(), vectors):
        for n in range(count):
            at = UNITS * UNIT + start + n
            vector[:, n * UNIT : (n + 1) * UNIT] = full[at : at + 1, :].astype(jnp.float32)
    for copy in copies:
        copy.wait()


def widen(full):
    shapes = [(down * UNIT, across * UNIT) for _, across, down in MATRICES]
    return pl.pallas_call(
        widen_kernel,
        out_shape=[jax.ShapeDtypeStruct((1,) + shape, jnp.float32) for shape in shapes]
        + [jax.ShapeDtypeStruct((1, count * UNIT), jnp.float32) for _, count in VECTORS.values()],
        in_specs=[pl.BlockSpec(memory_space=pltpu.VMEM)],
        out_specs=any_specs(4) + vmem_specs(8),
        scratch_shapes=[pltpu.VMEM(shape, jnp.float32) for shape in shapes]
        + [pltpu.SemaphoreType.DMA((sum(down for _, _, down in MATRICES),))],
        compiler_params=pltpu.CompilerParams(vmem_limit_bytes=36 << 20),
        name="widen",
    )(full)


def mix_tables(length):
    places = jnp.arange(2 * CHUNK, dtype=jnp.int32)
    angles = places.astype(jnp.float32) * ((0.5 * math.pi) / length.astype(jnp.float32))
    cosine, sine, document = lax.optimization_barrier(
        (jnp.cos(angles), jnp.sin(angles), places // length)
    )

    def table(start):
        later, earlier = slice(start, start + CHUNK), slice(0, CHUNK)
        seen = jnp.logical_and(
            document[later, None] == document[None, earlier],
            places[later, None] >= places[None, earlier],
        )
        near = cosine[later, None] * cosine[None, earlier] + sine[later, None] * sine[None, earlier]
        return jnp.where(seen, near, 0.0)

    return jnp.stack([table(0), table(CHUNK)])


def shards(
    endpoints,
    projection,
    projection_bias,
    output_weight,
    output_bias,
    first_gain,
    first_shift,
    up_weight,
    up_bias,
    down_weight,
    down_bias,
    second_gain,
    second_shift,
    segment_length,
):
    dp_size = lax.axis_size("dp")
    mats = (projection[0], output_weight[0], up_weight[0], down_weight[0])
    rows = (
        projection_bias, output_bias, first_gain, first_shift, up_bias, down_bias, second_gain,
        second_shift,
    )
    mix = mix_tables(segment_length[0])
    results, left, right, vec = run_layers(endpoints[0], mats, rows, mix)
    full = reduce_gradients(left, right, vec, dp_size)
    proj, out, up, down, bp, bo, g1, h1, bu, bd, g2, h2 = widen(full)
    return (results[None], proj, bp, out, bo, g1, h1, up, bu, down, bd, g2, h2)


def solution(mesh):
    in_specs = (
        P("section", "dp", None),
        P("section", None, None),
        P("section", None),
        P("section", None, None),
        P("section", None),
        P("section", None),
        P("section", None),
        P("section", None, None),
        P("section", None),
        P("section", None, None),
        P("section", None),
        P("section", None),
        P("section", None),
        P("dp"),
    )
    out_specs = (
        P("section", "dp", None),
        P("section", None, None),
        P("section", None),
        P("section", None, None),
        P("section", None),
        P("section", None),
        P("section", None),
        P("section", None, None),
        P("section", None),
        P("section", None, None),
        P("section", None),
        P("section", None),
        P("section", None),
    )
    return jax.shard_map(shards, mesh=mesh, in_specs=in_specs, out_specs=out_specs, check_vma=False)
```

```python
from functools import partial
import math

import jax
import jax.numpy as jnp
from jax import lax
from jax.experimental import pallas as pl
from jax.experimental.pallas import tpu as pltpu
from jax.sharding import PartitionSpec as P

HEADS = 12
EPSILON = 1e-05
MESH = pl.DeviceIdType.MESH


def rows_product(left_mat, right_mat):
    return lax.dot_general(
        left_mat, right_mat, (((0,), (0,)), ((), ())), preferred_element_type=jnp.float32
    )


def back_product(grad_mat, weight_mat):
    return lax.dot_general(
        grad_mat, weight_mat, (((1,), (1,)), ((), ())), preferred_element_type=jnp.float32
    )


def factor_dims(count):
    bits = count.bit_length() - 1
    return (1 << (bits // 3), 1 << ((bits + 1) // 3), 1 << ((bits + 2) // 3))


ORDERS = {"a": (0, 1, 2), "b": (1, 2, 0), "c": (2, 0, 1)}
PATTERN = "abacabc"
LAG = 3
END_LAG = 4
UNIT = 256
UNITS = 108
PIECE_ROWS = 512
SEM_SLOTS = 35


def stage_list(order, dims, rows):
    stages, size, landing = [], rows, 0
    for level, ax in enumerate(order):
        part = size // dims[ax]
        for step in range(1, dims[ax]):
            stages.append(("reduce", level, ax, step, part, landing))
            landing += part if dims[ax] == 2 else 2 * part
        size = part
    for level in reversed(range(3)):
        ax = order[level]
        for step in range(1, dims[ax]):
            stages.append(("gather", level, ax, step, size, 0))
        size *= dims[ax]
    return stages, landing


def unit_blocks(unit):
    up, out, proj = unit - 36, unit - 72, unit - 81
    left = jnp.where(
        unit < 36,
        unit // 3,
        jnp.where(unit < 72, 12 + up // 12, jnp.where(unit < 81, 15 + out // 3, 18 + proj // 9)),
    )
    right = jnp.where(
        unit < 36,
        unit % 3,
        jnp.where(unit < 72, 3 + up % 12, jnp.where(unit < 81, 15 + out % 3, 18 + proj % 9)),
    )
    return left, right


def axis_places(dims):
    here = lax.axis_index("dp")
    strides = (1, dims[0], dims[0] * dims[1])
    return here, strides, [(here // strides[ax]) % dims[ax] for ax in range(3)]


def greet_axes(dims, semaphore):
    here, strides, place = axis_places(dims)
    around = 0
    for ax in range(3):
        for sign, can in ((1, place[ax] < dims[ax] - 1), (-1, place[ax] > 0)):
            @pl.when(can)
            def _():
                pl.semaphore_signal(
                    semaphore, inc=1, device_id={"dp": here + sign * strides[ax]},
                    device_id_type=MESH,
                )
            around = around + can.astype(jnp.int32)
    return around


def gather_sends(spot, count):
    found = {}
    for at in range(count):
        sent = (at + 1 if at < count - 1 else 0) + (count - at if at > 0 else 0)
        found.setdefault(sent, []).append(spot == at)
    options = []
    for sent, spots in found.items():
        can = spots[0]
        for other in spots[1:]:
            can = jnp.logical_or(can, other)
        options.append((can, sent))
    return options


def guarded(can, action):
    if can is None:
        action()
    else:
        pl.when(can)(action)


def summing(dims, pieces, rows, acc, acc_slots, full, landing, land_slots, left_hbm,
            right_hbm, vec_hbm, vec, left_ring, right_ring, load_sem, vec_sem, send_sem, recv_sem):
    here, strides, place = axis_places(dims)
    ring, chunks = left_ring.shape[0], left_ring.shape[1]
    per_piece = rows // UNIT
    land_rows = landing.shape[0] // land_slots
    period = len(PATTERN)
    n_shards = dims[0] * dims[1] * dims[2]
    orders = {**ORDERS, "last": ORDERS[PATTERN[(pieces - 1) % period]]}
    sizes = {name: min(rows, 16 * n_shards) if name == "last" else rows for name in orders}
    plans = {name: stage_list(order, dims, sizes[name])[0] for name, order in orders.items()}
    n_stages = len(plans["a"])
    shard = rows // (dims[0] * dims[1] * dims[2])

    bases = {}
    for name, order in orders.items():
        base, size, found = 0, sizes[name], []
        for ax in order:
            found.append(base)
            size = size // dims[ax]
            base = base + place[ax] * size
        bases[name] = found + [base]

    sent_rows = {}
    for name, plan in plans.items():
        sure, options = 0, [(None, 0)]
        for kind, _, ax, step, part, _ in plan:
            if dims[ax] == 2 or kind == "reduce":
                sure += part
            elif step == 1:
                options = [
                    (can if other is None else jnp.logical_and(can, other), more + part * count)
                    for other, more in options
                    for can, count in gather_sends(place[ax], dims[ax])
                ]
        sent_rows[name] = [(can, sure + more) for can, more in options]

    def view(ref, slot, start, size):
        across = ref.shape[1] // UNIT
        first = pl.multiple_of(slot // across * rows + start, 16)
        if across == 1:
            return ref.at[pl.ds(first, size)]
        return ref.at[pl.ds(first, size), pl.ds(pl.multiple_of(slot % across * UNIT, UNIT), UNIT)]

    def loads(unit):
        slot = unit % ring
        left, right = unit_blocks(unit)
        return (
            pltpu.make_async_copy(left_hbm.at[left], left_ring.at[slot], load_sem.at[slot, 0]),
            pltpu.make_async_copy(right_hbm.at[right], right_ring.at[slot], load_sem.at[slot, 1]),
        )

    def prime():
        for unit in range(ring):
            for copy in loads(jnp.int32(unit)):
                copy.start()

    vec_copy = pltpu.make_async_copy(vec_hbm, vec.at[pl.ds(0, vec_hbm.shape[0])], vec_sem)

    def form(piece, sub):
        unit = piece * per_piece + sub
        target = view(acc, piece % acc_slots, sub * UNIT, UNIT)

        @pl.when(unit < UNITS)
        def _():
            for copy in loads(unit):
                copy.wait()
            slot = unit % ring
            tokens = chunks * left_ring.shape[2]
            target[...] = rows_product(
                left_ring[slot].reshape(tokens, UNIT), right_ring[slot].reshape(tokens, UNIT)
            ).astype(jnp.bfloat16)

            @pl.when(unit + ring < UNITS)
            def _():
                for copy in loads(unit + ring):
                    copy.start()

        @pl.when(unit >= UNITS)
        def _():
            if sub == 0:
                vec_copy.wait()
            target[...] = vec[sub * UNIT : (sub + 1) * UNIT, :].astype(jnp.bfloat16)

    def copies(name, stage, piece):
        kind, level, ax, step, part, land = plans[name][stage]
        count, spot = dims[ax], place[ax]
        slot = piece % SEM_SLOTS
        held, index = (acc, piece % acc_slots) if kind == "reduce" else (full, piece)
        land_start = piece % land_slots * land_rows + land

        def chunk(q):
            return view(held, index, bases[name][level] + q * part, part)

        def landed(way):
            return landing.at[pl.ds(pl.multiple_of(land_start + way * part, 16), part)]

        def remote(src, dst, way, sign):
            return lambda: pltpu.make_async_remote_copy(
                src_ref=src, dst_ref=dst, send_sem=send_sem.at[slot],
                recv_sem=recv_sem.at[slot, stage, way],
                device_id={"dp": here + sign * strides[ax]}, device_id_type=MESH,
            )

        sends, receives = [], []
        if count == 2:
            sign = 1 - 2 * spot
            mine, other = spot, 1 - spot
            if kind == "reduce":
                sends.append((None, remote(chunk(other), landed(0), 0, sign)))
                receives.append((None, remote(chunk(mine), landed(0), 0, sign), mine, landed(0)))
            else:
                sends.append((None, remote(chunk(mine), chunk(mine), 0, sign)))
                receives.append((None, remote(chunk(other), chunk(other), 0, sign), other, None))
            return sends, receives, chunk
        back = count - 1 - spot
        if kind == "reduce":
            for way, sign, can, q in (
                (0, 1, spot < step, spot + count - step),
                (1, -1, back < step, step - 1 - back),
            ):
                q = jnp.clip(q, 0, count - 1)
                sends.append((can, remote(chunk(q), landed(way), way, sign)))
            for way, sign, can, q in (
                (0, 1, jnp.logical_and(spot >= 1, spot - 1 < step), spot - 1 + count - step),
                (1, -1, jnp.logical_and(back >= 1, back - 1 < step), step - back),
            ):
                q = jnp.clip(q, 0, count - 1)
                receives.append((can, remote(chunk(q), landed(way), way, sign), q, landed(way)))
        else:
            for way, sign, can, q in (
                (0, 1, jnp.logical_and(back >= 1, spot >= step - 1), spot - step + 1),
                (1, -1, jnp.logical_and(spot >= 1, back >= step - 1), spot + step - 1),
            ):
                q = jnp.clip(q, 0, count - 1)
                sends.append((can, remote(chunk(q), chunk(q), way, sign)))
            for way, sign, can, q in (
                (0, 1, spot >= step, spot - step),
                (1, -1, back >= step, spot + step),
            ):
                q = jnp.clip(q, 0, count - 1)
                receives.append((can, remote(chunk(q), chunk(q), way, sign), q, None))
        return sends, receives, chunk

    def work(name, stage, piece):
        if stage > 0:
            sends, receives, chunk = copies(name, stage - 1, piece)
            for can, copy, q, landed in receives:
                def finish():
                    copy().wait_recv()
                    if landed is not None:
                        block = chunk(q)
                        block[...] = block[...] + landed[...]
                guarded(can, finish)
        if stage == n_stages // 2:
            mine = bases[name][3]
            shard = sizes[name] // n_shards
            own = view(full, piece, mine, shard)
            own[...] = view(acc, piece % acc_slots, mine, shard)[...]
        if stage < n_stages:
            for can, copy in copies(name, stage, piece)[0]:
                guarded(can, lambda: copy().start())
        if stage == n_stages:
            for can, amount in sent_rows[name]:
                sent = landing.at[pl.ds(0, amount)]
                guarded(
                    can,
                    lambda: pltpu.make_async_copy(
                        sent, sent, send_sem.at[piece % SEM_SLOTS]
                    ).wait(),
                )

    starts = [0]
    for stage in range(n_stages):
        starts.append(starts[-1] + (END_LAG if stage in (0, n_stages - 1) else LAG))
    total_ticks = pieces + starts[-1]

    def run(meet):
        prime()
        vec[...] = jnp.zeros_like(vec)
        vec_copy.start()
        meet()

        def some_ticks(turn, carry):
            for spot_in in range(period):
                now = turn * period + spot_in
                for stage in range(n_stages + 1):
                    piece = now - starts[stage]
                    name = PATTERN[(spot_in - starts[stage]) % period]

                    @pl.when(jnp.logical_and(piece >= 0, piece < pieces - 1))
                    def _():
                        at = jnp.clip(piece, 0, pieces - 2)
                        if stage == 0:
                            for sub in range(per_piece):
                                form(at, sub)
                        work(name, stage, at)

                    if (spot_in - starts[stage] - pieces + 1) % period == 0:
                        @pl.when(piece == pieces - 1)
                        def _():
                            if stage == 0:
                                for sub in range(sizes["last"] // UNIT):
                                    form(jnp.int32(pieces - 1), sub)
                            work("last", stage, jnp.int32(pieces - 1))

            return carry

        lax.fori_loop(0, -(-total_ticks // period), some_ticks, 0)

    return run


def sum_sizes(dp_size):
    dims = factor_dims(dp_size)
    rows = max(PIECE_ROWS, 16 * dp_size)
    land = max(stage_list(order, dims, rows)[1] for order in ORDERS.values())
    return dims, rows, -(-(UNITS + 1) * UNIT // rows), land, 2 * (sum(dims) - 3)


def sum_semaphores(ring, stages):
    return [
        pltpu.SemaphoreType.DMA((ring, 2)),
        pltpu.SemaphoreType.DMA,
        pltpu.SemaphoreType.DMA((SEM_SLOTS,)),
        pltpu.SemaphoreType.DMA((SEM_SLOTS, stages, 2)),
    ]


def reduce_kernel(dims, pieces, rows, left_hbm, right_hbm, vec_hbm, full, acc, landing, vec, left_ring,
                  right_ring, load_sem, vec_sem, send_sem, recv_sem):
    barrier = pltpu.get_barrier_semaphore()
    around = greet_axes(dims, barrier)
    slots = acc.shape[0] // rows
    run = summing(
        dims, pieces, rows, acc, slots, full, landing, slots, left_hbm, right_hbm, vec_hbm, vec,
        left_ring, right_ring, load_sem, vec_sem, send_sem, recv_sem,
    )
    run(lambda: pl.semaphore_wait(barrier, around))


def reduce_gradients(left, right, vec, dp_size):
    dims, rows, pieces, land, stages = sum_sizes(dp_size)
    ring = 4 if dp_size <= 16 else 2
    slots = min(SEM_SLOTS, pieces)
    return pl.pallas_call(
        partial(reduce_kernel, dims, pieces, rows),
        out_shape=pltpu.VMEM((pieces * rows, UNIT), jnp.bfloat16),
        in_specs=any_specs(3),
        out_specs=pl.BlockSpec(memory_space=pltpu.VMEM),
        scratch_shapes=[
            pltpu.VMEM((slots * rows, UNIT), jnp.bfloat16),
            pltpu.VMEM((slots * land, UNIT), jnp.bfloat16),
            pltpu.VMEM((rows, UNIT), jnp.float32),
            pltpu.VMEM((ring,) + left.shape[1:], jnp.bfloat16),
            pltpu.VMEM((ring,) + left.shape[1:], jnp.bfloat16),
        ]
        + sum_semaphores(ring, stages),
        compiler_params=pltpu.CompilerParams(
            collective_id=1, has_side_effects=True, vmem_limit_bytes=47 << 20
        ),
        name="reduce",
    )(left, right, vec)


CHUNK = 256
KEEP_A = {"slope": 0, "u1": 3072, "u2": 3840}
KEEP_A_WIDTH = 4608
STAT_A = {"rden": 0, "s1": 768, "s2": 896}
STAT_A_WIDTH = 1024
KEEP_B = {"q": 0, "k": 768, "sq": 1536, "sk": 2304, "v": 3072}
KEEP_B_WIDTH = 3840
VECTORS = {
    "bp": (0, 9), "bo": (9, 3), "g1": (12, 3), "h1": (15, 3), "bu": (18, 12), "bd": (30, 3), "g2": (33, 3),
    "h2": (36, 3),
}
TAIL_SCALE = 0.45
TAIL_POLY = (
    0.25396798653159114,
    0.25170428274474826,
    0.24846812412232888,
    0.08947906819608953,
    0.2922223682202733,
    -0.13585125317877522,
)


def dot(left_mat, right_mat):
    return jnp.dot(left_mat, right_mat, preferred_element_type=jnp.float32)


def inverse(value):
    return pl.reciprocal(value, approx=True)


def gelu_pair(hidden):
    bell = jnp.exp2(hidden * hidden * (-0.5 * math.log2(math.e)))
    t = inverse(1.0 + (TAIL_SCALE * math.sqrt(0.5)) * jnp.abs(hidden))
    poly = jnp.full_like(t, 0.5 * TAIL_POLY[-1])
    for coefficient in TAIL_POLY[-2::-1]:
        poly = poly * t + 0.5 * coefficient
    tail = poly * t * bell
    below = jnp.where(hidden >= 0, 1.0 - tail, tail)
    return hidden * below, below + hidden * (bell * (1.0 / math.sqrt(2.0 * math.pi)))


def softplus_pair(value):
    small = jnp.exp2(jnp.abs(value) * -math.log2(math.e))
    whole = 1.0 + small
    log_whole = jnp.where(small < 2e-3, small * (1.0 - 0.5 * small), jnp.log(whole))
    return (
        jnp.maximum(value, 0.0) + log_whole,
        jnp.where(value >= 0, 1.0, small) * inverse(whole),
    )


def centred(rows):
    centre = rows - jnp.mean(rows, axis=-1, keepdims=True)
    scaling = lax.rsqrt(jnp.mean(centre * centre, axis=-1, keepdims=True) + EPSILON)
    return centre * scaling, scaling


def wide(column, width=128):
    return jnp.broadcast_to(column, (column.shape[0], width))


def first_half(rows):
    return lax.broadcasted_iota(jnp.int32, (rows, 128), 1) < 64


def row(ref):
    return ref[...].astype(jnp.float32)


def any_specs(count):
    return [pl.BlockSpec(memory_space=pl.ANY)] * count


def vmem_specs(count):
    return [pl.BlockSpec(memory_space=pltpu.VMEM)] * count


def norm_back(grad, unit_rows, scaling):
    mean_grad = jnp.mean(grad, axis=-1, keepdims=True)
    mean_cross = jnp.mean(grad * unit_rows, axis=-1, keepdims=True)
    return scaling * (grad - mean_grad - unit_rows * mean_cross)


def layers_kernel(chunks, *refs):
    (ends_hbm, wp_hbm, wo_hbm, wu_hbm, wd_hbm, bp, bo, g1, h1, bu, bd, g2, h2, mix) = refs[:14]
    left_hbm, right_hbm = refs[14:16]
    own_hbm, peer_hbm, peer_w_hbm = refs[16:20], refs[20:24], refs[24:28]
    res_hbm, vec_out = refs[28:30]
    (wp, wo, wu, wd, x_in, e_in, handed, left, right, keep_a, stat_a, keep_b, stat_b, rows_out, nums, dq,
     dk, dv, carry_k, carry_v, dn1, weighed, vec, vec_sent, vec_peer, gains, gains_peer, cut_in, rest_in, rest, w_sem, x_sem, xo_sem, e_sem, left_sem,
     right_sem, load_sem, res_sem, send_f, recv_f, send_b, recv_b, send_w, recv_w, send_e, recv_e,
     send_k, recv_k, send_r, recv_r, send_v, recv_v, send_g, recv_g) = refs[30:]

    section = lax.axis_index("section")
    first = section == 0
    second = jnp.logical_not(first)
    partner = {"section": 1 - section}
    width = ends_hbm.shape[1]
    pairs = width // 128
    half = chunks // 2
    mats_hbm, mats = (wp_hbm, wo_hbm, wu_hbm, wd_hbm), (wp, wo, wu, wd)
    kept_bufs = (keep_a, stat_a, keep_b, stat_b)

    def w_copy(which, sources=mats_hbm):
        return pltpu.make_async_copy(sources[which], mats[which], w_sem.at[which])

    def remote(src, dst, send, recv):
        return pltpu.make_async_remote_copy(
            src_ref=src, dst_ref=dst, send_sem=send, recv_sem=recv, device_id=partner,
            device_id_type=MESH,
        )

    def w_push(which):
        return remote(mats_hbm[which], peer_w_hbm[which], send_w.at[which], recv_w.at[which])

    def rows_of(i):
        return pl.ds(pl.multiple_of(i * CHUNK, CHUNK), CHUNK)

    def x_copy(i):
        return pltpu.make_async_copy(ends_hbm.at[rows_of(i)], x_in.at[i], x_sem.at[i])

    def x_out_copies(i):
        return [
            pltpu.make_async_copy(
                x_in.at[i, :, n * UNIT : (n + 1) * UNIT], left_hbm.at[18 + n, i], xo_sem.at[i, n]
            )
            for n in range(3)
        ]

    def e_copy(i):
        return pltpu.make_async_copy(ends_hbm.at[rows_of(i)], e_in.at[i], e_sem.at[i])

    def e_push(i):
        return remote(ends_hbm.at[rows_of(i)], e_in.at[i], send_e.at[i], recv_e.at[i])

    def hand_on(i):
        return remote(handed.at[i], x_in.at[i], send_f.at[i], recv_f.at[i])

    def hand_back(i):
        at = i - half
        return [
            remote(
                right.at[18 + 3 * n : 21 + 3 * n], cut_in.at[at, 3 * n : 3 * n + 3],
                send_b.at[at, n], recv_b.at[at, n],
            )
            for n in range(3)
        ] + [remote(rest.at[at], rest_in.at[at], send_b.at[at, 3], recv_b.at[at, 3])]

    def left_copy(i):
        return pltpu.make_async_copy(left, left_hbm.at[0:18, i], left_sem)

    spans = ((0, 15), (15, 18), (18, 27))

    def right_copy(i, n):
        start, end = spans[n]
        return pltpu.make_async_copy(
            right.at[start:end], right_hbm.at[start:end, i], right_sem.at[n]
        )

    def right_push(i, n):
        start, end = spans[n]
        return remote(
            right.at[start:end], right_hbm.at[start:end, i], send_r.at[n], recv_r.at[i, n]
        )

    def save(i, slot, n):
        return pltpu.make_async_copy(
            kept_bufs[n].at[slot], own_hbm[n].at[rows_of(i)], load_sem.at[slot, n]
        )

    def push(i, slot, n):
        return remote(
            kept_bufs[n].at[slot], peer_hbm[n].at[rows_of(i)], send_k.at[i, n], recv_k.at[i, n]
        )

    def load(i, slot, n, source):
        return pltpu.make_async_copy(
            source[n].at[rows_of(i)], kept_bufs[n].at[slot], load_sem.at[slot, n]
        )

    def res_copy(i):
        return pltpu.make_async_copy(rows_out, res_hbm.at[rows_of(i)], res_sem)

    def own_gains():
        gains[0:1, :] = row(g1)
        gains[1:2, :] = row(g2)

    def gains_push():
        return remote(gains, gains_peer, send_g, recv_g)

    def vec_push():
        return remote(vec_sent, vec_peer, send_v, recv_v)

    @pl.when(first)
    def _():
        x_copy(0).start()

    for which in range(4):
        w_copy(which).start()

    @pl.when(first)
    def _():
        for i in range(1, chunks):
            x_copy(i).start()

    @pl.when(second)
    def _():
        for i in range(half, chunks):
            e_copy(i).start()

    barrier = pltpu.get_barrier_semaphore()
    pl.semaphore_signal(barrier, inc=1, device_id=partner, device_id_type=MESH)
    vec[...] = jnp.zeros_like(vec)
    gains[...] = jnp.zeros_like(gains)
    own_gains()
    pl.semaphore_wait(barrier, 1)

    @pl.when(second)
    def _():
        gains_push().start()
        for i in range(half):
            e_push(i).start()
        for which in (3, 2, 1, 0):
            w_push(which).start()

    def weights_ready(i, which):
        @pl.when(i == 0)
        def _():
            w_copy(which).wait()

    lanes = lax.broadcasted_iota(jnp.int32, (CHUNK, 128), 1)
    low = lanes < 64

    def forward_chunk(i, carry):
        slot = lax.rem(i, 2)

        @pl.when(i >= 2)
        def _():
            @pl.when(first)
            def _():
                for n in range(4):
                    save(i - 2, slot, n).wait()

            @pl.when(second)
            def _():
                for n in range(4):
                    push(i - 2, slot, n).wait_send()

        weights_ready(i, 0)

        @pl.when(first)
        def _():
            x_copy(i).wait()

        @pl.when(second)
        def _():
            hand_on(i).wait_recv()

        for copy in x_out_copies(i):
            copy.start()
        now_a, now_b, old_b = keep_a.at[slot], keep_b.at[slot], keep_b.at[1 - slot]

        def keep(ref, start, value):
            ref[:, start : start + value.shape[1]] = value.astype(jnp.bfloat16)

        def blocks(first_block, value):
            for n in range(value.shape[1] // UNIT):
                left[first_block + n] = value[:, n * UNIT : (n + 1) * UNIT]

        x = x_in[i]
        for part, (name, slope) in enumerate((("q", "sq"), ("k", "sk"))):
            cols = slice(part * width, (part + 1) * width)
            soft, sigma = softplus_pair(dot(x, wp[:, cols]) + row(bp)[:, cols])
            keep(now_b, KEEP_B[name], soft)
            keep(now_b, KEEP_B[slope], sigma)
        cols = slice(2 * width, 3 * width)
        keep(now_b, KEEP_B["v"], dot(x, wp[:, cols]) + row(bp)[:, cols])

        def mix_pair(pair, source, table, fresh):
            def cut(ref, name):
                return ref[:, KEEP_B[name] + pair * 128 : KEEP_B[name] + (pair + 1) * 128]

            queries, keys_in, values = cut(now_b, "q"), cut(source, "k"), cut(source, "v")
            zero, one = jnp.zeros_like(keys_in), jnp.ones_like(values)
            for half in range(2):
                own = low if half == 0 else jnp.logical_not(low)
                scores = back_product(queries, jnp.where(own, keys_in, zero)) * table
                num = dot(scores.astype(jnp.bfloat16), jnp.where(own, values, one))
                at = 2 * pair + half
                nums[at] = num if fresh else nums[at] + num

        for pair in range(pairs):
            mix_pair(pair, now_b, mix[0], True)

        @pl.when(slot == 1)
        def _():
            for pair in range(pairs):
                mix_pair(pair, old_b, mix[1], False)

        @pl.when(i >= 1)
        def _():
            left_copy(i - 1).wait()

        for pair in range(pairs):
            num_a, num_b = nums[2 * pair], nums[2 * pair + 1]
            inv = inverse(
                jnp.where(low, pltpu.roll(num_a, 64, 1), pltpu.roll(num_b, 64, 1))
            )
            span = slice(pair * 128, (pair + 1) * 128)
            stat_b[slot, :, span] = jnp.where(low, num_a, num_b) * inv
            stat_a[slot, :, span] = inv
        mixed_low = stat_b[slot].astype(jnp.bfloat16)
        blocks(15, mixed_low)
        weights_ready(i, 1)
        first_sum = x.astype(jnp.float32) + row(bo) + dot(mixed_low, wo[...])

        @pl.when(jnp.logical_and(first, i == chunks - 1))
        def _():
            for which in (1, 0):
                w_push(which).wait_recv()
                w_copy(which, peer_w_hbm).start()

        unit_one, scale_one = centred(first_sum)
        keep(now_a, KEEP_A["u1"], unit_one)
        stat_a[slot, :, STAT_A["s1"] : STAT_A["s1"] + 128] = wide(scale_one)
        normed = unit_one * row(g1) + row(h1)
        resid = dn1
        resid[...] = normed + row(bd)
        up_in = normed.astype(jnp.bfloat16)
        blocks(12, up_in)
        weights_ready(i, 2)

        def hidden_of(n):
            cols = slice(n * width, (n + 1) * width)
            return dot(up_in, wu[:, cols]) + row(bu)[:, cols]

        hidden = hidden_of(0)
        for n in range(4):
            later = hidden_of(n + 1) if n < 3 else None
            active, slope = gelu_pair(hidden)
            active = active.astype(jnp.bfloat16)
            blocks(3 * n, active)
            keep(now_a, n * width, slope)
            if n == 0:
                weights_ready(i, 3)
            resid[...] += dot(active, wd[n * width : (n + 1) * width, :])
            hidden = later

            @pl.when(jnp.logical_and(first, i == chunks - 1))
            def _():
                if n == 0:
                    w_push(3).wait_recv()
                    w_push(2).wait_recv()
                quarter = pl.ds(n * width, width)
                pltpu.make_async_copy(
                    peer_w_hbm[3].at[quarter], wd.at[quarter], w_sem.at[3]
                ).start()
                pltpu.make_async_copy(
                    peer_w_hbm[2].at[:, quarter], wu.at[:, quarter], w_sem.at[2]
                ).start()
        unit_two, scale_two = centred(resid[...])
        keep(now_a, KEEP_A["u2"], unit_two)
        stat_a[slot, :, STAT_A["s2"] : STAT_A["s2"] + 128] = wide(scale_two)
        result = unit_two * row(g2) + row(h2)

        @pl.when(first)
        def _():
            handed[i] = result.astype(jnp.bfloat16)
            hand_on(i).start()

        @pl.when(second)
        def _():
            @pl.when(i >= 1)
            def _():
                res_copy(i - 1).wait()

            rows_out[...] = result
            res_copy(i).start()

        left_copy(i).start()

        @pl.when(first)
        def _():
            for n in range(4):
                save(i, slot, n).start()

        @pl.when(jnp.logical_and(second, i < half))
        def _():
            for n in range(4):
                push(i, slot, n).start()

        return carry

    lax.fori_loop(0, chunks, forward_chunk, 0)
    @pl.when(first)
    def _():
        def fetch(i, some):
            for n in some:
                save(i + half, i, n).wait()
                push(i, i, n).wait_recv()
                load(i, i, n, peer_hbm).start()

        fetch(1, (0, 1))
        fetch(1, (2, 3))
        fetch(0, (2, 3, 0, 1))
        for i in range(chunks):
            hand_on(i).wait_send()

    left_copy(chunks - 1).wait()
    for i in range(chunks):
        for copy in x_out_copies(i):
            copy.wait()

    @pl.when(second)
    def _():
        res_copy(chunks - 1).wait()
        for i in range(half):
            e_push(i).wait_send()
        gains_push().wait_send()
        for which in range(4):
            w_push(which).wait_send()

    def tally(name, start, values):
        total = jnp.sum(values.astype(jnp.float32), axis=0, keepdims=True)
        at = VECTORS[name][0] + start // UNIT
        for n in range(values.shape[1] // UNIT):
            vec[at + n : at + n + 1, :] += total[:, n * UNIT : (n + 1) * UNIT]

    def right_blocks(first_block, value):
        for n in range(value.shape[1] // UNIT):
            right[first_block + n] = value[:, n * UNIT : (n + 1) * UNIT]

    turns = jnp.where(first, chunks + half, half)

    def chunk_of(turn):
        late = jnp.where(first, turn >= chunks, True)
        return 1 - lax.rem(turn, 2) + jnp.where(late, half, 0)

    def loads(turn, some, action):
        for peers in (True, False):
            @pl.when((turn < half) if peers else (turn >= half))
            def _():
                i = chunk_of(turn)
                for n in some:
                    action(load(i, lax.rem(i, 2), n, peer_hbm if peers else own_hbm))

    def right_done(turn, n):
        i = chunk_of(turn)

        @pl.when(jnp.logical_and(first, turn < half))
        def _():
            right_push(i, n).wait_send()

        @pl.when(jnp.logical_not(jnp.logical_and(first, turn < half)))
        def _():
            right_copy(i, n).wait()

    def right_go(turn, n):
        i = chunk_of(turn)

        @pl.when(jnp.logical_and(first, turn < half))
        def _():
            right_push(i, n).start()

        @pl.when(jnp.logical_not(jnp.logical_and(first, turn < half)))
        def _():
            right_copy(i, n).start()

    def tail_part(turn, i):
        slot = lax.rem(i, 2)

        @pl.when(first)
        def _():
            loads(turn, (0, 1), lambda copy: copy.wait())

            @pl.when(turn < half)
            def _():
                e_push(i).wait_recv()

            @pl.when(turn == 0)
            def _():
                gains_push().wait_recv()
                gains[...] = gains_peer[...]

            @pl.when(turn == half)
            def _():
                own_gains()

        @pl.when(second)
        def _():
            e_copy(i).wait()

        @pl.when(turn >= 1)
        def _():
            for n in range(2):
                right_done(turn - 1, n)

        def ready(which):
            @pl.when(jnp.logical_and(first, jnp.logical_or(turn == 0, turn == half)))
            def _():
                w_copy(which).wait()

        now_a, total = keep_a.at[slot], dn1

        def kept(name, start=0):
            at = KEEP_A[name] + start
            return now_a[:, at : at + width].astype(jnp.float32)

        e = e_in[i].astype(jnp.float32)
        unit_two = kept("u2")
        tally("g2", 0, e * unit_two)
        tally("h2", 0, e)
        second_full = norm_back(
            e * gains[1:2, :], unit_two, stat_a[slot, :, STAT_A["s2"] : STAT_A["s2"] + 1]
        )
        second_low = second_full.astype(jnp.bfloat16)
        right_blocks(0, second_low)
        tally("bd", 0, second_low)
        total[...] = second_full

        ready(3)

        def pulled(n):
            return back_product(second_low, wd[n * width : (n + 1) * width, :])

        grad = pulled(0)
        for n in range(4):
            later = pulled(n + 1) if n < 3 else None
            hidden_low = (grad * kept("slope", n * width)).astype(jnp.bfloat16)
            right_blocks(3 + 3 * n, hidden_low)
            tally("bu", n * width, hidden_low)
            if n == 0:
                ready(2)
            total[...] += back_product(hidden_low, wu[:, n * width : (n + 1) * width])
            grad = later
        right_go(turn, 0)
        grad_normed = total[...]
        unit_one = kept("u1")
        tally("g1", 0, grad_normed * unit_one)
        tally("h1", 0, grad_normed)
        grad_first = norm_back(
            grad_normed * gains[0:1, :], unit_one, stat_a[slot, :, STAT_A["s1"] : STAT_A["s1"] + 1]
        )
        total[...] = grad_first
        first_low = grad_first.astype(jnp.bfloat16)
        right_blocks(15, first_low)
        right_go(turn, 1)
        tally("bo", 0, first_low)
        ready(1)
        grad_mixed = back_product(first_low, wo[...]).astype(jnp.bfloat16).astype(jnp.float32)
        weighed[...] = (grad_mixed * stat_a[slot, :, 0:width]).astype(jnp.bfloat16)

        @pl.when(second)
        def _():
            rest[i - half] = total[...]
            hand_back(i)[3].start()

        @pl.when(first)
        def _():
            @pl.when(turn + 2 < turns)
            def _():
                loads(turn + 2, (0, 1), lambda copy: copy.start())

            @pl.when(turn == half - 1)
            def _():
                for which in (3, 2, 1):
                    w_copy(which).start()

    def pair_part(i, pair):
        slot = lax.rem(i, 2)
        now_b, old_b = keep_b.at[slot], keep_b.at[1 - slot]
        span = pl.ds(pl.multiple_of(pair * 128, 128), 128)

        def cut(ref, name):
            return ref[:, pl.ds(pl.multiple_of(KEEP_B[name] + pair * 128, 128), 128)]

        queries = cut(now_b, "q")
        w = weighed[:, span]
        cross = w.astype(jnp.float32) * stat_b[slot, :, span]
        zero, one = jnp.zeros_like(w), jnp.ones_like(w)
        halves = []
        for part in range(2):
            own = low if part == 0 else jnp.logical_not(low)
            spare = 64 * (1 - part)
            inner = jnp.sum(jnp.where(own, cross, 0.0), axis=-1, keepdims=True)
            rough = inner.astype(jnp.bfloat16).astype(jnp.float32)
            extra = jnp.where(
                lanes == spare, -rough, jnp.where(lanes == spare + 1, rough - inner, 0.0)
            ).astype(jnp.bfloat16)
            halves.append(
                (own, jnp.where(own, w, extra), jnp.where(own, queries, zero), jnp.where(own, w, zero))
            )

        def half_block(source, table):
            keys_in, values = cut(source, "k"), cut(source, "v")
            total_q, total_k, total_v = 0.0, 0.0, 0.0
            for own, w_extra, own_queries, own_w in halves:
                own_keys = jnp.where(own, keys_in, zero)
                scores = (back_product(queries, own_keys) * table).astype(jnp.bfloat16)
                grads = (back_product(w_extra, jnp.where(own, values, one)) * table).astype(
                    jnp.bfloat16
                )
                total_q += dot(grads, own_keys)
                total_k += rows_product(grads, own_queries)
                total_v += rows_product(scores, own_w)
            return total_q, total_k, total_v

        total_q, total_k, total_v = half_block(now_b, mix[0])
        dq[:, span] = total_q
        dk[:, span] = total_k
        dv[:, span] = total_v

        @pl.when(slot == 0)
        def _():
            dk[:, span] += carry_k[:, span]
            dv[:, span] += carry_v[:, span]

        @pl.when(slot == 1)
        def _():
            far_q, far_k, far_v = half_block(old_b, mix[1])
            dq[:, span] += far_q
            carry_k[:, span] = far_k
            carry_v[:, span] = far_v

    def head_part(turn, i):
        slot = lax.rem(i, 2)

        @pl.when(turn >= 1)
        def _():
            right_done(turn - 1, 2)

            @pl.when(second)
            def _():
                for copy in hand_back(chunk_of(turn - 1))[:3]:
                    copy.wait_send()

        @pl.when(jnp.logical_and(first, jnp.logical_or(turn == 0, turn == half)))
        def _():
            w_copy(0).wait()

        now_b = keep_b.at[slot]
        for n, (source, slope) in enumerate(((dq, "sq"), (dk, "sk"), (dv, None))):
            values = source[...]
            if slope:
                at = KEEP_B[slope]
                values = values * now_b[:, at : at + width].astype(jnp.float32)
            values = values.astype(jnp.bfloat16)
            right_blocks(18 + 3 * n, values)

            @pl.when(second)
            def _():
                hand_back(i)[n].start()

            tally("bp", n * width, values)
        right_go(turn, 2)

        def through(blocks_of, start):
            for n in range(3):
                values = jnp.concatenate([blocks_of[3 * n + m] for m in range(3)], axis=1)
                start += back_product(values, wp[:, n * width : (n + 1) * width])
            return start

        @pl.when(first)
        def _():
            grad_in = through(right.at[18:27], dn1[...])

            @pl.when(turn < half)
            def _():
                e_in[i] = grad_in.astype(jnp.bfloat16)

            @pl.when(turn >= half)
            def _():
                @pl.when(turn > half)
                def _():
                    res_copy(chunk_of(turn - 1)).wait()

                rows_out[...] = grad_in
                res_copy(i).start()

            @pl.when(turn + 2 < turns)
            def _():
                loads(turn + 2, (2, 3), lambda copy: copy.start())

            @pl.when(turn == half - 1)
            def _():
                vec_sent[...] = vec[...]
                vec_push().start()
                vec[...] = jnp.zeros_like(vec)
                for late in (chunks - 1, chunks - 2):
                    for copy in hand_back(late):
                        copy.wait_recv()
                    e_in[late] = through(cut_in.at[late - half], rest_in[late - half]).astype(
                        jnp.bfloat16
                    )
                w_copy(0).start()

    def one_turn(turn, carry):
        i = chunk_of(turn)
        tail_part(turn, i)

        @pl.when(jnp.logical_and(first, lax.rem(turn, 2) == 0))
        def _():
            loads(turn, (2, 3), lambda copy: copy.wait())
            loads(turn + 1, (2, 3), lambda copy: copy.wait())

        def one_pair(pair, inner):
            pair_part(i, pair)
            return inner

        lax.fori_loop(0, pairs, one_pair, 0)
        head_part(turn, i)
        return carry

    lax.fori_loop(0, turns, one_turn, 0)
    for n in range(3):
        right_copy(half, n).wait()

    @pl.when(first)
    def _():
        res_copy(half).wait()
        vec_push().wait_send()

    @pl.when(second)
    def _():
        for copy in hand_back(half)[:3]:
            copy.wait_send()
        for i in range(half, chunks):
            hand_back(i)[3].wait_send()
        vec_push().wait_recv()
        vec[...] += vec_peer[...]
        for i in range(half):
            for n in range(3):
                right_push(i, n).wait_recv()

    out_copy = pltpu.make_async_copy(vec, vec_out, w_sem.at[0])
    out_copy.start()
    out_copy.wait()


def run_layers(ends, mats, rows_in, mix):
    tokens, width = ends.shape
    chunks = tokens // CHUNK
    bf16, f32 = jnp.bfloat16, jnp.float32

    def kept(count):
        return [
            jax.ShapeDtypeStruct((count * CHUNK, columns), dtype)
            for columns, dtype in (
                (KEEP_A_WIDTH, bf16), (STAT_A_WIDTH, f32), (KEEP_B_WIDTH, bf16), (width, f32)
            )
        ]

    out_shape = (
        [
            jax.ShapeDtypeStruct((21, chunks, CHUNK, UNIT), bf16),
            jax.ShapeDtypeStruct((27, chunks, CHUNK, UNIT), bf16),
        ]
        + kept(chunks)
        + kept(chunks // 2)
        + [jax.ShapeDtypeStruct(mat.shape, mat.dtype) for mat in mats]
        + [
            jax.ShapeDtypeStruct((tokens, width), f32),
            jax.ShapeDtypeStruct((40, UNIT), f32),
        ]
    )
    chunk_f32 = pltpu.VMEM((CHUNK, width), f32)
    all_rows = pltpu.VMEM((chunks, CHUNK, width), bf16)
    dma = pltpu.SemaphoreType.DMA
    outs = pl.pallas_call(
        partial(layers_kernel, chunks),
        out_shape=out_shape,
        in_specs=any_specs(5) + vmem_specs(9),
        out_specs=any_specs(16),
        scratch_shapes=[pltpu.VMEM(mat.shape, mat.dtype) for mat in mats]
        + [
            all_rows,
            all_rows,
            all_rows,
            pltpu.VMEM((18, CHUNK, UNIT), bf16),
            pltpu.VMEM((27, CHUNK, UNIT), bf16),
            pltpu.VMEM((2, CHUNK, KEEP_A_WIDTH), bf16),
            pltpu.VMEM((2, CHUNK, STAT_A_WIDTH), f32),
            pltpu.VMEM((2, CHUNK, KEEP_B_WIDTH), bf16),
            pltpu.VMEM((2, CHUNK, width), f32),
            chunk_f32,
            pltpu.VMEM((HEADS, CHUNK, 128), f32),
            chunk_f32,
            chunk_f32,
            chunk_f32,
            chunk_f32,
            chunk_f32,
            chunk_f32,
            pltpu.VMEM((CHUNK, width), bf16),
            pltpu.VMEM((40, UNIT), f32),
            pltpu.VMEM((40, UNIT), f32),
            pltpu.VMEM((40, UNIT), f32),
            pltpu.VMEM((8, width), f32),
            pltpu.VMEM((8, width), f32),
            pltpu.VMEM((chunks // 2, 9, CHUNK, UNIT), bf16),
            pltpu.VMEM((chunks // 2, CHUNK, width), f32),
            pltpu.VMEM((chunks // 2, CHUNK, width), f32),
            dma((4,)),
            dma((chunks,)),
            dma((chunks, 3)),
            dma((chunks,)),
            dma,
            dma((3,)),
            dma((2, 4)),
            dma,
            dma((chunks,)),
            dma((chunks,)),
            dma((chunks // 2, 4)),
            dma((chunks // 2, 4)),
            dma((4,)),
            dma((4,)),
            dma((chunks // 2,)),
            dma((chunks // 2,)),
            dma((chunks // 2, 4)),
            dma((chunks // 2, 4)),
            dma((3,)),
            dma((chunks // 2, 3)),
            dma,
            dma,
            dma,
            dma,
        ],
        compiler_params=pltpu.CompilerParams(
            collective_id=2, has_side_effects=True, vmem_limit_bytes=62 << 20
        ),
        name="layers",
    )(ends, *mats, *rows_in, mix)
    return outs[14], outs[0], outs[1], outs[15]


MATRICES = ((81, 9, 3), (72, 3, 3), (36, 12, 3), (0, 3, 12))


def widen_kernel(full, *refs):
    targets, vectors, held, out_sem = refs[:4], refs[4:12], refs[12:16], refs[16]
    copies, turn = [], 0
    for which, (begin, across, down) in enumerate(MATRICES):
        for block in range(down):
            span = pl.ds(block * UNIT, UNIT)
            copy = pltpu.make_async_copy(
                held[which].at[span], targets[which].at[0, span], out_sem.at[turn]
            )

            def one(n, carry):
                start = pl.multiple_of((begin + block * across + n) * UNIT, UNIT)
                held[which][span, pl.ds(pl.multiple_of(n * UNIT, UNIT), UNIT)] = full[
                    pl.ds(start, UNIT), :
                ].astype(jnp.float32)
                return carry

            lax.fori_loop(0, across, one, 0)
            copy.start()
            copies.append(copy)
            turn += 1
    for (start, count), vector in zip(VECTORS.values(), vectors):
        for n in range(count):
            at = UNITS * UNIT + start + n
            vector[:, n * UNIT : (n + 1) * UNIT] = full[at : at + 1, :].astype(jnp.float32)
    for copy in copies:
        copy.wait()


def widen(full):
    shapes = [(down * UNIT, across * UNIT) for _, across, down in MATRICES]
    return pl.pallas_call(
        widen_kernel,
        out_shape=[jax.ShapeDtypeStruct((1,) + shape, jnp.float32) for shape in shapes]
        + [jax.ShapeDtypeStruct((1, count * UNIT), jnp.float32) for _, count in VECTORS.values()],
        in_specs=[pl.BlockSpec(memory_space=pltpu.VMEM)],
        out_specs=any_specs(4) + vmem_specs(8),
        scratch_shapes=[pltpu.VMEM(shape, jnp.float32) for shape in shapes]
        + [pltpu.SemaphoreType.DMA((sum(down for _, _, down in MATRICES),))],
        compiler_params=pltpu.CompilerParams(vmem_limit_bytes=36 << 20),
        name="widen",
    )(full)


def mix_tables(length):
    places = jnp.arange(2 * CHUNK, dtype=jnp.int32)
    angles = places.astype(jnp.float32) * ((0.5 * math.pi) / length.astype(jnp.float32))
    cosine, sine, document = lax.optimization_barrier(
        (jnp.cos(angles), jnp.sin(angles), places // length)
    )

    def table(start):
        later, earlier = slice(start, start + CHUNK), slice(0, CHUNK)
        seen = jnp.logical_and(
            document[later, None] == document[None, earlier],
            places[later, None] >= places[None, earlier],
        )
        near = cosine[later, None] * cosine[None, earlier] + sine[later, None] * sine[None, earlier]
        return jnp.where(seen, near, 0.0)

    return jnp.stack([table(0), table(CHUNK)])


def shards(
    endpoints,
    projection,
    projection_bias,
    output_weight,
    output_bias,
    first_gain,
    first_shift,
    up_weight,
    up_bias,
    down_weight,
    down_bias,
    second_gain,
    second_shift,
    segment_length,
):
    dp_size = lax.axis_size("dp")
    mats = (projection[0], output_weight[0], up_weight[0], down_weight[0])
    rows = (
        projection_bias, output_bias, first_gain, first_shift, up_bias, down_bias, second_gain,
        second_shift,
    )
    mix = mix_tables(segment_length[0])
    results, left, right, vec = run_layers(endpoints[0], mats, rows, mix)
    full = reduce_gradients(left, right, vec, dp_size)
    proj, out, up, down, bp, bo, g1, h1, bu, bd, g2, h2 = widen(full)
    return (results[None], proj, bp, out, bo, g1, h1, up, bu, down, bd, g2, h2)


def solution(mesh):
    in_specs = (
        P("section", "dp", None),
        P("section", None, None),
        P("section", None),
        P("section", None, None),
        P("section", None),
        P("section", None),
        P("section", None),
        P("section", None, None),
        P("section", None),
        P("section", None, None),
        P("section", None),
        P("section", None),
        P("section", None),
        P("dp"),
    )
    out_specs = (
        P("section", "dp", None),
        P("section", None, None),
        P("section", None),
        P("section", None, None),
        P("section", None),
        P("section", None),
        P("section", None),
        P("section", None, None),
        P("section", None),
        P("section", None, None),
        P("section", None),
        P("section", None),
        P("section", None),
    )
    return jax.shard_map(shards, mesh=mesh, in_specs=in_specs, out_specs=out_specs, check_vma=False)
```
